32 devices in a mesh: groups: 2 (over x), loop: 16 (over z, y, core).
Axes of the slice: x: 2, y: 2, z: 4, core: 2. Of those that a mesh axis runs over, the one named last changes fastest.
Arguments:
- hidden: bfloat16 [512, 5376], P(('groups', 'loop')), parts along dimension 0, may hold values from -6 to 6
- exit_depth: int32 [512], P(('groups', 'loop')), parts along dimension 0, may hold values from 0 to 3
- teacher: int32 [512], P(('groups', 'loop')), parts along dimension 0, may hold values from 0 to 16383
- normalizer: float32 [512], P(('groups', 'loop')), parts along dimension 0, as said below
- tied_head: bfloat16 [16384, 5376], P('loop'), may hold values from -0.25 to 0.25
- depth_gain: float32 [4, 5376], replicated, may hold values from 0.5 to 1.5
- depth_bias: float32 [4, 5376], replicated, may hold values from -1.75 to 1.75
Outputs:
- row_mass: float32 [512], P(('groups', 'loop')), parts along dimension 0
- grad_gain: float32 [8, 5376], P('groups'), parts along dimension 0
- grad_bias: float32 [8, 5376], P('groups'), parts along dimension 0
The draws below stay inside these ranges and needn't reach their ends.
There are 2 independent parts, one for each index of `groups`. The reference program is written for one: setup_inputs(seed, part) draws one part's arguments, and reference() takes and returns one part's arrays. A program takes and returns all parts, laid end to end along the dimension named above; an argument that names none is the same for every part. Nothing has to cross between parts.
Inputs may be any that keep to these rules, and one draw needn't show every extreme that they name: A log-normalizer near that of the row's logits.
All inputs are finite; a program needn't handle non-finite values.
Results may differ from the reference program's by a relative error of at most 0.012.
The reference program's roundings to bfloat16 on the way (of `mapped` and `slopes`) count: a program that leaves them out, or rounds other values in their place, can miss the bound.
Values may be sent and summed in bfloat16 or wider, within the bound.
No kernel may reach another device: no remote copies, remote signals or barrier semaphores. Data moves between devices by JAX's collectives and lax.ppermute only.
A program may use at most 128 MiB of HBM per device.

```python
import math
import jax
import jax.numpy as jnp
from jax import lax

D = 5376
VOC_DEV = 1024
DEPTHS = 4
ROWS = 256
VOCAB = 16384
N_LOOP = 16


def draw_normalizer(key, part):
    key = jax.random.fold_in(key, 11)
    center = math.log(VOCAB) + 5.0
    offset = jax.random.uniform(key, (ROWS,), jnp.float32, -1.0, 1.0)
    return (center + offset).astype(jnp.float32)


def plant(result, key, smallest, high):
    longest = result.shape.index(max(result.shape))
    spots = []
    for shift in (0, 1):
        where = [jax.random.randint(jax.random.fold_in(key, axis), (), 0, length) for axis, length in enumerate(result.shape)]
        where[longest] = (where[longest] + shift) % result.shape[longest]
        spots.append(tuple(where))
    return result.at[spots[0]].set(smallest).at[spots[1]].set(high)


def steps_of(key, dims, split, low, high):
    gain, own = 1.0, jax.random.fold_in(key, 6)
    for dim, shards_of in split:
        heights = jnp.exp(jax.random.uniform(jax.random.fold_in(own, dim), (shards_of,), jnp.float32, low / len(split), high / len(split)))
        gain = gain * jnp.repeat(heights, dims[dim] // shards_of).reshape([-1 if axis == dim else 1 for axis in range(len(dims))])
    return gain


def normal_values(key, extent, scale, reach, cuts=(), kind=jnp.bfloat16):
    factor_of = steps_of(key, extent, cuts, -0.22, 0.18) if cuts else 1.0
    array = jax.random.normal(key, extent, jnp.float32) * scale * factor_of
    return jnp.minimum(jnp.maximum(array, -reach), reach).astype(kind)


def setup_inputs(seed: int = 0, part: int = 0) -> dict:
    key_list = jax.random.split(jax.random.key(seed), 8)
    part_splits = jax.random.split(jax.random.fold_in(key_list[7], part), 8)
    return {
        "hidden": normal_values(part_splits[0], (ROWS, D), 1.0, 6.0, ((0, 16),)),
        "exit_depth": plant(jax.random.randint(part_splits[1], (ROWS,), 0, DEPTHS), jax.random.fold_in(part_splits[1], 1), 0, DEPTHS - 1).astype(jnp.int32),
        "teacher": plant(jax.random.randint(part_splits[2], (ROWS,), 0, VOCAB), jax.random.fold_in(part_splits[2], 1), 0, VOCAB - 1).astype(jnp.int32),
        "normalizer": draw_normalizer(jax.random.fold_in(jax.random.fold_in(key_list[7], part), 71), part),
        "tied_head": normal_values(key_list[4], (VOCAB, D), (3.0 * D ** -0.5), 0.25, ((0, 16),)),
        "depth_gain": jnp.clip(1.0 + 0.1 * jax.random.normal(key_list[5], (DEPTHS, D), jnp.float32), 0.5, 1.5),
        "depth_bias": normal_values(key_list[6], (DEPTHS, D), 0.3, 1.75, (), jnp.float32),
    }


def reference(hidden, exit_depth, teacher, normalizer, tied_head, depth_gain, depth_bias):
    widened = hidden.astype(jnp.float32)
    normed = widened * lax.rsqrt(lax.optimization_barrier(jnp.mean(widened * widened, axis=-1, keepdims=True)) + 1e-06)
    mapped = (normed * depth_gain[exit_depth] + depth_bias[exit_depth]).astype(jnp.bfloat16)
    blocks = tied_head.reshape(N_LOOP, VOC_DEV, D)
    firsts = jnp.arange(N_LOOP, dtype=jnp.int32) * VOC_DEV

    def advance(totals, inputs):
        block_rows, first_col = inputs
        logits = jnp.dot(mapped, block_rows.T, preferred_element_type=jnp.float32)
        prob_rows = jnp.exp(logits - normalizer[:, None])
        columns = first_col + jnp.arange(VOC_DEV, dtype=jnp.int32)
        onehot = (teacher[:, None] == columns[None, :]).astype(jnp.float32)
        slopes = (prob_rows - onehot).astype(jnp.bfloat16)
        mass_sum, back_sum = totals
        mass_sum = mass_sum + lax.optimization_barrier(jnp.sum(prob_rows, axis=1))
        back_sum = back_sum + jnp.dot(slopes, block_rows, preferred_element_type=jnp.float32)
        return ((mass_sum, back_sum), None)
    initial = (jnp.zeros((ROWS,), jnp.float32), jnp.zeros((ROWS, D), jnp.float32))
    (row_mass, back_grad), _ = lax.scan(advance, initial, (blocks, firsts))
    depth_pick = (exit_depth[:, None] == jnp.arange(DEPTHS, dtype=jnp.int32)[None, :]).astype(jnp.float32)
    grad_gain = jnp.dot(depth_pick.T, back_grad * normed, precision=lax.Precision.HIGHEST, preferred_element_type=jnp.float32)
    grad_bias = jnp.dot(depth_pick.T, back_grad, precision=lax.Precision.HIGHEST, preferred_element_type=jnp.float32)
    return (row_mass, grad_gain, grad_bias)
```

```python
import jax
import jax.numpy as jnp
from jax import lax
from jax.sharding import PartitionSpec as P

BF16 = jnp.bfloat16
F32 = jnp.float32


def ring_of(chips):
    order = list(range(0, chips, 2)) + list(range(chips - 1, 0, -2))
    return order if len(order) == chips else list(range(chips))


def ring_pairs(order):
    chips = len(order)
    return [
        (2 * order[i] + core, 2 * order[(i + 1) % chips] + core)
        for i in range(chips)
        for core in range(2)
    ]


def pieces(value):
    top = lax.reduce_precision(value, 8, 7)
    rest = value - top
    middle = lax.reduce_precision(rest, 8, 7)
    return [top, middle, rest - middle]


def digits(token):
    return [(token & 127), (token >> 7) & 127, token >> 14]


def pack(hidden, exit_depth, teacher, normalizer):
    columns = (
        pieces(normalizer)
        + [d.astype(F32) for d in digits(teacher)]
        + [exit_depth.astype(F32)]
    )
    meta = jnp.stack(columns, axis=1).astype(BF16)
    meta = jnp.pad(meta, ((0, 0), (0, 128 - meta.shape[1])))
    return jnp.concatenate([hidden, meta], axis=1)


def gather_rows(block, loop):
    chips = loop // 2
    order = ring_of(chips)
    right = ring_pairs(order)
    left = [(b, a) for a, b in right]
    swap = [(i, i ^ 1) for i in range(loop)]
    send = lambda x, pairs: lax.ppermute(x, "loop", pairs)
    mine = [None] * chips
    mine[0] = block
    from_left = from_right = block
    for step in range(1, (chips + 1) // 2):
        from_left, from_right = send(from_left, right), send(from_right, left)
        mine[chips - step], mine[step] = from_left, from_right
    if chips % 2 == 0:
        half = block.shape[1] // 256 * 128
        mine[chips // 2] = jnp.concatenate(
            [send(from_left[:, :half], right), send(from_right[:, half:], left)], axis=1
        )
    return mine + [send(x, swap) for x in mine]


def shards(loop, hidden, exit_depth, teacher, normalizer, tied_head, depth_gain, depth_bias):
    rows_dev, width = hidden.shape
    levels = depth_gain.shape[0]
    voc_local = tied_head.shape[0]
    chips = loop // 2
    rows = rows_dev * loop
    me = lax.axis_index("loop")
    order = jnp.array(ring_of(chips), jnp.int32)
    place = jnp.argmax(order == me // 2).astype(jnp.int32)
    core = me % 2

    every = jnp.concatenate(
        gather_rows(pack(hidden, exit_depth, teacher, normalizer), loop), axis=0
    )
    meta = every[:, width:].astype(F32)
    norm = (meta[:, 0] + meta[:, 1]) + meta[:, 2]
    target = (meta[:, 3] + 128.0 * meta[:, 4] + 16384.0 * meta[:, 5]).astype(jnp.int32)
    pick = (meta[:, 6:7] == jnp.arange(levels, dtype=F32)[None, :]).astype(F32)
    widened = every[:, :width].astype(F32)
    normed = widened * lax.rsqrt(jnp.mean(widened * widened, axis=-1, keepdims=True) + 1e-06)
    row_gain = jnp.dot(pick, depth_gain, precision=lax.Precision.HIGHEST)
    row_bias = jnp.dot(pick, depth_bias, precision=lax.Precision.HIGHEST)
    mapped = (normed * row_gain + row_bias).astype(BF16)
    logits = jnp.einsum("rd,vd->rv", mapped, tied_head, preferred_element_type=F32)
    prob_rows = jnp.exp(logits - norm[:, None])
    columns = me * voc_local + jnp.arange(voc_local, dtype=jnp.int32)
    onehot = (target[:, None] == columns[None, :]).astype(F32)
    slopes = (prob_rows - onehot).astype(BF16)
    back = jnp.dot(slopes, tied_head, preferred_element_type=F32)
    gain_part = jnp.dot(pick.T, back * normed, precision=lax.Precision.HIGHEST)
    bias_part = jnp.dot(pick.T, back, precision=lax.Precision.HIGHEST)
    mass = jnp.sum(prob_rows, axis=1).reshape(2, rows // 2)
    mass = jnp.roll(mass, place * rows_dev, axis=1)
    mass = jnp.where(core == 0, mass, mass[::-1]).reshape(rows)

    total = jnp.concatenate(
        [
            jnp.concatenate([gain_part, bias_part], axis=0),
            jnp.pad(mass[None, :], ((0, 2 * levels - 1), (0, 0))),
        ],
        axis=1,
    )
    total = total + lax.ppermute(total, "loop", [(i, i ^ 1) for i in range(loop)])
    bit = 2
    while bit < loop:
        pairs = [(i, i ^ bit) for i in range(loop)]
        total = lax.reduce_precision(total, 8, 7)
        total = total + lax.ppermute(total.astype(BF16), "loop", pairs).astype(F32)
        bit *= 2
    row_mass = lax.dynamic_slice(
        total[0, width:], (core * (rows // 2) + place * rows_dev,), (rows_dev,)
    )
    return row_mass, total[:levels, :width], total[levels:, :width]


def solution(mesh):
    loop = mesh.shape["loop"]

    def body(*args):
        return shards(loop, *args)

    return jax.shard_map(
        body,
        mesh=mesh,
        in_specs=(
            P(("groups", "loop"), None),
            P(("groups", "loop")),
            P(("groups", "loop")),
            P(("groups", "loop")),
            P("loop", None),
            P(),
            P(),
        ),
        out_specs=(P(("groups", "loop")), P("groups", None), P("groups", None)),
        check_vma=False,
    )
```

```python
import functools

import jax
import jax.numpy as jnp
from jax import lax
from jax.experimental import pallas as pl
from jax.experimental.pallas import tpu as pltpu
from jax.sharding import PartitionSpec as P

BF16 = jnp.bfloat16
F32 = jnp.float32
LANES = 128
NT = (((1,), (1,)), ((), ()))
VMEM = pl.BlockSpec(memory_space=pltpu.VMEM)


def ring_of(chips):
    return list(range(0, chips, 2)) + list(range(chips - 1, 0, -2))


def chip_at(place, chips):
    return jnp.where(place < chips // 2, 2 * place, 2 * (chips - 1 - place) + 1)


def place_of(chip, chips):
    return jnp.where(chip % 2 == 0, chip // 2, chips - 1 - chip // 2)


def pieces(value):
    top = value.astype(BF16).astype(F32)
    rest = value - top
    middle = rest.astype(BF16).astype(F32)
    return [top, middle, rest - middle]


def prep_kernel(hidden, exit_depth, teacher, normalizer, out):
    rows, width = hidden.shape
    block = hidden[...]
    out[:, :width] = block
    wide = block.astype(F32)
    mean = jnp.sum(wide * wide, axis=1, keepdims=True) * (1.0 / width)
    scale = lax.rsqrt(mean + 1e-06)
    down = lax.broadcasted_iota(jnp.int32, (rows, rows), 0)
    across = lax.broadcasted_iota(jnp.int32, (rows, rows), 1)

    def column(line):
        square = jnp.broadcast_to(line, (rows, rows))
        return jnp.sum(jnp.where(down == across, square, 0.0), axis=1, keepdims=True)

    token = teacher[...]
    columns = pieces(scale) + pieces(column(normalizer[...]))
    for digit in (token & 127, (token >> 7) & 127, token >> 14):
        columns.append(column(digit.astype(F32)))
    columns.append(column(exit_depth[...].astype(F32)))
    lane = lax.broadcasted_iota(jnp.int32, (rows, LANES), 1)
    meta = jnp.zeros((rows, LANES), F32)
    for i, value in enumerate(columns):
        meta = jnp.where(lane == i, value, meta)
    out[:, width:] = meta.astype(BF16)


def prep(hidden, exit_depth, teacher, normalizer):
    rows, width = hidden.shape
    line = pl.BlockSpec((1, rows), lambda i: (0, 0))
    return pl.pallas_call(
        prep_kernel,
        grid=(1,),
        out_shape=jax.ShapeDtypeStruct((rows, width + LANES), BF16),
        in_specs=[pl.BlockSpec((rows, width), lambda i: (0, 0)), line, line, line],
        out_specs=VMEM,
        compiler_params=pltpu.CompilerParams(vmem_limit_bytes=8 << 20),
    )(
        hidden,
        exit_depth.reshape(1, rows),
        teacher.reshape(1, rows),
        normalizer.reshape(1, rows),
    )


def gather_blocks(block, loop):
    chips = loop // 2
    order = ring_of(chips)
    pairs = []
    for i in range(chips):
        here, after = order[i], order[(i + 1) % chips]
        pairs += [(2 * here, 2 * after), (2 * after + 1, 2 * here + 1)]
    swap_pairs = [(i, i ^ 1) for i in range(loop)]
    swap = lambda x: lax.ppermute(x, "loop", swap_pairs)
    hop = lambda x: lax.ppermute(x, "loop", pairs)
    same, other = [None] * chips, [None] * chips
    same[0], other[0] = block, swap(block)
    half = chips // 2
    for step in range(1, half + 1):
        same[step] = hop(same[step - 1])
        if step < half:
            other[step] = hop(other[step - 1])
            other[chips - step] = swap(same[step])
            same[chips - step] = swap(other[step])
        else:
            other[step] = swap(same[step])
    return same + other


def main_kernel(loop, levels, count, *refs):
    blocks = refs[:count]
    head, gain, bias, out, mapped, slopes = refs[count:]
    voc, width = head.shape
    rows = mapped.shape[0]
    rows_dev = rows // loop
    chips = loop // 2
    me = lax.axis_index("loop")
    meta = jnp.concatenate([b[:, width:] for b in blocks], axis=0).astype(F32)
    col = lambda i: meta[:, i : i + 1]
    scale = (col(0) + col(1)) + col(2)
    norm = (col(3) + col(4)) + col(5)
    target = (col(6) + 128.0 * col(7) + 16384.0 * col(8)).astype(jnp.int32)
    depth = col(9)

    cut = width // 3
    logits = None
    for k in range(3):
        at = slice(k * cut, (k + 1) * cut)
        row = 0
        for b in blocks:
            part = slice(row, row + b.shape[0])
            g, c = gain[0:1, at], bias[0:1, at]
            for level in range(1, levels):
                here = depth[part] == float(level)
                g = jnp.where(here, gain[level : level + 1, at], g)
                c = jnp.where(here, bias[level : level + 1, at], c)
            mapped[part, at] = ((b[:, at].astype(F32) * scale[part]) * g + c).astype(BF16)
            row += b.shape[0]
        term = lax.dot_general(mapped[:, at], head[:, at], NT, preferred_element_type=F32)
        logits = term if logits is None else logits + term
    prob = jnp.exp(logits - norm)
    columns = me * voc + lax.broadcasted_iota(jnp.int32, (rows, voc), 1)
    slopes[:rows, :] = jnp.where(columns == target, prob - 1.0, prob).astype(BF16)

    mass = prob[:, :LANES]
    for j in range(1, voc // LANES):
        mass = mass + prob[:, j * LANES : (j + 1) * LANES]
    mass = jnp.sum(mass.T, axis=0, keepdims=True)
    index = lax.broadcasted_iota(jnp.int32, (rows, rows), 0)
    flip = index // (rows // 2)
    relative = (index - flip * (rows // 2)) // rows_dev
    core = me % 2
    place = place_of(me // 2, chips) + jnp.where(core == 0, chips - relative, relative)
    place = jnp.where(place >= chips, place - chips, place)
    owner = 2 * chip_at(place, chips) + jnp.where(flip == 0, core, 1 - core)
    goes_to = owner * rows_dev + index % rows_dev
    move = goes_to == lax.broadcasted_iota(jnp.int32, (rows, rows), 1)
    move = jnp.where(move, 1.0, 0.0).astype(BF16)
    lines = jnp.concatenate(pieces(mass) + [jnp.zeros((13, rows), F32)], axis=0)
    moved = jnp.dot(lines.astype(BF16), move, preferred_element_type=F32)
    moved = (moved[0:1] + moved[1:2]) + moved[2:3]
    out[:, width:] = jnp.broadcast_to(moved, (2 * levels, rows))

    lane = lax.broadcasted_iota(jnp.int32, (rows, LANES), 1).astype(F32)
    pick = jnp.where(lane == depth, 1.0, 0.0).T[:levels]
    scaled = pick * jnp.broadcast_to(scale, (rows, LANES)).T[:levels]
    none = jnp.zeros((16 - 3 * levels, rows), F32)
    scaled = jnp.concatenate(pieces(scaled) + [none], axis=0).astype(BF16)
    sums = jnp.dot(pick.astype(BF16), slopes[:rows, :], preferred_element_type=F32)
    none = jnp.zeros((16 - 3 * levels, voc), F32)
    slopes[rows:, :] = jnp.concatenate(pieces(sums) + [none], axis=0).astype(BF16)
    add3 = lambda x: (x[:levels] + x[levels : 2 * levels]) + x[2 * levels : 3 * levels]
    for k in range(width // 256):
        at = slice(k * 256, (k + 1) * 256)
        back = jnp.dot(slopes[...], head[:, at], preferred_element_type=F32)
        wide = jnp.concatenate([b[:, at] for b in blocks], axis=0).astype(F32)
        mapped[:, at] = (back[:rows] * wide).astype(BF16)
        out[levels : 2 * levels, at] = add3(back[rows:])
    out[:levels, :width] = add3(jnp.dot(scaled, mapped[...], preferred_element_type=F32))


def main(blocks, tied_head, depth_gain, depth_bias, loop):
    levels = depth_gain.shape[0]
    voc, width = tied_head.shape
    rows = sum(b.shape[0] for b in blocks)
    return pl.pallas_call(
        functools.partial(main_kernel, loop, levels, len(blocks)),
        out_shape=jax.ShapeDtypeStruct((2 * levels, width + rows), F32),
        in_specs=[VMEM] * (len(blocks) + 3),
        out_specs=VMEM,
        scratch_shapes=[
            pltpu.VMEM((rows, width), BF16),
            pltpu.VMEM((rows + 16, voc), BF16),
        ],
        compiler_params=pltpu.CompilerParams(vmem_limit_bytes=24 << 20),
        cost_estimate=pl.CostEstimate(
            flops=4 * rows * voc * width,
            bytes_accessed=2 * voc * width,
            transcendentals=rows * voc,
        ),
    )(*blocks, tied_head, depth_gain, depth_bias)


def shards(loop, hidden, exit_depth, teacher, normalizer, tied_head, depth_gain, depth_bias):
    rows_dev, width = hidden.shape
    levels = depth_gain.shape[0]
    me = lax.axis_index("loop")
    blocks = gather_blocks(prep(hidden, exit_depth, teacher, normalizer), loop)
    if rows_dev % 16:
        whole = jnp.concatenate(blocks, axis=0)
        blocks = [whole[i : i + 16] for i in range(0, whole.shape[0], 16)]
    total = main(blocks, tied_head, depth_gain, depth_bias, loop)
    total = total + lax.ppermute(total, "loop", [(i, i ^ 1) for i in range(loop)])
    bit = 2
    while bit < loop:
        pairs = [(i, i ^ bit) for i in range(loop)]
        total = lax.reduce_precision(total, 8, 7)
        total = total + lax.ppermute(total.astype(BF16), "loop", pairs).astype(F32)
        bit *= 2
    row_mass = lax.dynamic_slice(total[0], (width + me * rows_dev,), (rows_dev,))
    return row_mass, total[:levels, :width], total[levels:, :width]


def solution(mesh):
    loop = mesh.shape["loop"]

    def body(*args):
        return shards(loop, *args)

    return jax.shard_map(
        body,
        mesh=mesh,
        in_specs=(
            P(("groups", "loop"), None),
            P(("groups", "loop")),
            P(("groups", "loop")),
            P(("groups", "loop")),
            P("loop", None),
            P(),
            P(),
        ),
        out_specs=(P(("groups", "loop")), P("groups", None), P("groups", None)),
        check_vma=False,
    )
```

```python
import functools

import jax
import jax.numpy as jnp
from jax import lax
from jax.experimental import pallas as pl
from jax.experimental.pallas import tpu as pltpu
from jax.sharding import PartitionSpec as P

BF16 = jnp.bfloat16
F32 = jnp.float32
LANES = 128
NT = (((1,), (1,)), ((), ()))
VMEM = pl.BlockSpec(memory_space=pltpu.VMEM)
HBM = pl.BlockSpec(memory_space=pl.ANY)


def in_hbm(x):
    return pltpu.with_memory_space_constraint(x, pltpu.HBM)


def ring_of(chips):
    return list(range(0, chips, 2)) + list(range(chips - 1, 0, -2))


def chip_at(place, chips):
    return jnp.where(place < chips // 2, 2 * place, 2 * (chips - 1 - place) + 1)


def place_of(chip, chips):
    return jnp.where(chip % 2 == 0, chip // 2, chips - 1 - chip // 2)


def pieces(value):
    top = value.astype(BF16).astype(F32)
    rest = value - top
    middle = rest.astype(BF16).astype(F32)
    return [top, middle, rest - middle]


def prep_kernel(
    hidden, exit_depth, teacher, normalizer, depth_gain, depth_bias,
    out, gain_out, bias_out, row_buf, int_buf, float_buf, sems,
):
    rows, width = hidden.shape
    copies = [
        pltpu.make_async_copy(hidden, row_buf, sems.at[0]),
        pltpu.make_async_copy(exit_depth, int_buf.at[0], sems.at[1]),
        pltpu.make_async_copy(teacher, int_buf.at[1], sems.at[2]),
        pltpu.make_async_copy(normalizer, float_buf, sems.at[3]),
        pltpu.make_async_copy(depth_gain, gain_out, sems.at[4]),
        pltpu.make_async_copy(depth_bias, bias_out, sems.at[5]),
    ]
    for copy in copies:
        copy.start()
    for copy in copies[:4]:
        copy.wait()
    block = row_buf[...]
    out[:, :width] = block
    wide = block.astype(F32)
    mean = jnp.sum(wide * wide, axis=1, keepdims=True) * (1.0 / width)
    scale = lax.rsqrt(mean + 1e-06)
    down = lax.broadcasted_iota(jnp.int32, (rows, rows), 0)
    across = lax.broadcasted_iota(jnp.int32, (rows, rows), 1)

    def column(line):
        square = jnp.broadcast_to(line, (rows, rows))
        return jnp.sum(jnp.where(down == across, square, 0.0), axis=1, keepdims=True)

    token = int_buf[1]
    columns = pieces(scale) + pieces(column(float_buf[...]))
    for digit in (token & 127, (token >> 7) & 127, token >> 14):
        columns.append(column(digit.astype(F32)))
    columns.append(column(int_buf[0].astype(F32)))
    lane = lax.broadcasted_iota(jnp.int32, (rows, LANES), 1)
    meta = jnp.zeros((rows, LANES), F32)
    for i, value in enumerate(columns):
        meta = jnp.where(lane == i, value, meta)
    out[:, width:] = meta.astype(BF16)
    for copy in copies[4:]:
        copy.wait()


def prep(hidden, exit_depth, teacher, normalizer, depth_gain, depth_bias):
    rows, width = hidden.shape
    return pl.pallas_call(
        prep_kernel,
        out_shape=(
            pltpu.VMEM((rows, width + LANES), BF16),
            pltpu.VMEM(depth_gain.shape, F32),
            pltpu.VMEM(depth_bias.shape, F32),
        ),
        in_specs=[HBM] * 6,
        out_specs=(VMEM, VMEM, VMEM),
        scratch_shapes=[
            pltpu.VMEM((rows, width), BF16),
            pltpu.VMEM((2, 1, rows), jnp.int32),
            pltpu.VMEM((1, rows), F32),
            pltpu.SemaphoreType.DMA((6,)),
        ],
        compiler_params=pltpu.CompilerParams(vmem_limit_bytes=8 << 20),
    )(
        in_hbm(hidden),
        in_hbm(exit_depth.reshape(1, rows)),
        in_hbm(teacher.reshape(1, rows)),
        in_hbm(normalizer.reshape(1, rows)),
        in_hbm(depth_gain),
        in_hbm(depth_bias),
    )


def gather_blocks(block, loop):
    chips = loop // 2
    order = ring_of(chips)
    pairs, cross_pairs = [], []
    for i in range(chips):
        here, after = order[i], order[(i + 1) % chips]
        pairs += [(2 * here, 2 * after), (2 * after + 1, 2 * here + 1)]
        cross_pairs += [(2 * here + 1, 2 * after), (2 * after, 2 * here + 1)]
    swap_pairs = [(i, i ^ 1) for i in range(loop)]
    swap = lambda x: lax.ppermute(x, "loop", swap_pairs)
    hop = lambda x: lax.ppermute(x, "loop", pairs)
    same, other = [None] * chips, [None] * chips
    same[0] = block
    half = chips // 2
    for step in range(1, half + 1):
        same[step] = hop(same[step - 1])
        if step == 1:
            other[step] = lax.ppermute(block, "loop", cross_pairs)
            other[0] = swap(block)
        elif step < half:
            other[step] = hop(other[step - 1])
        if step < half:
            other[chips - step] = swap(same[step])
            same[chips - step] = swap(other[step])
        else:
            other[step] = swap(same[step])
    return same + other


def main_kernel(loop, levels, count, *refs):
    blocks = refs[:count]
    head_hbm, gain, bias, out, head, mapped, slopes, sems = refs[count:]
    voc, width = head.shape
    cuts = 7 if width % (7 * LANES) == 0 else 1
    cut = width // cuts
    copies = []
    for k in range(cuts):
        at = pl.ds(k * cut, cut)
        copies.append(pltpu.make_async_copy(head_hbm.at[:, at], head.at[:, at], sems.at[k]))
    for copy in copies:
        copy.start()
    rows = mapped.shape[0]
    rows_dev = rows // loop
    chips = loop // 2
    me = lax.axis_index("loop")
    meta = jnp.concatenate([b[:, width:] for b in blocks], axis=0).astype(F32)
    col = lambda i: meta[:, i : i + 1]
    scale = (col(0) + col(1)) + col(2)
    norm = (col(3) + col(4)) + col(5)
    target = (col(6) + 128.0 * col(7) + 16384.0 * col(8)).astype(jnp.int32)
    depth = col(9)

    logits = None
    for k in range(cuts):
        at = slice(k * cut, (k + 1) * cut)
        row = 0
        for b in blocks:
            part = slice(row, row + b.shape[0])
            g, c = gain[0:1, at], bias[0:1, at]
            for level in range(1, levels):
                here = depth[part] == float(level)
                g = jnp.where(here, gain[level : level + 1, at], g)
                c = jnp.where(here, bias[level : level + 1, at], c)
            mapped[part, at] = ((b[:, at].astype(F32) * scale[part]) * g + c).astype(BF16)
            row += b.shape[0]
        copies[k].wait()
        term = lax.dot_general(mapped[:, at], head[:, at], NT, preferred_element_type=F32)
        logits = term if logits is None else logits + term
    prob = jnp.exp(logits - norm)
    columns = me * voc + lax.broadcasted_iota(jnp.int32, (rows, voc), 1)
    slopes[:rows, :] = jnp.where(columns == target, prob - 1.0, prob).astype(BF16)

    mass = prob[:, :LANES]
    for j in range(1, voc // LANES):
        mass = mass + prob[:, j * LANES : (j + 1) * LANES]
    mass = jnp.sum(mass.T, axis=0, keepdims=True)
    index = lax.broadcasted_iota(jnp.int32, (rows, rows), 0)
    flip = index // (rows // 2)
    relative = (index - flip * (rows // 2)) // rows_dev
    core = me % 2
    place = place_of(me // 2, chips) + jnp.where(core == 0, chips - relative, relative)
    place = jnp.where(place >= chips, place - chips, place)
    owner = 2 * chip_at(place, chips) + jnp.where(flip == 0, core, 1 - core)
    goes_to = owner * rows_dev + index % rows_dev
    move = goes_to == lax.broadcasted_iota(jnp.int32, (rows, rows), 1)
    move = jnp.where(move, 1.0, 0.0).astype(BF16)
    lines = jnp.concatenate(pieces(mass) + [jnp.zeros((13, rows), F32)], axis=0)
    moved = jnp.dot(lines.astype(BF16), move, preferred_element_type=F32)
    moved = (moved[0:1] + moved[1:2]) + moved[2:3]
    out[:, width:] = jnp.broadcast_to(moved, (2 * levels, rows))

    lane = lax.broadcasted_iota(jnp.int32, (rows, LANES), 1).astype(F32)
    pick = jnp.where(lane == depth, 1.0, 0.0).T[:levels]
    scaled = pick * jnp.broadcast_to(scale, (rows, LANES)).T[:levels]
    none = jnp.zeros((16 - 3 * levels, rows), F32)
    scaled = jnp.concatenate(pieces(scaled) + [none], axis=0).astype(BF16)
    sums = jnp.dot(pick.astype(BF16), slopes[:rows, :], preferred_element_type=F32)
    none = jnp.zeros((16 - 3 * levels, voc), F32)
    slopes[rows:, :] = jnp.concatenate(pieces(sums) + [none], axis=0).astype(BF16)
    add3 = lambda x: (x[:levels] + x[levels : 2 * levels]) + x[2 * levels : 3 * levels]
    for k in range(width // 256):
        at = slice(k * 256, (k + 1) * 256)
        back = jnp.dot(slopes[...], head[:, at], preferred_element_type=F32)
        wide = jnp.concatenate([b[:, at] for b in blocks], axis=0).astype(F32)
        mapped[:, at] = (back[:rows] * wide).astype(BF16)
        out[levels : 2 * levels, at] = add3(back[rows:])
    out[:levels, :width] = add3(jnp.dot(scaled, mapped[...], preferred_element_type=F32))


def main(blocks, tied_head, depth_gain, depth_bias, loop):
    levels = depth_gain.shape[0]
    voc, width = tied_head.shape
    rows = sum(b.shape[0] for b in blocks)
    return pl.pallas_call(
        functools.partial(main_kernel, loop, levels, len(blocks)),
        out_shape=pltpu.VMEM((2 * levels, width + rows), F32),
        in_specs=[VMEM] * len(blocks) + [HBM, VMEM, VMEM],
        out_specs=VMEM,
        scratch_shapes=[
            pltpu.VMEM((voc, width), BF16),
            pltpu.VMEM((rows, width), BF16),
            pltpu.VMEM((rows + 16, voc), BF16),
            pltpu.SemaphoreType.DMA((7,)),
        ],
        compiler_params=pltpu.CompilerParams(vmem_limit_bytes=32 << 20),
        cost_estimate=pl.CostEstimate(
            flops=4 * rows * voc * width,
            bytes_accessed=2 * voc * width,
            transcendentals=rows * voc,
        ),
    )(*blocks, in_hbm(tied_head), depth_gain, depth_bias)


def sum_over_loop(part, loop):
    send = lambda x, pairs: lax.ppermute(x, "loop", pairs)
    odd = range(1, loop, 2)
    total = part + send(part, [(i - 1, i) for i in odd])
    bits = [1 << k for k in range(1, loop.bit_length() - 1)]
    rounds = [bits[:1]] + [bits[k : k + 2] for k in range(1, len(bits), 2)]
    for dims in rounds:
        mine = lax.reduce_precision(total, 8, 7)
        sent = mine.astype(BF16)
        take = lambda mask: send(sent, [(i, i ^ mask) for i in odd]).astype(F32)
        total = mine + take(dims[0])
        if len(dims) == 2:
            total = total + (take(dims[1]) + take(dims[0] ^ dims[1]))
    return total, send(total, [(i, i - 1) for i in odd])


def last_kernel(levels, rows, total, arrived, mass_out, gain_out, bias_out, buf, line, sems):
    width = gain_out.shape[1]
    me = lax.axis_index("loop")
    buf[...] = jnp.where(me % 2 == 0, arrived[...], total[...])
    every = buf[0:1, width:]
    spread = lax.broadcasted_iota(jnp.int32, (every.shape[1], LANES), 0)
    target = lax.broadcasted_iota(jnp.int32, (every.shape[1], LANES), 1)
    move = jnp.where(spread - me * rows == target, 1.0, 0.0).astype(BF16)
    lines = jnp.concatenate(pieces(every) + [jnp.zeros((13, every.shape[1]), F32)], axis=0)
    own = jnp.dot(lines.astype(BF16), move, preferred_element_type=F32)
    line[...] = ((own[0:1] + own[1:2]) + own[2:3])[:, :rows]
    copies = [
        pltpu.make_async_copy(buf.at[pl.ds(0, levels), pl.ds(0, width)], gain_out, sems.at[0]),
        pltpu.make_async_copy(buf.at[pl.ds(levels, levels), pl.ds(0, width)], bias_out, sems.at[1]),
        pltpu.make_async_copy(line, mass_out, sems.at[2]),
    ]
    for copy in copies:
        copy.start()
    for copy in copies:
        copy.wait()


def last(total, arrived, levels, width, rows):
    grad = pltpu.HBM((levels, width), F32)
    mass, gain, bias = pl.pallas_call(
        functools.partial(last_kernel, levels, rows),
        out_shape=(pltpu.HBM((1, rows), F32), grad, grad),
        in_specs=[VMEM, VMEM],
        out_specs=(HBM, HBM, HBM),
        scratch_shapes=[
            pltpu.VMEM(total.shape, F32),
            pltpu.VMEM((1, rows), F32),
            pltpu.SemaphoreType.DMA((3,)),
        ],
        compiler_params=pltpu.CompilerParams(vmem_limit_bytes=8 << 20),
    )(total, arrived)
    return mass.reshape(rows), gain, bias


def shards(loop, hidden, exit_depth, teacher, normalizer, tied_head, depth_gain, depth_bias):
    rows_dev, width = hidden.shape
    levels = depth_gain.shape[0]
    block, gain, bias = prep(hidden, exit_depth, teacher, normalizer, depth_gain, depth_bias)
    blocks = gather_blocks(block, loop)
    if rows_dev % 16:
        whole = jnp.concatenate(blocks, axis=0)
        blocks = [whole[i : i + 16] for i in range(0, whole.shape[0], 16)]
    part = main(blocks, tied_head, gain, bias, loop)
    total, arrived = sum_over_loop(part, loop)
    return last(total, arrived, levels, width, rows_dev)


def solution(mesh):
    loop = mesh.shape["loop"]

    def body(*args):
        return shards(loop, *args)

    return jax.shard_map(
        body,
        mesh=mesh,
        in_specs=(
            P(("groups", "loop"), None),
            P(("groups", "loop")),
            P(("groups", "loop")),
            P(("groups", "loop")),
            P("loop", None),
            P(),
            P(),
        ),
        out_specs=(P(("groups", "loop")), P("groups", None), P("groups", None)),
        check_vma=False,
    )
```

```python
import functools

import jax
import jax.numpy as jnp
from jax import lax
from jax.experimental import pallas as pl
from jax.experimental.pallas import tpu as pltpu
from jax.sharding import PartitionSpec as P

BF16 = jnp.bfloat16
F32 = jnp.float32
LANES = 128
NT = (((1,), (1,)), ((), ()))
VMEM = pl.BlockSpec(memory_space=pltpu.VMEM)
HBM = pl.BlockSpec(memory_space=pl.ANY)


def in_hbm(x):
    return pltpu.with_memory_space_constraint(x, pltpu.HBM)


def ring_of(chips):
    return list(range(0, chips, 2)) + list(range(chips - 1, 0, -2))


def chip_at(place, chips):
    return jnp.where(place < chips // 2, 2 * place, 2 * (chips - 1 - place) + 1)


def place_of(chip, chips):
    return jnp.where(chip % 2 == 0, chip // 2, chips - 1 - chip // 2)


def pieces(value):
    top = value.astype(BF16).astype(F32)
    rest = value - top
    middle = rest.astype(BF16).astype(F32)
    return [top, middle, rest - middle]


def prep_kernel(
    hidden, exit_depth, teacher, normalizer, depth_gain, depth_bias,
    out, gain_out, bias_out, row_buf, int_buf, float_buf, sems,
):
    rows, width = hidden.shape
    copies = [
        pltpu.make_async_copy(hidden, row_buf, sems.at[0]),
        pltpu.make_async_copy(exit_depth, int_buf.at[0], sems.at[1]),
        pltpu.make_async_copy(teacher, int_buf.at[1], sems.at[2]),
        pltpu.make_async_copy(normalizer, float_buf, sems.at[3]),
        pltpu.make_async_copy(depth_gain, gain_out, sems.at[4]),
        pltpu.make_async_copy(depth_bias, bias_out, sems.at[5]),
    ]
    for copy in copies:
        copy.start()
    for copy in copies[:4]:
        copy.wait()
    block = row_buf[...]
    out[:, :width] = block
    wide = block.astype(F32)
    mean = jnp.sum(wide * wide, axis=1, keepdims=True) * (1.0 / width)
    scale = lax.rsqrt(mean + 1e-06)
    down = lax.broadcasted_iota(jnp.int32, (rows, rows), 0)
    across = lax.broadcasted_iota(jnp.int32, (rows, rows), 1)

    def column(line):
        square = jnp.broadcast_to(line, (rows, rows))
        return jnp.sum(jnp.where(down == across, square, 0.0), axis=1, keepdims=True)

    token = int_buf[1]
    columns = pieces(scale) + pieces(column(float_buf[...]))
    for digit in (token & 127, (token >> 7) & 127, token >> 14):
        columns.append(column(digit.astype(F32)))
    columns.append(column(int_buf[0].astype(F32)))
    lane = lax.broadcasted_iota(jnp.int32, (rows, LANES), 1)
    meta = jnp.zeros((rows, LANES), F32)
    for i, value in enumerate(columns):
        meta = jnp.where(lane == i, value, meta)
    out[:, width:] = meta.astype(BF16)
    for copy in copies[4:]:
        copy.wait()


def prep(hidden, exit_depth, teacher, normalizer, depth_gain, depth_bias):
    rows, width = hidden.shape
    return pl.pallas_call(
        prep_kernel,
        out_shape=(
            pltpu.VMEM((rows, width + LANES), BF16),
            pltpu.VMEM(depth_gain.shape, F32),
            pltpu.VMEM(depth_bias.shape, F32),
        ),
        in_specs=[HBM] * 6,
        out_specs=(VMEM, VMEM, VMEM),
        scratch_shapes=[
            pltpu.VMEM((rows, width), BF16),
            pltpu.VMEM((2, 1, rows), jnp.int32),
            pltpu.VMEM((1, rows), F32),
            pltpu.SemaphoreType.DMA((6,)),
        ],
        compiler_params=pltpu.CompilerParams(vmem_limit_bytes=8 << 20),
    )(
        in_hbm(hidden),
        in_hbm(exit_depth.reshape(1, rows)),
        in_hbm(teacher.reshape(1, rows)),
        in_hbm(normalizer.reshape(1, rows)),
        in_hbm(depth_gain),
        in_hbm(depth_bias),
    )


def hop_pairs(order, step, cross):
    chips = len(order)
    first = 1 - step % 2
    pairs = []
    for i in range(chips):
        here, after = 2 * order[i], 2 * order[(i + 1) % chips]
        if cross:
            pairs += [(here + first, after + 1 - first), (after + 1 - first, here + first)]
        else:
            pairs += [(here + 1 - first, after + 1 - first), (after + first, here + first)]
    return pairs


def gather_blocks(block, loop, beside):
    chips = loop // 2
    order = ring_of(chips)
    half = chips // 2
    swap_pairs = [(i, i ^ 1) for i in range(loop)]
    send = lambda x, pairs: lax.ppermute(x, "loop", pairs)
    same, other = [None] * chips, [None] * chips
    same[0], other[0] = block, send(block, swap_pairs)
    crossed = plain = block
    for step in range(1, half + 1):
        crossed = send(crossed, hop_pairs(order, step, True))
        if step < half:
            plain = send(plain, hop_pairs(order, step, step > 1))
        if step == 1:
            crossed, beside = lax.optimization_barrier((crossed, beside))
        far = step if step % 2 else chips - step
        near = chips - far
        mine, theirs = (other, same) if step % 2 else (same, other)
        mine[far] = crossed
        if step < half:
            theirs[far] = plain
            theirs[near] = send(crossed, swap_pairs)
            mine[near] = send(plain, swap_pairs)
        else:
            theirs[far] = send(crossed, swap_pairs)
    return same + other, beside


def load_kernel(head_hbm, head, sems):
    parts = sems.shape[0]
    size = head.shape[0] // parts
    copies = [
        pltpu.make_async_copy(
            head_hbm.at[pl.ds(k * size, size)], head.at[pl.ds(k * size, size)], sems.at[k]
        )
        for k in range(parts)
    ]
    for copy in copies:
        copy.start()
    for copy in copies:
        copy.wait()


def load(tied_head):
    return pl.pallas_call(
        load_kernel,
        out_shape=pltpu.VMEM(tied_head.shape, BF16),
        in_specs=[HBM],
        out_specs=VMEM,
        scratch_shapes=[pltpu.SemaphoreType.DMA((4,))],
        compiler_params=pltpu.CompilerParams(vmem_limit_bytes=16 << 20),
        cost_estimate=pl.CostEstimate(
            flops=0, bytes_accessed=4 * tied_head.shape[0] * tied_head.shape[1], transcendentals=0
        ),
    )(in_hbm(tied_head))


def main_kernel(loop, levels, count, *refs):
    blocks = refs[:count]
    head, gain, bias, out, mapped, slopes = refs[count:]
    voc, width = head.shape
    cuts = 3 if width % (3 * LANES) == 0 else 1
    cut = width // cuts
    rows = mapped.shape[0]
    rows_dev = rows // loop
    chips = loop // 2
    me = lax.axis_index("loop")
    meta = jnp.concatenate([b[:, width:] for b in blocks], axis=0).astype(F32)
    col = lambda i: meta[:, i : i + 1]
    scale = (col(0) + col(1)) + col(2)
    norm = (col(3) + col(4)) + col(5)
    target = (col(6) + 128.0 * col(7) + 16384.0 * col(8)).astype(jnp.int32)
    depth = col(9)

    logits = None
    for k in range(cuts):
        at = slice(k * cut, (k + 1) * cut)
        row = 0
        for b in blocks:
            part = slice(row, row + b.shape[0])
            g, c = gain[0:1, at], bias[0:1, at]
            for level in range(1, levels):
                here = depth[part] == float(level)
                g = jnp.where(here, gain[level : level + 1, at], g)
                c = jnp.where(here, bias[level : level + 1, at], c)
            mapped[part, at] = ((b[:, at].astype(F32) * scale[part]) * g + c).astype(BF16)
            row += b.shape[0]
        term = lax.dot_general(mapped[:, at], head[:, at], NT, preferred_element_type=F32)
        logits = term if logits is None else logits + term
    prob = jnp.exp(logits - norm)
    columns = me * voc + lax.broadcasted_iota(jnp.int32, (rows, voc), 1)
    slopes[:rows, :] = jnp.where(columns == target, prob - 1.0, prob).astype(BF16)

    mass = prob[:, :LANES]
    for j in range(1, voc // LANES):
        mass = mass + prob[:, j * LANES : (j + 1) * LANES]
    mass = jnp.sum(mass.T, axis=0, keepdims=True)
    index = lax.broadcasted_iota(jnp.int32, (rows, rows), 0)
    flip = index // (rows // 2)
    relative = (index - flip * (rows // 2)) // rows_dev
    core = me % 2
    place = place_of(me // 2, chips) + jnp.where(core == 0, relative, chips - relative)
    place = jnp.where(place >= chips, place - chips, place)
    owner = 2 * chip_at(place, chips) + jnp.where(flip == 0, core, 1 - core)
    goes_to = owner * rows_dev + index % rows_dev
    move = goes_to == lax.broadcasted_iota(jnp.int32, (rows, rows), 1)
    move = jnp.where(move, 1.0, 0.0).astype(BF16)
    lines = jnp.concatenate(pieces(mass) + [jnp.zeros((13, rows), F32)], axis=0)
    moved = jnp.dot(lines.astype(BF16), move, preferred_element_type=F32)
    moved = (moved[0:1] + moved[1:2]) + moved[2:3]
    out[:, width:] = jnp.broadcast_to(moved, (2 * levels, rows))

    lane = lax.broadcasted_iota(jnp.int32, (rows, LANES), 1).astype(F32)
    pick = jnp.where(lane == depth, 1.0, 0.0).T[:levels]
    scaled = pick * jnp.broadcast_to(scale, (rows, LANES)).T[:levels]
    none = jnp.zeros((16 - 3 * levels, rows), F32)
    scaled = jnp.concatenate(pieces(scaled) + [none], axis=0).astype(BF16)
    sums = jnp.dot(pick.astype(BF16), slopes[:rows, :], preferred_element_type=F32)
    none = jnp.zeros((16 - 3 * levels, voc), F32)
    slopes[rows:, :] = jnp.concatenate(pieces(sums) + [none], axis=0).astype(BF16)
    add3 = lambda x: (x[:levels] + x[levels : 2 * levels]) + x[2 * levels : 3 * levels]
    for k in range(width // 256):
        at = slice(k * 256, (k + 1) * 256)
        back = jnp.dot(slopes[...], head[:, at], preferred_element_type=F32)
        wide = jnp.concatenate([b[:, at] for b in blocks], axis=0).astype(F32)
        mapped[:, at] = (back[:rows] * wide).astype(BF16)
        out[levels : 2 * levels, at] = add3(back[rows:])
    out[:levels, :width] = add3(jnp.dot(scaled, mapped[...], preferred_element_type=F32))


def main(blocks, tied_head, depth_gain, depth_bias, loop):
    levels = depth_gain.shape[0]
    voc, width = tied_head.shape
    rows = sum(b.shape[0] for b in blocks)
    return pl.pallas_call(
        functools.partial(main_kernel, loop, levels, len(blocks)),
        out_shape=pltpu.VMEM((2 * levels, width + rows), F32),
        in_specs=[VMEM] * (len(blocks) + 3),
        out_specs=VMEM,
        scratch_shapes=[
            pltpu.VMEM((rows, width), BF16),
            pltpu.VMEM((rows + 16, voc), BF16),
        ],
        compiler_params=pltpu.CompilerParams(vmem_limit_bytes=20 << 20),
        cost_estimate=pl.CostEstimate(
            flops=4 * rows * voc * width,
            bytes_accessed=2 * voc * width,
            transcendentals=rows * voc,
        ),
    )(*blocks, tied_head, depth_gain, depth_bias)


def sum_over_loop(total, loop):
    total = total + lax.ppermute(total, "loop", [(i, i ^ 1) for i in range(loop)])
    bit = 2
    while bit < loop:
        pairs = [(i, i ^ bit) for i in range(loop)]
        total = lax.reduce_precision(total, 8, 7)
        total = total + lax.ppermute(total.astype(BF16), "loop", pairs).astype(F32)
        bit *= 2
    return total


def last_kernel(levels, rows, buf, mass_out, gain_out, bias_out, line, sems):
    width = gain_out.shape[1]
    me = lax.axis_index("loop")
    every = buf[0:1, width:]
    spread = lax.broadcasted_iota(jnp.int32, (every.shape[1], LANES), 0)
    target = lax.broadcasted_iota(jnp.int32, (every.shape[1], LANES), 1)
    move = jnp.where(spread - me * rows == target, 1.0, 0.0).astype(BF16)
    lines = jnp.concatenate(pieces(every) + [jnp.zeros((13, every.shape[1]), F32)], axis=0)
    own = jnp.dot(lines.astype(BF16), move, preferred_element_type=F32)
    line[...] = ((own[0:1] + own[1:2]) + own[2:3])[:, :rows]
    copies = [
        pltpu.make_async_copy(buf.at[pl.ds(0, levels), pl.ds(0, width)], gain_out, sems.at[0]),
        pltpu.make_async_copy(buf.at[pl.ds(levels, levels), pl.ds(0, width)], bias_out, sems.at[1]),
        pltpu.make_async_copy(line, mass_out, sems.at[2]),
    ]
    for copy in copies:
        copy.start()
    for copy in copies:
        copy.wait()


def last(total, levels, width, rows):
    grad = pltpu.HBM((levels, width), F32)
    mass, gain, bias = pl.pallas_call(
        functools.partial(last_kernel, levels, rows),
        out_shape=(pltpu.HBM((1, rows), F32), grad, grad),
        in_specs=[VMEM],
        out_specs=(HBM, HBM, HBM),
        scratch_shapes=[
            pltpu.VMEM((1, rows), F32),
            pltpu.SemaphoreType.DMA((3,)),
        ],
        compiler_params=pltpu.CompilerParams(vmem_limit_bytes=8 << 20),
    )(total)
    return mass.reshape(rows), gain, bias


def shards(loop, hidden, exit_depth, teacher, normalizer, tied_head, depth_gain, depth_bias):
    rows_dev, width = hidden.shape
    levels = depth_gain.shape[0]
    block, gain, bias = prep(hidden, exit_depth, teacher, normalizer, depth_gain, depth_bias)
    blocks, head = gather_blocks(block, loop, load(tied_head))
    if rows_dev % 16:
        whole = jnp.concatenate(blocks, axis=0)
        blocks = [whole[i : i + 16] for i in range(0, whole.shape[0], 16)]
    part = main(blocks, head, gain, bias, loop)
    return last(sum_over_loop(part, loop), levels, width, rows_dev)


def solution(mesh):
    loop = mesh.shape["loop"]

    def body(*args):
        return shards(loop, *args)

    return jax.shard_map(
        body,
        mesh=mesh,
        in_specs=(
            P(("groups", "loop"), None),
            P(("groups", "loop")),
            P(("groups", "loop")),
            P(("groups", "loop")),
            P("loop", None),
            P(),
            P(),
        ),
        out_specs=(P(("groups", "loop")), P("groups", None), P("groups", None)),
        check_vma=False,
    )
```

```python
import functools

import jax
import jax.numpy as jnp
from jax import lax
from jax.experimental import pallas as pl
from jax.experimental.pallas import tpu as pltpu
from jax.sharding import PartitionSpec as P

BF16 = jnp.bfloat16
F32 = jnp.float32
LANES = 128
NT = (((1,), (1,)), ((), ()))
VMEM = pl.BlockSpec(memory_space=pltpu.VMEM)
HBM = pl.BlockSpec(memory_space=pl.ANY)


def in_hbm(x):
    return pltpu.with_memory_space_constraint(x, pltpu.HBM)


def ring_of(chips):
    return list(range(0, chips, 2)) + list(range(chips - 1, 0, -2))


def chip_at(place, chips):
    return jnp.where(place < chips // 2, 2 * place, 2 * (chips - 1 - place) + 1)


def place_of(chip, chips):
    return jnp.where(chip % 2 == 0, chip // 2, chips - 1 - chip // 2)


def pieces(value):
    top = value.astype(BF16).astype(F32)
    rest = value - top
    middle = rest.astype(BF16).astype(F32)
    return [top, middle, rest - middle]


def prep_kernel(
    hidden, exit_depth, teacher, normalizer, depth_gain, depth_bias,
    out, gain_out, bias_out, row_buf, int_buf, float_buf, sems,
):
    rows, width = hidden.shape
    copies = [
        pltpu.make_async_copy(hidden, row_buf, sems.at[0]),
        pltpu.make_async_copy(exit_depth, int_buf.at[0], sems.at[1]),
        pltpu.make_async_copy(teacher, int_buf.at[1], sems.at[2]),
        pltpu.make_async_copy(normalizer, float_buf, sems.at[3]),
        pltpu.make_async_copy(depth_gain, gain_out, sems.at[4]),
        pltpu.make_async_copy(depth_bias, bias_out, sems.at[5]),
    ]
    for copy in copies:
        copy.start()
    for copy in copies[:4]:
        copy.wait()
    block = row_buf[...]
    out[:, :width] = block
    wide = block.astype(F32)
    mean = jnp.sum(wide * wide, axis=1, keepdims=True) * (1.0 / width)
    scale = lax.rsqrt(mean + 1e-06)
    down = lax.broadcasted_iota(jnp.int32, (rows, rows), 0)
    across = lax.broadcasted_iota(jnp.int32, (rows, rows), 1)

    def column(line):
        square = jnp.broadcast_to(line, (rows, rows))
        return jnp.sum(jnp.where(down == across, square, 0.0), axis=1, keepdims=True)

    token = int_buf[1]
    columns = pieces(scale) + pieces(column(float_buf[...]))
    for digit in (token & 127, (token >> 7) & 127, token >> 14):
        columns.append(column(digit.astype(F32)))
    columns.append(column(int_buf[0].astype(F32)))
    lane = lax.broadcasted_iota(jnp.int32, (rows, LANES), 1)
    meta = jnp.zeros((rows, LANES), F32)
    for i, value in enumerate(columns):
        meta = jnp.where(lane == i, value, meta)
    out[:, width:] = meta.astype(BF16)
    for copy in copies[4:]:
        copy.wait()


def prep(hidden, exit_depth, teacher, normalizer, depth_gain, depth_bias):
    rows, width = hidden.shape
    return pl.pallas_call(
        prep_kernel,
        out_shape=(
            pltpu.VMEM((rows, width + LANES), BF16),
            pltpu.VMEM(depth_gain.shape, F32),
            pltpu.VMEM(depth_bias.shape, F32),
        ),
        in_specs=[HBM] * 6,
        out_specs=(VMEM, VMEM, VMEM),
        scratch_shapes=[
            pltpu.VMEM((rows, width), BF16),
            pltpu.VMEM((2, 1, rows), jnp.int32),
            pltpu.VMEM((1, rows), F32),
            pltpu.SemaphoreType.DMA((6,)),
        ],
        compiler_params=pltpu.CompilerParams(vmem_limit_bytes=8 << 20),
    )(
        in_hbm(hidden),
        in_hbm(exit_depth.reshape(1, rows)),
        in_hbm(teacher.reshape(1, rows)),
        in_hbm(normalizer.reshape(1, rows)),
        in_hbm(depth_gain),
        in_hbm(depth_bias),
    )


def hop_pairs(order, step, cross):
    chips = len(order)
    first = 1 - step % 2
    pairs = []
    for i in range(chips):
        here, after = 2 * order[i], 2 * order[(i + 1) % chips]
        if cross:
            pairs += [(here + first, after + 1 - first), (after + 1 - first, here + first)]
        else:
            pairs += [(here + 1 - first, after + 1 - first), (after + first, here + first)]
    return pairs


def gather_blocks(block, loop, head, mapper):
    chips = loop // 2
    order = ring_of(chips)
    half = chips // 2
    tie = lambda *xs: lax.optimization_barrier(xs)
    send = lambda x, pairs: lax.ppermute(x, "loop", pairs)
    swap = lambda x: send(x, [(i, i ^ 1) for i in range(loop)])
    blocks = [None] * loop
    first = swap(block)
    blocks[0], blocks[chips] = block, first
    crossed = plain = block
    ready = [0, chips]
    mapped = None
    for step in range(1, half + 1):
        crossed = send(crossed, hop_pairs(order, step, True))
        if step < half:
            plain = send(plain, hop_pairs(order, step, step > 1))
        if step == 1:
            crossed, plain, head, first = tie(crossed, plain, head, first)
            blocks[chips] = first
        if mapper is not None and step == 3:
            mapped = mapper(None, {i: blocks[i] for i in ready[:6]})
            plain, mapped = tie(plain, mapped)
        if mapper is not None and step == half:
            mapped = mapper(mapped, {i: blocks[i] for i in ready[6:12]})
            crossed, mapped = tie(crossed, mapped)
        far = step if step % 2 else chips - step
        near = chips - far
        mine, theirs = (chips, 0) if step % 2 else (0, chips)
        blocks[mine + far] = crossed
        if step < half:
            blocks[theirs + far] = plain
            blocks[theirs + near] = swap(crossed)
            blocks[mine + near] = swap(plain)
            ready += [mine + far, theirs + far, theirs + near, mine + near]
        else:
            blocks[theirs + far] = swap(crossed)
            ready += [mine + far, theirs + far]
    return blocks, head, mapped, ready[12:] if mapper is not None else ready


def map_rows(block, gain, bias, mapped, first):
    rows, width = block.shape[0], mapped.shape[1]
    levels = gain.shape[0]
    meta = block[:, width:].astype(F32)
    scale = (meta[:, 0:1] + meta[:, 1:2]) + meta[:, 2:3]
    depth = meta[:, 9:10]
    cuts = 3 if width % (3 * LANES) == 0 else 1
    cut = width // cuts
    for k in range(cuts):
        at = slice(k * cut, (k + 1) * cut)
        g, c = gain[0:1, at], bias[0:1, at]
        for level in range(1, levels):
            here = depth == float(level)
            g = jnp.where(here, gain[level : level + 1, at], g)
            c = jnp.where(here, bias[level : level + 1, at], c)
        value = (block[:, at].astype(F32) * scale) * g + c
        mapped[first : first + rows, at] = value.astype(BF16)


def map_kernel(places, *refs):
    blocks = refs[: len(places)]
    gain, bias = refs[len(places) : len(places) + 2]
    for place, block in zip(places, blocks):
        map_rows(block, gain, bias, refs[-1], place * block.shape[0])


def map_early(rows, gain, bias, mapped, blocks):
    places, blocks = list(blocks), list(blocks.values())
    width = gain.shape[1]
    operands = blocks + [gain, bias] + ([] if mapped is None else [mapped])
    count = len(blocks) * blocks[0].shape[0]
    return pl.pallas_call(
        functools.partial(map_kernel, places),
        out_shape=pltpu.VMEM((rows, width), BF16),
        in_specs=[VMEM] * len(operands),
        out_specs=VMEM,
        input_output_aliases={} if mapped is None else {len(operands) - 1: 0},
        compiler_params=pltpu.CompilerParams(vmem_limit_bytes=8 << 20),
        cost_estimate=pl.CostEstimate(
            flops=20 * count * width, bytes_accessed=4 * count * width, transcendentals=0
        ),
    )(*operands)


def load_kernel(head_hbm, head, sems):
    parts = sems.shape[0]
    size = head.shape[0] // parts
    copies = [
        pltpu.make_async_copy(
            head_hbm.at[pl.ds(k * size, size)], head.at[pl.ds(k * size, size)], sems.at[k]
        )
        for k in range(parts)
    ]
    for copy in copies:
        copy.start()
    for copy in copies:
        copy.wait()


def load(tied_head):
    return pl.pallas_call(
        load_kernel,
        out_shape=pltpu.VMEM(tied_head.shape, BF16),
        in_specs=[HBM],
        out_specs=VMEM,
        scratch_shapes=[pltpu.SemaphoreType.DMA((4,))],
        compiler_params=pltpu.CompilerParams(vmem_limit_bytes=16 << 20),
        cost_estimate=pl.CostEstimate(
            flops=0, bytes_accessed=4 * tied_head.shape[0] * tied_head.shape[1], transcendentals=0
        ),
    )(in_hbm(tied_head))


def main_kernel(loop, levels, count, late, *refs):
    blocks = refs[:count]
    head, gain, bias = refs[count : count + 3]
    keep, give, mapped, out, slopes = refs[-5:]
    voc, width = head.shape
    rows = mapped.shape[0]
    rows_dev = rows // loop
    chips = loop // 2
    me = lax.axis_index("loop")
    meta = jnp.concatenate([b[:, width:] for b in blocks], axis=0).astype(F32)
    col = lambda i: meta[:, i : i + 1]
    scale = (col(0) + col(1)) + col(2)
    norm = (col(3) + col(4)) + col(5)
    target = (col(6) + 128.0 * col(7) + 16384.0 * col(8)).astype(jnp.int32)
    depth = col(9)

    for i in late:
        map_rows(blocks[i], gain, bias, mapped, i * blocks[i].shape[0])
    logits = lax.dot_general(mapped[...], head[...], NT, preferred_element_type=F32)
    prob = jnp.exp(logits - norm)
    columns = me * voc + lax.broadcasted_iota(jnp.int32, (rows, voc), 1)
    slopes[:rows, :] = jnp.where(columns == target, prob - 1.0, prob).astype(BF16)

    mass = prob[:, :LANES]
    for j in range(1, voc // LANES):
        mass = mass + prob[:, j * LANES : (j + 1) * LANES]
    mass = jnp.sum(mass.T, axis=0, keepdims=True)
    index = lax.broadcasted_iota(jnp.int32, (rows, rows), 0)
    flip = index // (rows // 2)
    relative = (index - flip * (rows // 2)) // rows_dev
    core = me % 2
    place = place_of(me // 2, chips) + jnp.where(core == 0, relative, chips - relative)
    place = jnp.where(place >= chips, place - chips, place)
    owner = 2 * chip_at(place, chips) + jnp.where(flip == 0, core, 1 - core)
    goes_to = owner * rows_dev + index % rows_dev
    move = goes_to == lax.broadcasted_iota(jnp.int32, (rows, rows), 1)
    move = jnp.where(move, 1.0, 0.0).astype(BF16)
    lines = jnp.concatenate(pieces(mass) + [jnp.zeros((13, rows), F32)], axis=0)
    moved = jnp.dot(lines.astype(BF16), move, preferred_element_type=F32)
    moved = (moved[0:1] + moved[1:2]) + moved[2:3]
    out[:, width:] = jnp.broadcast_to(moved, (2 * levels, rows))

    lane = lax.broadcasted_iota(jnp.int32, (rows, LANES), 1).astype(F32)
    pick = jnp.where(lane == depth, 1.0, 0.0).T[:levels]
    scaled = pick * jnp.broadcast_to(scale, (rows, LANES)).T[:levels]
    none = jnp.zeros((16 - 3 * levels, rows), F32)
    scaled = jnp.concatenate(pieces(scaled) + [none], axis=0).astype(BF16)
    sums = jnp.dot(pick.astype(BF16), slopes[:rows, :], preferred_element_type=F32)
    none = jnp.zeros((16 - 3 * levels, voc), F32)
    slopes[rows:, :] = jnp.concatenate(pieces(sums) + [none], axis=0).astype(BF16)
    add3 = lambda x: (x[:levels] + x[levels : 2 * levels]) + x[2 * levels : 3 * levels]
    for k in range(width // 256):
        at = slice(k * 256, (k + 1) * 256)
        back = jnp.dot(slopes[...], head[:, at], preferred_element_type=F32)
        wide = jnp.concatenate([b[:, at] for b in blocks], axis=0).astype(F32)
        mapped[:, at] = (back[:rows] * wide).astype(BF16)
        out[levels : 2 * levels, at] = add3(back[rows:])
    out[:levels, :width] = add3(jnp.dot(scaled, mapped[...], preferred_element_type=F32))
    middle = out.shape[1] // 2
    low, high = out[:, :middle], out[:, middle:]
    keep[...] = jnp.where(core == 0, low, high)
    give[...] = jnp.where(core == 0, high, low)


def main(blocks, head, gain, bias, mapped, late, loop):
    levels = gain.shape[0]
    voc, width = head.shape
    rows = sum(b.shape[0] for b in blocks)
    columns = width + rows
    half = pltpu.VMEM((2 * levels, columns // 2), F32)
    operands = list(blocks) + [head, gain, bias] + ([] if mapped is None else [mapped])
    return pl.pallas_call(
        functools.partial(main_kernel, loop, levels, len(blocks), late),
        out_shape=(half, half, pltpu.VMEM((rows, width), BF16)),
        in_specs=[VMEM] * len(operands),
        out_specs=(VMEM, VMEM, VMEM),
        input_output_aliases={} if mapped is None else {len(operands) - 1: 2},
        scratch_shapes=[
            pltpu.VMEM((2 * levels, columns), F32),
            pltpu.VMEM((rows + 16, voc), BF16),
        ],
        compiler_params=pltpu.CompilerParams(vmem_limit_bytes=20 << 20),
        cost_estimate=pl.CostEstimate(
            flops=4 * rows * voc * width,
            bytes_accessed=2 * voc * width,
            transcendentals=rows * voc,
        ),
    )(*operands)[:2]


def sum_over_loop(keep, give, loop):
    swap = lambda x: lax.ppermute(x, "loop", [(i, i ^ 1) for i in range(loop)])
    total = keep + swap(give)
    bit = 2
    while bit < loop:
        pairs = [(i, i ^ bit) for i in range(loop)]
        total = lax.reduce_precision(total, 8, 7)
        total = total + lax.ppermute(total.astype(BF16), "loop", pairs).astype(F32)
        bit *= 2
    return total, swap(total)


def last_kernel(levels, rows, kept, given, mass_out, gain_out, bias_out, buf, line, sems):
    width = gain_out.shape[1]
    me = lax.axis_index("loop")
    middle = kept.shape[1]
    buf[:, :middle] = jnp.where(me % 2 == 0, kept[...], given[...])
    buf[:, middle:] = jnp.where(me % 2 == 0, given[...], kept[...])
    every = buf[0:1, width:]
    spread = lax.broadcasted_iota(jnp.int32, (every.shape[1], LANES), 0)
    target = lax.broadcasted_iota(jnp.int32, (every.shape[1], LANES), 1)
    move = jnp.where(spread - me * rows == target, 1.0, 0.0).astype(BF16)
    lines = jnp.concatenate(pieces(every) + [jnp.zeros((13, every.shape[1]), F32)], axis=0)
    own = jnp.dot(lines.astype(BF16), move, preferred_element_type=F32)
    line[...] = ((own[0:1] + own[1:2]) + own[2:3])[:, :rows]
    copies = [
        pltpu.make_async_copy(buf.at[pl.ds(0, levels), pl.ds(0, width)], gain_out, sems.at[0]),
        pltpu.make_async_copy(buf.at[pl.ds(levels, levels), pl.ds(0, width)], bias_out, sems.at[1]),
        pltpu.make_async_copy(line, mass_out, sems.at[2]),
    ]
    for copy in copies:
        copy.start()
    for copy in copies:
        copy.wait()


def last(kept, given, levels, width, rows):
    grad = pltpu.HBM((levels, width), F32)
    mass, gain, bias = pl.pallas_call(
        functools.partial(last_kernel, levels, rows),
        out_shape=(pltpu.HBM((1, rows), F32), grad, grad),
        in_specs=[VMEM, VMEM],
        out_specs=(HBM, HBM, HBM),
        scratch_shapes=[
            pltpu.VMEM((kept.shape[0], 2 * kept.shape[1]), F32),
            pltpu.VMEM((1, rows), F32),
            pltpu.SemaphoreType.DMA((3,)),
        ],
        compiler_params=pltpu.CompilerParams(vmem_limit_bytes=8 << 20),
    )(kept, given)
    return mass.reshape(rows), gain, bias


def shards(loop, hidden, exit_depth, teacher, normalizer, tied_head, depth_gain, depth_bias):
    rows_dev, width = hidden.shape
    levels = depth_gain.shape[0]
    block, gain, bias = prep(hidden, exit_depth, teacher, normalizer, depth_gain, depth_bias)
    rows = rows_dev * loop
    early = rows_dev % 16 == 0 and loop == 16
    mapper = functools.partial(map_early, rows, gain, bias) if early else None
    blocks, head, mapped, late = gather_blocks(block, loop, load(tied_head), mapper)
    if rows_dev % 16:
        whole = jnp.concatenate(blocks, axis=0)
        blocks = [whole[i : i + 16] for i in range(0, rows, 16)]
        late = range(len(blocks))
    keep, give = main(blocks, head, gain, bias, mapped, late, loop)
    return last(*sum_over_loop(keep, give, loop), levels, width, rows_dev)


def solution(mesh):
    loop = mesh.shape["loop"]

    def body(*args):
        return shards(loop, *args)

    return jax.shard_map(
        body,
        mesh=mesh,
        in_specs=(
            P(("groups", "loop"), None),
            P(("groups", "loop")),
            P(("groups", "loop")),
            P(("groups", "loop")),
            P("loop", None),
            P(),
            P(),
        ),
        out_specs=(P(("groups", "loop")), P("groups", None), P("groups", None)),
        check_vma=False,
    )
```

```python
import functools

import jax
import jax.numpy as jnp
from jax import lax
from jax.experimental import pallas as pl
from jax.experimental.pallas import tpu as pltpu
from jax.sharding import PartitionSpec as P

BF16 = jnp.bfloat16
F32 = jnp.float32
LANES = 128
NT = (((1,), (1,)), ((), ()))
VMEM = pl.BlockSpec(memory_space=pltpu.VMEM)
HBM = pl.BlockSpec(memory_space=pl.ANY)


def in_hbm(x):
    return pltpu.with_memory_space_constraint(x, pltpu.HBM)


def ring_of(chips):
    return list(range(0, chips, 2)) + list(range(chips - 1, 0, -2))


def chip_at(place, chips):
    return jnp.where(place < chips // 2, 2 * place, 2 * (chips - 1 - place) + 1)


def place_of(chip, chips):
    return jnp.where(chip % 2 == 0, chip // 2, chips - 1 - chip // 2)


def pieces(value):
    top = value.astype(BF16).astype(F32)
    rest = value - top
    middle = rest.astype(BF16).astype(F32)
    return [top, middle, rest - middle]


def prep_kernel(
    hidden, exit_depth, teacher, normalizer, depth_gain, depth_bias,
    out, gain_out, bias_out, row_buf, int_buf, float_buf, sems,
):
    rows, width = hidden.shape
    copies = [
        pltpu.make_async_copy(hidden, row_buf, sems.at[0]),
        pltpu.make_async_copy(exit_depth, int_buf.at[0], sems.at[1]),
        pltpu.make_async_copy(teacher, int_buf.at[1], sems.at[2]),
        pltpu.make_async_copy(normalizer, float_buf, sems.at[3]),
        pltpu.make_async_copy(depth_gain, gain_out, sems.at[4]),
        pltpu.make_async_copy(depth_bias, bias_out, sems.at[5]),
    ]
    for copy in copies:
        copy.start()
    for copy in copies[:4]:
        copy.wait()
    block = row_buf[...]
    out[:, :width] = block
    wide = block.astype(F32)
    mean = jnp.sum(wide * wide, axis=1, keepdims=True) * (1.0 / width)
    scale = lax.rsqrt(mean + 1e-06)
    down = lax.broadcasted_iota(jnp.int32, (rows, rows), 0)
    across = lax.broadcasted_iota(jnp.int32, (rows, rows), 1)

    def column(line):
        square = jnp.broadcast_to(line, (rows, rows))
        return jnp.sum(jnp.where(down == across, square, 0.0), axis=1, keepdims=True)

    token = int_buf[1]
    columns = pieces(scale) + pieces(column(float_buf[...]))
    for digit in (token & 127, (token >> 7) & 127, token >> 14):
        columns.append(column(digit.astype(F32)))
    columns.append(column(int_buf[0].astype(F32)))
    lane = lax.broadcasted_iota(jnp.int32, (rows, LANES), 1)
    meta = jnp.zeros((rows, LANES), F32)
    for i, value in enumerate(columns):
        meta = jnp.where(lane == i, value, meta)
    out[:, width:] = meta.astype(BF16)
    for copy in copies[4:]:
        copy.wait()


def prep(hidden, exit_depth, teacher, normalizer, depth_gain, depth_bias):
    rows, width = hidden.shape
    return pl.pallas_call(
        prep_kernel,
        out_shape=(
            pltpu.VMEM((rows, width + LANES), BF16),
            pltpu.VMEM(depth_gain.shape, F32),
            pltpu.VMEM(depth_bias.shape, F32),
        ),
        in_specs=[HBM] * 6,
        out_specs=(VMEM, VMEM, VMEM),
        scratch_shapes=[
            pltpu.VMEM((rows, width), BF16),
            pltpu.VMEM((2, 1, rows), jnp.int32),
            pltpu.VMEM((1, rows), F32),
            pltpu.SemaphoreType.DMA((6,)),
        ],
        compiler_params=pltpu.CompilerParams(vmem_limit_bytes=8 << 20),
    )(
        in_hbm(hidden),
        in_hbm(exit_depth.reshape(1, rows)),
        in_hbm(teacher.reshape(1, rows)),
        in_hbm(normalizer.reshape(1, rows)),
        in_hbm(depth_gain),
        in_hbm(depth_bias),
    )


def hop_pairs(order, step, cross):
    chips = len(order)
    first = 1 - step % 2
    pairs = []
    for i in range(chips):
        here, after = 2 * order[i], 2 * order[(i + 1) % chips]
        if cross:
            pairs += [(here + first, after + 1 - first), (after + 1 - first, here + first)]
        else:
            pairs += [(here + 1 - first, after + 1 - first), (after + first, here + first)]
    return pairs


def gather_blocks(block, loop, tied_head, mapper):
    chips = loop // 2
    order = ring_of(chips)
    half = chips // 2
    tie = lambda *xs: lax.optimization_barrier(xs)
    send = lambda x, pairs: lax.ppermute(x, "loop", pairs)
    swap = lambda x: send(x, [(i, i ^ 1) for i in range(loop)])
    blocks = [None] * loop
    first = swap(block)
    blocks[0], blocks[chips] = block, first
    crossed = plain = block
    ready = [0, chips]
    mapped = None
    for step in range(1, half + 1):
        crossed = send(crossed, hop_pairs(order, step, True))
        if step < half:
            plain = send(plain, hop_pairs(order, step, step > 1))
        if step == 1:
            head = load(tied_head, 0, 2)
            crossed, plain, head = tie(crossed, plain, head)
        if step == min(2, half):
            head = load(tied_head, 1, 2, head)
            crossed, plain, head, first = tie(crossed, plain, head, first)
            blocks[chips] = first
        if mapper is not None and step == 3:
            mapped = mapper(None, {i: blocks[i] for i in ready[:6]})
            plain, mapped = tie(plain, mapped)
        if mapper is not None and step == half:
            mapped = mapper(mapped, {i: blocks[i] for i in ready[6:12]})
            crossed, mapped = tie(crossed, mapped)
        far = step if step % 2 else chips - step
        near = chips - far
        mine, theirs = (chips, 0) if step % 2 else (0, chips)
        blocks[mine + far] = crossed
        if step < half:
            blocks[theirs + far] = plain
            blocks[theirs + near] = swap(crossed)
            blocks[mine + near] = swap(plain)
            ready += [mine + far, theirs + far, theirs + near, mine + near]
        else:
            blocks[theirs + far] = swap(crossed)
            ready += [mine + far, theirs + far]
    return blocks, head, mapped, ready[12:] if mapper is not None else ready


def map_rows(block, gain, bias, mapped, first):
    rows, width = block.shape[0], mapped.shape[1]
    levels = gain.shape[0]
    meta = block[:, width:].astype(F32)
    scale = (meta[:, 0:1] + meta[:, 1:2]) + meta[:, 2:3]
    depth = meta[:, 9:10]
    cuts = 3 if width % (3 * LANES) == 0 else 1
    cut = width // cuts
    for k in range(cuts):
        at = slice(k * cut, (k + 1) * cut)
        g, c = gain[0:1, at], bias[0:1, at]
        for level in range(1, levels):
            here = depth == float(level)
            g = jnp.where(here, gain[level : level + 1, at], g)
            c = jnp.where(here, bias[level : level + 1, at], c)
        value = (block[:, at].astype(F32) * scale) * g + c
        mapped[first : first + rows, at] = value.astype(BF16)


def map_kernel(places, *refs):
    blocks = refs[: len(places)]
    gain, bias = refs[len(places) : len(places) + 2]
    for place, block in zip(places, blocks):
        map_rows(block, gain, bias, refs[-1], place * block.shape[0])


def map_early(rows, gain, bias, mapped, blocks):
    places, blocks = list(blocks), list(blocks.values())
    width = gain.shape[1]
    operands = blocks + [gain, bias] + ([] if mapped is None else [mapped])
    count = len(blocks) * blocks[0].shape[0]
    return pl.pallas_call(
        functools.partial(map_kernel, places),
        out_shape=pltpu.VMEM((rows, width), BF16),
        in_specs=[VMEM] * len(operands),
        out_specs=VMEM,
        input_output_aliases={} if mapped is None else {len(operands) - 1: 0},
        compiler_params=pltpu.CompilerParams(vmem_limit_bytes=8 << 20),
        cost_estimate=pl.CostEstimate(
            flops=20 * count * width, bytes_accessed=4 * count * width, transcendentals=0
        ),
    )(*operands)


def load_kernel(part, parts, head_hbm, *refs):
    head, sems = refs[-2:]
    count = sems.shape[0]
    size = head.shape[0] // (parts * count)
    copies = []
    for k in range(count):
        at = pl.ds((part * count + k) * size, size)
        copies.append(pltpu.make_async_copy(head_hbm.at[at], head.at[at], sems.at[k]))
    for copy in copies:
        copy.start()
    for copy in copies:
        copy.wait()


def load(tied_head, part, parts, loaded=None):
    operands = [in_hbm(tied_head)] + ([] if loaded is None else [loaded])
    voc, width = tied_head.shape
    return pl.pallas_call(
        functools.partial(load_kernel, part, parts),
        out_shape=pltpu.VMEM(tied_head.shape, BF16),
        in_specs=[HBM] + [VMEM] * (len(operands) - 1),
        out_specs=VMEM,
        input_output_aliases={} if loaded is None else {1: 0},
        scratch_shapes=[pltpu.SemaphoreType.DMA((4,))],
        compiler_params=pltpu.CompilerParams(vmem_limit_bytes=16 << 20),
        cost_estimate=pl.CostEstimate(
            flops=0, bytes_accessed=4 * voc * width // parts, transcendentals=0
        ),
    )(*operands)


def half_sums(blocks, head, slopes, scaled, mass, which, work, out):
    levels = out.shape[0] // 2
    rows = sum(b.shape[0] for b in blocks)
    half = head.shape[1] // 2
    add3 = lambda x: (x[:levels] + x[levels : 2 * levels]) + x[2 * levels : 3 * levels]
    done = 0
    while done < half:
        size = min(256, half - done)
        here = slice(done, done + size)
        at = pl.ds(pl.multiple_of(which * half + done, LANES), size)
        back = jnp.dot(slopes[...], head[:, at], preferred_element_type=F32)
        wide = jnp.concatenate([b[:, at] for b in blocks], axis=0).astype(F32)
        work[:, here] = (back[:rows] * wide).astype(BF16)
        out[levels:, here] = add3(back[rows:])
        done += size
    out[:levels, :half] = add3(jnp.dot(scaled, work[:, :half], preferred_element_type=F32))
    out[:, half:] = jnp.broadcast_to(mass, (2 * levels, mass.shape[1]))


def front_kernel(loop, levels, count, late, *refs):
    blocks = refs[:count]
    head, gain, bias = refs[count : count + 3]
    give, slopes, scaled_out, mass_out, mapped = refs[-5:]
    voc, width = head.shape
    rows = mapped.shape[0]
    rows_dev = rows // loop
    chips = loop // 2
    me = lax.axis_index("loop")
    core = me % 2
    meta = jnp.concatenate([b[:, width:] for b in blocks], axis=0).astype(F32)
    col = lambda i: meta[:, i : i + 1]
    scale = (col(0) + col(1)) + col(2)
    norm = (col(3) + col(4)) + col(5)
    target = (col(6) + 128.0 * col(7) + 16384.0 * col(8)).astype(jnp.int32)
    depth = col(9)

    for i in late:
        map_rows(blocks[i], gain, bias, mapped, i * blocks[i].shape[0])
    logits = lax.dot_general(mapped[...], head[...], NT, preferred_element_type=F32)
    prob = jnp.exp(logits - norm)
    columns = me * voc + lax.broadcasted_iota(jnp.int32, (rows, voc), 1)
    slopes[:rows, :] = jnp.where(columns == target, prob - 1.0, prob).astype(BF16)

    mass = prob[:, :LANES]
    for j in range(1, voc // LANES):
        mass = mass + prob[:, j * LANES : (j + 1) * LANES]
    mass = jnp.sum(mass.T, axis=0, keepdims=True)
    index = lax.broadcasted_iota(jnp.int32, (rows, rows), 0)
    flip = index // (rows // 2)
    relative = (index - flip * (rows // 2)) // rows_dev
    place = place_of(me // 2, chips) + jnp.where(core == 0, relative, chips - relative)
    place = jnp.where(place >= chips, place - chips, place)
    owner = 2 * chip_at(place, chips) + jnp.where(flip == 0, core, 1 - core)
    goes_to = owner * rows_dev + index % rows_dev
    move = goes_to == lax.broadcasted_iota(jnp.int32, (rows, rows), 1)
    move = jnp.where(move, 1.0, 0.0).astype(BF16)
    lines = jnp.concatenate(pieces(mass) + [jnp.zeros((13, rows), F32)], axis=0)
    moved = jnp.dot(lines.astype(BF16), move, preferred_element_type=F32)
    moved = (moved[0:1] + moved[1:2]) + moved[2:3]
    low, high = moved[:, : rows // 2], moved[:, rows // 2 :]
    mass_out[...] = jnp.where(core == 0, low, high)

    lane = lax.broadcasted_iota(jnp.int32, (rows, LANES), 1).astype(F32)
    pick = jnp.where(lane == depth, 1.0, 0.0).T[:levels]
    scaled = pick * jnp.broadcast_to(scale, (rows, LANES)).T[:levels]
    none = jnp.zeros((16 - 3 * levels, rows), F32)
    scaled = jnp.concatenate(pieces(scaled) + [none], axis=0).astype(BF16)
    scaled_out[...] = scaled
    sums = jnp.dot(pick.astype(BF16), slopes[:rows, :], preferred_element_type=F32)
    none = jnp.zeros((16 - 3 * levels, voc), F32)
    slopes[rows:, :] = jnp.concatenate(pieces(sums) + [none], axis=0).astype(BF16)
    other = jnp.where(core == 0, high, low)
    half_sums(blocks, head, slopes, scaled, other, 1 - core, mapped, give)


def back_kernel(count, *refs):
    blocks = refs[:count]
    head, slopes, scaled, mass, keep, work = refs[count:]
    core = lax.axis_index("loop") % 2
    half_sums(blocks, head, slopes, scaled[...], mass[...], core, work, keep)


def main(blocks, head, gain, bias, mapped, late, loop):
    levels = gain.shape[0]
    voc, width = head.shape
    rows = sum(b.shape[0] for b in blocks)
    half = pltpu.VMEM((2 * levels, (width + rows) // 2), F32)
    operands = list(blocks) + [head, gain, bias] + ([] if mapped is None else [mapped])
    cost = lambda passes: pl.CostEstimate(
        flops=passes * rows * voc * width, bytes_accessed=voc * width, transcendentals=0
    )
    give, slopes, scaled, mass, _ = pl.pallas_call(
        functools.partial(front_kernel, loop, levels, len(blocks), late),
        out_shape=(
            half,
            pltpu.VMEM((rows + 16, voc), BF16),
            pltpu.VMEM((16, rows), BF16),
            pltpu.VMEM((1, rows // 2), F32),
            pltpu.VMEM((rows, width), BF16),
        ),
        in_specs=[VMEM] * len(operands),
        out_specs=(VMEM,) * 5,
        input_output_aliases={} if mapped is None else {len(operands) - 1: 4},
        compiler_params=pltpu.CompilerParams(vmem_limit_bytes=16 << 20),
        cost_estimate=cost(3),
    )(*operands)
    operands = list(blocks) + [head, slopes, scaled, mass]
    keep = pl.pallas_call(
        functools.partial(back_kernel, len(blocks)),
        out_shape=half,
        in_specs=[VMEM] * len(operands),
        out_specs=VMEM,
        scratch_shapes=[pltpu.VMEM((rows, width // 2), BF16)],
        compiler_params=pltpu.CompilerParams(vmem_limit_bytes=16 << 20),
        cost_estimate=cost(1),
    )(*operands)
    return keep, give


def sum_over_loop(keep, give, loop):
    send = lambda x, mask: lax.ppermute(x, "loop", [(i, i ^ mask) for i in range(loop)])
    total = keep + send(give, 1)
    bits = [1 << k for k in range(1, loop.bit_length() - 1)]
    for k in range(0, len(bits) - 1, 2):
        dims = bits[:-1][k : k + 2]
        total = lax.reduce_precision(total, 8, 7)
        sent = total.astype(BF16)
        take = lambda mask: send(sent, mask).astype(F32)
        total = total + take(dims[0])
        if len(dims) == 2:
            total = total + (take(dims[1]) + take(dims[0] ^ dims[1]))
    total = lax.reduce_precision(total, 8, 7)
    sent = total.astype(BF16)
    take = lambda mask: send(sent, mask).astype(F32)
    return total + take(bits[-1]), take(1) + take(bits[-1] ^ 1)


def last_kernel(levels, rows, kept, given, mass_out, gain_out, bias_out, buf, line, sems):
    width = gain_out.shape[1]
    me = lax.axis_index("loop")
    cut = width // 2
    low = jnp.where(me % 2 == 0, kept[...], given[...])
    high = jnp.where(me % 2 == 0, given[...], kept[...])
    buf[:, :cut], buf[:, cut:width] = low[:, :cut], high[:, :cut]
    buf[:, width:] = jnp.concatenate([low[:, cut:], high[:, cut:]], axis=1)
    every = buf[0:1, width:]
    spread = lax.broadcasted_iota(jnp.int32, (every.shape[1], LANES), 0)
    target = lax.broadcasted_iota(jnp.int32, (every.shape[1], LANES), 1)
    move = jnp.where(spread - me * rows == target, 1.0, 0.0).astype(BF16)
    lines = jnp.concatenate(pieces(every) + [jnp.zeros((13, every.shape[1]), F32)], axis=0)
    own = jnp.dot(lines.astype(BF16), move, preferred_element_type=F32)
    line[...] = ((own[0:1] + own[1:2]) + own[2:3])[:, :rows]
    copies = [
        pltpu.make_async_copy(buf.at[pl.ds(0, levels), pl.ds(0, width)], gain_out, sems.at[0]),
        pltpu.make_async_copy(buf.at[pl.ds(levels, levels), pl.ds(0, width)], bias_out, sems.at[1]),
        pltpu.make_async_copy(line, mass_out, sems.at[2]),
    ]
    for copy in copies:
        copy.start()
    for copy in copies:
        copy.wait()


def last(kept, given, levels, width, rows):
    grad = pltpu.HBM((levels, width), F32)
    mass, gain, bias = pl.pallas_call(
        functools.partial(last_kernel, levels, rows),
        out_shape=(pltpu.HBM((1, rows), F32), grad, grad),
        in_specs=[VMEM, VMEM],
        out_specs=(HBM, HBM, HBM),
        scratch_shapes=[
            pltpu.VMEM((kept.shape[0], 2 * kept.shape[1]), F32),
            pltpu.VMEM((1, rows), F32),
            pltpu.SemaphoreType.DMA((3,)),
        ],
        compiler_params=pltpu.CompilerParams(vmem_limit_bytes=8 << 20),
    )(kept, given)
    return mass.reshape(rows), gain, bias


def shards(loop, hidden, exit_depth, teacher, normalizer, tied_head, depth_gain, depth_bias):
    rows_dev, width = hidden.shape
    levels = depth_gain.shape[0]
    block, gain, bias = prep(hidden, exit_depth, teacher, normalizer, depth_gain, depth_bias)
    rows = rows_dev * loop
    early = rows_dev % 16 == 0 and loop == 16
    mapper = functools.partial(map_early, rows, gain, bias) if early else None
    blocks, head, mapped, late = gather_blocks(block, loop, tied_head, mapper)
    if rows_dev % 16:
        whole = jnp.concatenate(blocks, axis=0)
        blocks = [whole[i : i + 16] for i in range(0, rows, 16)]
        late = range(len(blocks))
    keep, give = main(blocks, head, gain, bias, mapped, late, loop)
    return last(*sum_over_loop(keep, give, loop), levels, width, rows_dev)


def solution(mesh):
    loop = mesh.shape["loop"]

    def body(*args):
        return shards(loop, *args)

    return jax.shard_map(
        body,
        mesh=mesh,
        in_specs=(
            P(("groups", "loop"), None),
            P(("groups", "loop")),
            P(("groups", "loop")),
            P(("groups", "loop")),
            P("loop", None),
            P(),
            P(),
        ),
        out_specs=(P(("groups", "loop")), P("groups", None), P("groups", None)),
        check_vma=False,
    )
```

```python
import functools

import jax
import jax.numpy as jnp
from jax import lax
from jax.experimental import pallas as pl
from jax.experimental.pallas import tpu as pltpu
from jax.sharding import PartitionSpec as P

BF16 = jnp.bfloat16
F32 = jnp.float32
LANES = 128
NT = (((1,), (1,)), ((), ()))
VMEM = pl.BlockSpec(memory_space=pltpu.VMEM)
HBM = pl.BlockSpec(memory_space=pl.ANY)


def in_hbm(x):
    return pltpu.with_memory_space_constraint(x, pltpu.HBM)


def ring_of(chips):
    return list(range(0, chips, 2)) + list(range(chips - 1, 0, -2))


def chip_at(place, chips):
    return jnp.where(place < chips // 2, 2 * place, 2 * (chips - 1 - place) + 1)


def place_of(chip, chips):
    return jnp.where(chip % 2 == 0, chip // 2, chips - 1 - chip // 2)


def pieces(value):
    top = value.astype(BF16).astype(F32)
    rest = value - top
    middle = rest.astype(BF16).astype(F32)
    return [top, middle, rest - middle]


def prep_kernel(
    hidden, exit_depth, teacher, normalizer, depth_gain, depth_bias,
    out, gain_out, bias_out, row_buf, int_buf, float_buf, sems,
):
    rows, width = hidden.shape
    copies = [
        pltpu.make_async_copy(hidden, row_buf, sems.at[0]),
        pltpu.make_async_copy(exit_depth, int_buf.at[0], sems.at[1]),
        pltpu.make_async_copy(teacher, int_buf.at[1], sems.at[2]),
        pltpu.make_async_copy(normalizer, float_buf, sems.at[3]),
        pltpu.make_async_copy(depth_gain, gain_out, sems.at[4]),
        pltpu.make_async_copy(depth_bias, bias_out, sems.at[5]),
    ]
    for copy in copies:
        copy.start()
    for copy in copies[:4]:
        copy.wait()
    block = row_buf[...]
    out[:, :width] = block
    wide = block.astype(F32)
    mean = jnp.sum(wide * wide, axis=1, keepdims=True) * (1.0 / width)
    scale = lax.rsqrt(mean + 1e-06)
    down = lax.broadcasted_iota(jnp.int32, (rows, rows), 0)
    across = lax.broadcasted_iota(jnp.int32, (rows, rows), 1)

    def column(line):
        square = jnp.broadcast_to(line, (rows, rows))
        return jnp.sum(jnp.where(down == across, square, 0.0), axis=1, keepdims=True)

    token = int_buf[1]
    columns = pieces(scale) + pieces(column(float_buf[...]))
    for digit in (token & 127, (token >> 7) & 127, token >> 14):
        columns.append(column(digit.astype(F32)))
    columns.append(column(int_buf[0].astype(F32)))
    lane = lax.broadcasted_iota(jnp.int32, (rows, LANES), 1)
    meta = jnp.zeros((rows, LANES), F32)
    for i, value in enumerate(columns):
        meta = jnp.where(lane == i, value, meta)
    out[:, width:] = meta.astype(BF16)
    for copy in copies[4:]:
        copy.wait()


def prep(hidden, exit_depth, teacher, normalizer, depth_gain, depth_bias):
    rows, width = hidden.shape
    return pl.pallas_call(
        prep_kernel,
        out_shape=(
            pltpu.VMEM((rows, width + LANES), BF16),
            pltpu.VMEM(depth_gain.shape, F32),
            pltpu.VMEM(depth_bias.shape, F32),
        ),
        in_specs=[HBM] * 6,
        out_specs=(VMEM, VMEM, VMEM),
        scratch_shapes=[
            pltpu.VMEM((rows, width), BF16),
            pltpu.VMEM((2, 1, rows), jnp.int32),
            pltpu.VMEM((1, rows), F32),
            pltpu.SemaphoreType.DMA((6,)),
        ],
        compiler_params=pltpu.CompilerParams(vmem_limit_bytes=8 << 20),
    )(
        in_hbm(hidden),
        in_hbm(exit_depth.reshape(1, rows)),
        in_hbm(teacher.reshape(1, rows)),
        in_hbm(normalizer.reshape(1, rows)),
        in_hbm(depth_gain),
        in_hbm(depth_bias),
    )


def hop_pairs(order, step, cross):
    chips = len(order)
    first = 1 - step % 2
    pairs = []
    for i in range(chips):
        here, after = 2 * order[i], 2 * order[(i + 1) % chips]
        if cross:
            pairs += [(here + first, after + 1 - first), (after + 1 - first, here + first)]
        else:
            pairs += [(here + 1 - first, after + 1 - first), (after + first, here + first)]
    return pairs


def gather_blocks(block, loop, tied_head, mapper):
    chips = loop // 2
    order = ring_of(chips)
    half = chips // 2
    tie = lambda *xs: lax.optimization_barrier(xs)
    send = lambda x, pairs: lax.ppermute(x, "loop", pairs)
    swap = lambda x: send(x, [(i, i ^ 1) for i in range(loop)])
    blocks = [None] * loop
    blocks[0], blocks[chips] = block, swap(block)
    crossed = plain = block
    ready = [0, chips]
    mapped = None
    for step in range(1, half + 1):
        crossed = send(crossed, hop_pairs(order, step, True))
        if step < half:
            plain = send(plain, hop_pairs(order, step, step > 1))
        if step == 1:
            head = load(tied_head, 0, 2)
            crossed, head = tie(crossed, head)
        if step == min(2, half):
            head = load(tied_head, 1, 2, head)
            plain, head = tie(plain, head)
        if mapper is not None and step == 3:
            mapped = mapper(None, {i: blocks[i] for i in ready[:6]})
            plain, mapped = tie(plain, mapped)
        if mapper is not None and step == half:
            mapped = mapper(mapped, {i: blocks[i] for i in ready[6:12]})
            crossed, mapped = tie(crossed, mapped)
        far = step if step % 2 else chips - step
        near = chips - far
        mine, theirs = (chips, 0) if step % 2 else (0, chips)
        blocks[mine + far] = crossed
        if step < half:
            blocks[theirs + far] = plain
            blocks[theirs + near] = swap(crossed)
            blocks[mine + near] = swap(plain)
            ready += [mine + far, theirs + far, theirs + near, mine + near]
        else:
            blocks[theirs + far] = swap(crossed)
            ready += [mine + far, theirs + far]
    return blocks, head, mapped, ready[12:] if mapper is not None else ready


def map_rows(block, gain, bias, mapped, first):
    rows, width = block.shape[0], mapped.shape[1]
    levels = gain.shape[0]
    meta = block[:, width:].astype(F32)
    scale = (meta[:, 0:1] + meta[:, 1:2]) + meta[:, 2:3]
    depth = meta[:, 9:10]
    cuts = 3 if width % (3 * LANES) == 0 else 1
    cut = width // cuts
    for k in range(cuts):
        at = slice(k * cut, (k + 1) * cut)
        g, c = gain[0:1, at], bias[0:1, at]
        for level in range(1, levels):
            here = depth == float(level)
            g = jnp.where(here, gain[level : level + 1, at], g)
            c = jnp.where(here, bias[level : level + 1, at], c)
        value = (block[:, at].astype(F32) * scale) * g + c
        mapped[first : first + rows, at] = value.astype(BF16)


def map_kernel(places, *refs):
    blocks = refs[: len(places)]
    gain, bias = refs[len(places) : len(places) + 2]
    for place, block in zip(places, blocks):
        map_rows(block, gain, bias, refs[-1], place * block.shape[0])


def map_early(rows, gain, bias, mapped, blocks):
    places, blocks = list(blocks), list(blocks.values())
    width = gain.shape[1]
    operands = blocks + [gain, bias] + ([] if mapped is None else [mapped])
    count = len(blocks) * blocks[0].shape[0]
    return pl.pallas_call(
        functools.partial(map_kernel, places),
        out_shape=pltpu.VMEM((rows, width), BF16),
        in_specs=[VMEM] * len(operands),
        out_specs=VMEM,
        input_output_aliases={} if mapped is None else {len(operands) - 1: 0},
        compiler_params=pltpu.CompilerParams(vmem_limit_bytes=8 << 20),
        cost_estimate=pl.CostEstimate(
            flops=20 * count * width, bytes_accessed=4 * count * width, transcendentals=0
        ),
    )(*operands)


def load_kernel(part, parts, head_hbm, *refs):
    head, sems = refs[-2:]
    count = sems.shape[0]
    size = head.shape[0] // (parts * count)
    copies = []
    for k in range(count):
        at = pl.ds((part * count + k) * size, size)
        copies.append(pltpu.make_async_copy(head_hbm.at[at], head.at[at], sems.at[k]))
    for copy in copies:
        copy.start()
    for copy in copies:
        copy.wait()


def load(tied_head, part, parts, loaded=None):
    operands = [in_hbm(tied_head)] + ([] if loaded is None else [loaded])
    voc, width = tied_head.shape
    return pl.pallas_call(
        functools.partial(load_kernel, part, parts),
        out_shape=pltpu.VMEM(tied_head.shape, BF16),
        in_specs=[HBM] + [VMEM] * (len(operands) - 1),
        out_specs=VMEM,
        input_output_aliases={} if loaded is None else {1: 0},
        scratch_shapes=[pltpu.SemaphoreType.DMA((4,))],
        compiler_params=pltpu.CompilerParams(vmem_limit_bytes=16 << 20),
        cost_estimate=pl.CostEstimate(
            flops=0, bytes_accessed=4 * voc * width // parts, transcendentals=0
        ),
    )(*operands)


def half_sums(blocks, head, slopes, scaled, mass, which, work, out):
    levels = out.shape[0] // 2
    rows = sum(b.shape[0] for b in blocks)
    half = head.shape[1] // 2
    add3 = lambda x: (x[:levels] + x[levels : 2 * levels]) + x[2 * levels : 3 * levels]
    done = 0
    while done < half:
        size = min(256, half - done)
        here = slice(done, done + size)
        at = pl.ds(pl.multiple_of(which * half + done, LANES), size)
        back = jnp.dot(slopes[...], head[:, at], preferred_element_type=F32)
        wide = jnp.concatenate([b[:, at] for b in blocks], axis=0).astype(F32)
        work[:, here] = (back[:rows] * wide).astype(BF16)
        out[levels:, here] = add3(back[rows:])
        done += size
    out[:levels, :half] = add3(jnp.dot(scaled, work[:, :half], preferred_element_type=F32))
    out[:, half:] = jnp.broadcast_to(mass, (2 * levels, mass.shape[1]))


def front_kernel(loop, levels, count, late, *refs):
    blocks = refs[:count]
    head, gain, bias = refs[count : count + 3]
    give, slopes, scaled_out, mass_out, mapped = refs[-5:]
    voc, width = head.shape
    rows = mapped.shape[0]
    rows_dev = rows // loop
    chips = loop // 2
    me = lax.axis_index("loop")
    core = me % 2
    meta = jnp.concatenate([b[:, width:] for b in blocks], axis=0).astype(F32)
    col = lambda i: meta[:, i : i + 1]
    scale = (col(0) + col(1)) + col(2)
    norm = (col(3) + col(4)) + col(5)
    target = (col(6) + 128.0 * col(7) + 16384.0 * col(8)).astype(jnp.int32)
    depth = col(9)

    for i in late:
        map_rows(blocks[i], gain, bias, mapped, i * blocks[i].shape[0])
    logits = lax.dot_general(mapped[...], head[...], NT, preferred_element_type=F32)
    prob = jnp.exp(logits - norm)
    columns = me * voc + lax.broadcasted_iota(jnp.int32, (rows, voc), 1)
    slopes[:rows, :] = jnp.where(columns == target, prob - 1.0, prob).astype(BF16)

    mass = prob[:, :LANES]
    for j in range(1, voc // LANES):
        mass = mass + prob[:, j * LANES : (j + 1) * LANES]
    mass = jnp.sum(mass.T, axis=0, keepdims=True)
    index = lax.broadcasted_iota(jnp.int32, (rows, rows), 0)
    flip = index // (rows // 2)
    relative = (index - flip * (rows // 2)) // rows_dev
    place = place_of(me // 2, chips) + jnp.where(core == 0, relative, chips - relative)
    place = jnp.where(place >= chips, place - chips, place)
    owner = 2 * chip_at(place, chips) + jnp.where(flip == 0, core, 1 - core)
    goes_to = owner * rows_dev + index % rows_dev
    move = goes_to == lax.broadcasted_iota(jnp.int32, (rows, rows), 1)
    move = jnp.where(move, 1.0, 0.0).astype(BF16)
    lines = jnp.concatenate(pieces(mass) + [jnp.zeros((13, rows), F32)], axis=0)
    moved = jnp.dot(lines.astype(BF16), move, preferred_element_type=F32)
    moved = (moved[0:1] + moved[1:2]) + moved[2:3]
    low, high = moved[:, : rows // 2], moved[:, rows // 2 :]
    mass_out[...] = jnp.where(core == 0, low, high)

    lane = lax.broadcasted_iota(jnp.int32, (rows, LANES), 1).astype(F32)
    pick = jnp.where(lane == depth, 1.0, 0.0).T[:levels]
    scaled = pick * jnp.broadcast_to(scale, (rows, LANES)).T[:levels]
    none = jnp.zeros((16 - 3 * levels, rows), F32)
    scaled = jnp.concatenate(pieces(scaled) + [none], axis=0).astype(BF16)
    scaled_out[...] = scaled
    sums = jnp.dot(pick.astype(BF16), slopes[:rows, :], preferred_element_type=F32)
    none = jnp.zeros((16 - 3 * levels, voc), F32)
    slopes[rows:, :] = jnp.concatenate(pieces(sums) + [none], axis=0).astype(BF16)
    other = jnp.where(core == 0, high, low)
    half_sums(blocks, head, slopes, scaled, other, 1 - core, mapped, give)


def back_kernel(count, *refs):
    blocks = refs[:count]
    head, slopes, scaled, mass, keep, work = refs[count:]
    core = lax.axis_index("loop") % 2
    half_sums(blocks, head, slopes, scaled[...], mass[...], core, work, keep)


def main(blocks, head, gain, bias, mapped, late, loop):
    levels = gain.shape[0]
    voc, width = head.shape
    rows = sum(b.shape[0] for b in blocks)
    half = pltpu.VMEM((2 * levels, (width + rows) // 2), F32)
    operands = list(blocks) + [head, gain, bias] + ([] if mapped is None else [mapped])
    cost = lambda passes: pl.CostEstimate(
        flops=passes * rows * voc * width, bytes_accessed=voc * width, transcendentals=0
    )
    give, slopes, scaled, mass, _ = pl.pallas_call(
        functools.partial(front_kernel, loop, levels, len(blocks), late),
        out_shape=(
            half,
            pltpu.VMEM((rows + 16, voc), BF16),
            pltpu.VMEM((16, rows), BF16),
            pltpu.VMEM((1, rows // 2), F32),
            pltpu.VMEM((rows, width), BF16),
        ),
        in_specs=[VMEM] * len(operands),
        out_specs=(VMEM,) * 5,
        input_output_aliases={} if mapped is None else {len(operands) - 1: 4},
        compiler_params=pltpu.CompilerParams(vmem_limit_bytes=16 << 20),
        cost_estimate=cost(3),
    )(*operands)
    operands = list(blocks) + [head, slopes, scaled, mass]
    keep = pl.pallas_call(
        functools.partial(back_kernel, len(blocks)),
        out_shape=half,
        in_specs=[VMEM] * len(operands),
        out_specs=VMEM,
        scratch_shapes=[pltpu.VMEM((rows, width // 2), BF16)],
        compiler_params=pltpu.CompilerParams(vmem_limit_bytes=16 << 20),
        cost_estimate=cost(1),
    )(*operands)
    return keep, give


def sum_over_loop(keep, give, loop):
    send = lambda x, mask: lax.ppermute(x, "loop", [(i, i ^ mask) for i in range(loop)])
    total = keep + send(give, 1)
    bits = [1 << k for k in range(1, loop.bit_length() - 1)]
    for k in range(0, len(bits) - 1, 2):
        dims = bits[:-1][k : k + 2]
        total = lax.reduce_precision(total, 8, 7)
        sent = total.astype(BF16)
        take = lambda mask: send(sent, mask).astype(F32)
        total = total + take(dims[0])
        if len(dims) == 2:
            total = total + (take(dims[1]) + take(dims[0] ^ dims[1]))
    total = lax.reduce_precision(total, 8, 7)
    total = total + send(total.astype(BF16), bits[-1]).astype(F32)
    return total, send(total, 1)


def last_kernel(levels, rows, kept, given, mass_out, gain_out, bias_out, buf, line, sems):
    width = gain_out.shape[1]
    me = lax.axis_index("loop")
    cut = width // 2
    low = jnp.where(me % 2 == 0, kept[...], given[...])
    high = jnp.where(me % 2 == 0, given[...], kept[...])
    buf[:, :cut], buf[:, cut:width] = low[:, :cut], high[:, :cut]
    buf[:, width:] = jnp.concatenate([low[:, cut:], high[:, cut:]], axis=1)
    every = buf[0:1, width:]
    spread = lax.broadcasted_iota(jnp.int32, (every.shape[1], LANES), 0)
    target = lax.broadcasted_iota(jnp.int32, (every.shape[1], LANES), 1)
    move = jnp.where(spread - me * rows == target, 1.0, 0.0).astype(BF16)
    lines = jnp.concatenate(pieces(every) + [jnp.zeros((13, every.shape[1]), F32)], axis=0)
    own = jnp.dot(lines.astype(BF16), move, preferred_element_type=F32)
    line[...] = ((own[0:1] + own[1:2]) + own[2:3])[:, :rows]
    copies = [
        pltpu.make_async_copy(buf.at[pl.ds(0, levels), pl.ds(0, width)], gain_out, sems.at[0]),
        pltpu.make_async_copy(buf.at[pl.ds(levels, levels), pl.ds(0, width)], bias_out, sems.at[1]),
        pltpu.make_async_copy(line, mass_out, sems.at[2]),
    ]
    for copy in copies:
        copy.start()
    for copy in copies:
        copy.wait()


def last(kept, given, levels, width, rows):
    grad = pltpu.HBM((levels, width), F32)
    mass, gain, bias = pl.pallas_call(
        functools.partial(last_kernel, levels, rows),
        out_shape=(pltpu.HBM((1, rows), F32), grad, grad),
        in_specs=[VMEM, VMEM],
        out_specs=(HBM, HBM, HBM),
        scratch_shapes=[
            pltpu.VMEM((kept.shape[0], 2 * kept.shape[1]), F32),
            pltpu.VMEM((1, rows), F32),
            pltpu.SemaphoreType.DMA((3,)),
        ],
        compiler_params=pltpu.CompilerParams(vmem_limit_bytes=8 << 20),
    )(kept, given)
    return mass.reshape(rows), gain, bias


def shards(loop, hidden, exit_depth, teacher, normalizer, tied_head, depth_gain, depth_bias):
    rows_dev, width = hidden.shape
    levels = depth_gain.shape[0]
    block, gain, bias = prep(hidden, exit_depth, teacher, normalizer, depth_gain, depth_bias)
    rows = rows_dev * loop
    early = rows_dev % 16 == 0 and loop == 16
    mapper = functools.partial(map_early, rows, gain, bias) if early else None
    blocks, head, mapped, late = gather_blocks(block, loop, tied_head, mapper)
    if rows_dev % 16:
        whole = jnp.concatenate(blocks, axis=0)
        blocks = [whole[i : i + 16] for i in range(0, rows, 16)]
        late = range(len(blocks))
    keep, give = main(blocks, head, gain, bias, mapped, late, loop)
    return last(*sum_over_loop(keep, give, loop), levels, width, rows_dev)


def solution(mesh):
    loop = mesh.shape["loop"]

    def body(*args):
        return shards(loop, *args)

    return jax.shard_map(
        body,
        mesh=mesh,
        in_specs=(
            P(("groups", "loop"), None),
            P(("groups", "loop")),
            P(("groups", "loop")),
            P(("groups", "loop")),
            P("loop", None),
            P(),
            P(),
        ),
        out_specs=(P(("groups", "loop")), P("groups", None), P("groups", None)),
        check_vma=False,
    )
```

```python
import functools

import jax
import jax.numpy as jnp
from jax import lax
from jax.experimental import pallas as pl
from jax.experimental.pallas import tpu as pltpu
from jax.sharding import PartitionSpec as P

BF16 = jnp.bfloat16
F32 = jnp.float32
LANES = 128
NT = (((1,), (1,)), ((), ()))
VMEM = pl.BlockSpec(memory_space=pltpu.VMEM)
HBM = pl.BlockSpec(memory_space=pl.ANY)


def in_hbm(x):
    return pltpu.with_memory_space_constraint(x, pltpu.HBM)


def ring_of(chips):
    return list(range(0, chips, 2)) + list(range(chips - 1, 0, -2))


def chip_at(place, chips):
    return jnp.where(place < chips // 2, 2 * place, 2 * (chips - 1 - place) + 1)


def place_of(chip, chips):
    return jnp.where(chip % 2 == 0, chip // 2, chips - 1 - chip // 2)


def pieces(value):
    top = value.astype(BF16).astype(F32)
    rest = value - top
    middle = rest.astype(BF16).astype(F32)
    return [top, middle, rest - middle]


def prep_kernel(
    hidden, exit_depth, teacher, normalizer, depth_gain, depth_bias,
    out, gain_out, bias_out, row_buf, int_buf, float_buf, sems,
):
    rows, width = hidden.shape
    copies = [
        pltpu.make_async_copy(hidden, row_buf, sems.at[0]),
        pltpu.make_async_copy(exit_depth, int_buf.at[0], sems.at[1]),
        pltpu.make_async_copy(teacher, int_buf.at[1], sems.at[2]),
        pltpu.make_async_copy(normalizer, float_buf, sems.at[3]),
        pltpu.make_async_copy(depth_gain, gain_out, sems.at[4]),
        pltpu.make_async_copy(depth_bias, bias_out, sems.at[5]),
    ]
    for copy in copies:
        copy.start()
    for copy in copies[:4]:
        copy.wait()
    block = row_buf[...]
    out[:, :width] = block
    wide = block.astype(F32)
    mean = jnp.sum(wide * wide, axis=1, keepdims=True) * (1.0 / width)
    scale = lax.rsqrt(mean + 1e-06)
    down = lax.broadcasted_iota(jnp.int32, (rows, rows), 0)
    across = lax.broadcasted_iota(jnp.int32, (rows, rows), 1)

    def column(line):
        square = jnp.broadcast_to(line, (rows, rows))
        return jnp.sum(jnp.where(down == across, square, 0.0), axis=1, keepdims=True)

    token = int_buf[1]
    columns = pieces(scale) + pieces(column(float_buf[...]))
    for digit in (token & 127, (token >> 7) & 127, token >> 14):
        columns.append(column(digit.astype(F32)))
    columns.append(column(int_buf[0].astype(F32)))
    lane = lax.broadcasted_iota(jnp.int32, (rows, LANES), 1)
    meta = jnp.zeros((rows, LANES), F32)
    for i, value in enumerate(columns):
        meta = jnp.where(lane == i, value, meta)
    out[:, width:] = meta.astype(BF16)
    for copy in copies[4:]:
        copy.wait()


def prep(hidden, exit_depth, teacher, normalizer, depth_gain, depth_bias):
    rows, width = hidden.shape
    return pl.pallas_call(
        prep_kernel,
        out_shape=(
            pltpu.VMEM((rows, width + LANES), BF16),
            pltpu.VMEM(depth_gain.shape, F32),
            pltpu.VMEM(depth_bias.shape, F32),
        ),
        in_specs=[HBM] * 6,
        out_specs=(VMEM, VMEM, VMEM),
        scratch_shapes=[
            pltpu.VMEM((rows, width), BF16),
            pltpu.VMEM((2, 1, rows), jnp.int32),
            pltpu.VMEM((1, rows), F32),
            pltpu.SemaphoreType.DMA((6,)),
        ],
        compiler_params=pltpu.CompilerParams(vmem_limit_bytes=8 << 20),
    )(
        in_hbm(hidden),
        in_hbm(exit_depth.reshape(1, rows)),
        in_hbm(teacher.reshape(1, rows)),
        in_hbm(normalizer.reshape(1, rows)),
        in_hbm(depth_gain),
        in_hbm(depth_bias),
    )


def hop_pairs(order, step, cross):
    chips = len(order)
    first = 1 - step % 2
    pairs = []
    for i in range(chips):
        here, after = 2 * order[i], 2 * order[(i + 1) % chips]
        if cross:
            pairs += [(here + first, after + 1 - first), (after + 1 - first, here + first)]
        else:
            pairs += [(here + 1 - first, after + 1 - first), (after + first, here + first)]
    return pairs


def gather_blocks(block, loop, tied_head, mapper):
    chips = loop // 2
    order = ring_of(chips)
    half = chips // 2
    tie = lambda *xs: lax.optimization_barrier(xs)
    send = lambda x, pairs: lax.ppermute(x, "loop", pairs)
    swap = lambda x: send(x, [(i, i ^ 1) for i in range(loop)])
    blocks = [None] * loop
    blocks[0], blocks[chips] = block, swap(block)
    crossed = plain = block
    ready = [0, chips]
    mapped = None
    for step in range(1, half + 1):
        crossed = send(crossed, hop_pairs(order, step, True))
        if step < half:
            plain = send(plain, hop_pairs(order, step, step > 1))
        if step == 1:
            head = load(tied_head)
            crossed, head = tie(crossed, head)
        if mapper is not None and step == 3:
            mapped = mapper(None, {i: blocks[i] for i in ready[:6]})
            plain, mapped = tie(plain, mapped)
        if mapper is not None and step == half:
            mapped = mapper(mapped, {i: blocks[i] for i in ready[6:12]})
            crossed, mapped = tie(crossed, mapped)
        far = step if step % 2 else chips - step
        near = chips - far
        mine, theirs = (chips, 0) if step % 2 else (0, chips)
        blocks[mine + far] = crossed
        if step < half:
            blocks[theirs + far] = plain
            blocks[theirs + near] = swap(crossed)
            blocks[mine + near] = swap(plain)
            ready += [mine + far, theirs + far, theirs + near, mine + near]
        else:
            blocks[theirs + far] = swap(crossed)
            ready += [mine + far, theirs + far]
    return blocks, head, mapped, ready[12:] if mapper is not None else ready


def map_rows(block, gain, bias, mapped, first):
    rows, width = block.shape[0], mapped.shape[1]
    levels = gain.shape[0]
    meta = block[:, width:].astype(F32)
    scale = (meta[:, 0:1] + meta[:, 1:2]) + meta[:, 2:3]
    depth = meta[:, 9:10]
    cuts = 3 if width % (3 * LANES) == 0 else 1
    cut = width // cuts
    for k in range(cuts):
        at = slice(k * cut, (k + 1) * cut)
        g, c = gain[0:1, at], bias[0:1, at]
        for level in range(1, levels):
            here = depth == float(level)
            g = jnp.where(here, gain[level : level + 1, at], g)
            c = jnp.where(here, bias[level : level + 1, at], c)
        value = (block[:, at].astype(F32) * scale) * g + c
        mapped[first : first + rows, at] = value.astype(BF16)


def map_kernel(places, *refs):
    blocks = refs[: len(places)]
    gain, bias = refs[len(places) : len(places) + 2]
    for place, block in zip(places, blocks):
        map_rows(block, gain, bias, refs[-1], place * block.shape[0])


def map_early(rows, gain, bias, mapped, blocks):
    places, blocks = list(blocks), list(blocks.values())
    width = gain.shape[1]
    operands = blocks + [gain, bias] + ([] if mapped is None else [mapped])
    count = len(blocks) * blocks[0].shape[0]
    return pl.pallas_call(
        functools.partial(map_kernel, places),
        out_shape=pltpu.VMEM((rows, width), BF16),
        in_specs=[VMEM] * len(operands),
        out_specs=VMEM,
        input_output_aliases={} if mapped is None else {len(operands) - 1: 0},
        compiler_params=pltpu.CompilerParams(vmem_limit_bytes=8 << 20),
        cost_estimate=pl.CostEstimate(
            flops=20 * count * width, bytes_accessed=4 * count * width, transcendentals=0
        ),
    )(*operands)


def load_kernel(head_hbm, head, sems):
    count = sems.shape[0]
    size = head.shape[0] // count
    copies = []
    for k in range(count):
        at = pl.ds(k * size, size)
        copies.append(pltpu.make_async_copy(head_hbm.at[at], head.at[at], sems.at[k]))
    for copy in copies:
        copy.start()
    for copy in copies:
        copy.wait()


def load(tied_head):
    voc, width = tied_head.shape
    return pl.pallas_call(
        load_kernel,
        out_shape=pltpu.VMEM(tied_head.shape, BF16),
        in_specs=[HBM],
        out_specs=VMEM,
        scratch_shapes=[pltpu.SemaphoreType.DMA((4,))],
        compiler_params=pltpu.CompilerParams(vmem_limit_bytes=16 << 20),
        cost_estimate=pl.CostEstimate(
            flops=0, bytes_accessed=4 * voc * width, transcendentals=0
        ),
    )(in_hbm(tied_head))


def half_sums(blocks, head, slopes, scaled, mass, which, work, out):
    levels = out.shape[0] // 2
    rows = sum(b.shape[0] for b in blocks)
    half = head.shape[1] // 2
    add3 = lambda x: (x[:levels] + x[levels : 2 * levels]) + x[2 * levels : 3 * levels]
    done = 0
    while done < half:
        size = min(256, half - done)
        here = slice(done, done + size)
        at = pl.ds(pl.multiple_of(which * half + done, LANES), size)
        back = jnp.dot(slopes[...], head[:, at], preferred_element_type=F32)
        wide = jnp.concatenate([b[:, at] for b in blocks], axis=0).astype(F32)
        work[:, here] = (back[:rows] * wide).astype(BF16)
        out[levels:, here] = add3(back[rows:])
        done += size
    out[:levels, :half] = add3(jnp.dot(scaled, work[:, :half], preferred_element_type=F32))
    out[:, half:] = jnp.broadcast_to(mass, (2 * levels, mass.shape[1]))


def front_kernel(loop, levels, count, late, *refs):
    blocks = refs[:count]
    head, gain, bias = refs[count : count + 3]
    give, slopes, scaled_out, mass_out, mapped = refs[-5:]
    voc, width = head.shape
    rows = mapped.shape[0]
    rows_dev = rows // loop
    chips = loop // 2
    me = lax.axis_index("loop")
    core = me % 2
    meta = jnp.concatenate([b[:, width:] for b in blocks], axis=0).astype(F32)
    col = lambda i: meta[:, i : i + 1]
    scale = (col(0) + col(1)) + col(2)
    norm = (col(3) + col(4)) + col(5)
    target = (col(6) + 128.0 * col(7) + 16384.0 * col(8)).astype(jnp.int32)
    depth = col(9)

    for i in late:
        map_rows(blocks[i], gain, bias, mapped, i * blocks[i].shape[0])
    logits = lax.dot_general(mapped[...], head[...], NT, preferred_element_type=F32)
    prob = jnp.exp(logits - norm)
    columns = me * voc + lax.broadcasted_iota(jnp.int32, (rows, voc), 1)
    slopes[:rows, :] = jnp.where(columns == target, prob - 1.0, prob).astype(BF16)

    mass = prob[:, :LANES]
    for j in range(1, voc // LANES):
        mass = mass + prob[:, j * LANES : (j + 1) * LANES]
    mass = jnp.sum(mass.T, axis=0, keepdims=True)
    index = lax.broadcasted_iota(jnp.int32, (rows, rows), 0)
    flip = index // (rows // 2)
    relative = (index - flip * (rows // 2)) // rows_dev
    place = place_of(me // 2, chips) + jnp.where(core == 0, relative, chips - relative)
    place = jnp.where(place >= chips, place - chips, place)
    owner = 2 * chip_at(place, chips) + jnp.where(flip == 0, core, 1 - core)
    goes_to = owner * rows_dev + index % rows_dev
    move = goes_to == lax.broadcasted_iota(jnp.int32, (rows, rows), 1)
    move = jnp.where(move, 1.0, 0.0).astype(BF16)
    lines = jnp.concatenate(pieces(mass) + [jnp.zeros((13, rows), F32)], axis=0)
    moved = jnp.dot(lines.astype(BF16), move, preferred_element_type=F32)
    moved = (moved[0:1] + moved[1:2]) + moved[2:3]
    low, high = moved[:, : rows // 2], moved[:, rows // 2 :]
    mass_out[...] = jnp.where(core == 0, low, high)

    lane = lax.broadcasted_iota(jnp.int32, (rows, LANES), 1).astype(F32)
    pick = jnp.where(lane == depth, 1.0, 0.0).T[:levels]
    scaled = pick * jnp.broadcast_to(scale, (rows, LANES)).T[:levels]
    none = jnp.zeros((16 - 3 * levels, rows), F32)
    scaled = jnp.concatenate(pieces(scaled) + [none], axis=0).astype(BF16)
    scaled_out[...] = scaled
    sums = jnp.dot(pick.astype(BF16), slopes[:rows, :], preferred_element_type=F32)
    none = jnp.zeros((16 - 3 * levels, voc), F32)
    slopes[rows:, :] = jnp.concatenate(pieces(sums) + [none], axis=0).astype(BF16)
    other = jnp.where(core == 0, high, low)
    half_sums(blocks, head, slopes, scaled, other, 1 - core, mapped, give)


def back_kernel(count, *refs):
    blocks = refs[:count]
    head, slopes, scaled, mass, keep, work = refs[count:]
    core = lax.axis_index("loop") % 2
    half_sums(blocks, head, slopes, scaled[...], mass[...], core, work, keep)


def main(blocks, head, gain, bias, mapped, late, loop):
    levels = gain.shape[0]
    voc, width = head.shape
    rows = sum(b.shape[0] for b in blocks)
    half = pltpu.VMEM((2 * levels, (width + rows) // 2), F32)
    operands = list(blocks) + [head, gain, bias] + ([] if mapped is None else [mapped])
    cost = lambda passes: pl.CostEstimate(
        flops=passes * rows * voc * width, bytes_accessed=voc * width, transcendentals=0
    )
    give, slopes, scaled, mass, _ = pl.pallas_call(
        functools.partial(front_kernel, loop, levels, len(blocks), late),
        out_shape=(
            half,
            pltpu.VMEM((rows + 16, voc), BF16),
            pltpu.VMEM((16, rows), BF16),
            pltpu.VMEM((1, rows // 2), F32),
            pltpu.VMEM((rows, width), BF16),
        ),
        in_specs=[VMEM] * len(operands),
        out_specs=(VMEM,) * 5,
        input_output_aliases={} if mapped is None else {len(operands) - 1: 4},
        compiler_params=pltpu.CompilerParams(vmem_limit_bytes=16 << 20),
        cost_estimate=cost(3),
    )(*operands)
    operands = list(blocks) + [head, slopes, scaled, mass]
    keep = pl.pallas_call(
        functools.partial(back_kernel, len(blocks)),
        out_shape=half,
        in_specs=[VMEM] * len(operands),
        out_specs=VMEM,
        scratch_shapes=[pltpu.VMEM((rows, width // 2), BF16)],
        compiler_params=pltpu.CompilerParams(vmem_limit_bytes=16 << 20),
        cost_estimate=cost(1),
    )(*operands)
    return keep, give


def sum_over_loop(keep, give, loop):
    send = lambda x, mask: lax.ppermute(x, "loop", [(i, i ^ mask) for i in range(loop)])
    total = keep + send(give, 1)
    bits = [1 << k for k in range(1, loop.bit_length() - 1)]
    for k in range(0, len(bits) - 1, 2):
        dims = bits[:-1][k : k + 2]
        total = lax.reduce_precision(total, 8, 7)
        sent = total.astype(BF16)
        take = lambda mask: send(sent, mask).astype(F32)
        total = total + take(dims[0])
        if len(dims) == 2:
            total = total + (take(dims[1]) + take(dims[0] ^ dims[1]))
    total = lax.reduce_precision(total, 8, 7)
    total = total + send(total.astype(BF16), bits[-1]).astype(F32)
    return total, send(total, 1)


def last_kernel(levels, rows, kept, given, mass_out, gain_out, bias_out, buf, line, sems):
    width = gain_out.shape[1]
    me = lax.axis_index("loop")
    cut = width // 2
    low = jnp.where(me % 2 == 0, kept[...], given[...])
    high = jnp.where(me % 2 == 0, given[...], kept[...])
    buf[:, :cut], buf[:, cut:width] = low[:, :cut], high[:, :cut]
    buf[:, width:] = jnp.concatenate([low[:, cut:], high[:, cut:]], axis=1)
    every = buf[0:1, width:]
    spread = lax.broadcasted_iota(jnp.int32, (every.shape[1], LANES), 0)
    target = lax.broadcasted_iota(jnp.int32, (every.shape[1], LANES), 1)
    move = jnp.where(spread - me * rows == target, 1.0, 0.0).astype(BF16)
    lines = jnp.concatenate(pieces(every) + [jnp.zeros((13, every.shape[1]), F32)], axis=0)
    own = jnp.dot(lines.astype(BF16), move, preferred_element_type=F32)
    line[...] = ((own[0:1] + own[1:2]) + own[2:3])[:, :rows]
    copies = [
        pltpu.make_async_copy(buf.at[pl.ds(0, levels), pl.ds(0, width)], gain_out, sems.at[0]),
        pltpu.make_async_copy(buf.at[pl.ds(levels, levels), pl.ds(0, width)], bias_out, sems.at[1]),
        pltpu.make_async_copy(line, mass_out, sems.at[2]),
    ]
    for copy in copies:
        copy.start()
    for copy in copies:
        copy.wait()


def last(kept, given, levels, width, rows):
    grad = pltpu.HBM((levels, width), F32)
    mass, gain, bias = pl.pallas_call(
        functools.partial(last_kernel, levels, rows),
        out_shape=(pltpu.HBM((1, rows), F32), grad, grad),
        in_specs=[VMEM, VMEM],
        out_specs=(HBM, HBM, HBM),
        scratch_shapes=[
            pltpu.VMEM((kept.shape[0], 2 * kept.shape[1]), F32),
            pltpu.VMEM((1, rows), F32),
            pltpu.SemaphoreType.DMA((3,)),
        ],
        compiler_params=pltpu.CompilerParams(vmem_limit_bytes=8 << 20),
    )(kept, given)
    return mass.reshape(rows), gain, bias


def shards(loop, hidden, exit_depth, teacher, normalizer, tied_head, depth_gain, depth_bias):
    rows_dev, width = hidden.shape
    levels = depth_gain.shape[0]
    block, gain, bias = prep(hidden, exit_depth, teacher, normalizer, depth_gain, depth_bias)
    rows = rows_dev * loop
    early = rows_dev % 16 == 0 and loop == 16
    mapper = functools.partial(map_early, rows, gain, bias) if early else None
    blocks, head, mapped, late = gather_blocks(block, loop, tied_head, mapper)
    if rows_dev % 16:
        whole = jnp.concatenate(blocks, axis=0)
        blocks = [whole[i : i + 16] for i in range(0, rows, 16)]
        late = range(len(blocks))
    keep, give = main(blocks, head, gain, bias, mapped, late, loop)
    return last(*sum_over_loop(keep, give, loop), levels, width, rows_dev)


def solution(mesh):
    loop = mesh.shape["loop"]

    def body(*args):
        return shards(loop, *args)

    return jax.shard_map(
        body,
        mesh=mesh,
        in_specs=(
            P(("groups", "loop"), None),
            P(("groups", "loop")),
            P(("groups", "loop")),
            P(("groups", "loop")),
            P("loop", None),
            P(),
            P(),
        ),
        out_specs=(P(("groups", "loop")), P("groups", None), P("groups", None)),
        check_vma=False,
    )
```

```python
import functools

import jax
import jax.numpy as jnp
from jax import lax
from jax.experimental import pallas as pl
from jax.experimental.pallas import tpu as pltpu
from jax.sharding import PartitionSpec as P

BF16 = jnp.bfloat16
F32 = jnp.float32
LANES = 128
CUTS = 42
TOGETHER = 2
NT = (((1,), (1,)), ((), ()))
VMEM = pl.BlockSpec(memory_space=pltpu.VMEM)
HBM = pl.BlockSpec(memory_space=pl.ANY)


def in_hbm(x):
    return pltpu.with_memory_space_constraint(x, pltpu.HBM)


def ring_of(chips):
    return list(range(0, chips, 2)) + list(range(chips - 1, 0, -2))


def chip_at(place, chips):
    return jnp.where(place < chips // 2, 2 * place, 2 * (chips - 1 - place) + 1)


def place_of(chip, chips):
    return jnp.where(chip % 2 == 0, chip // 2, chips - 1 - chip // 2)


def pieces(value):
    top = value.astype(BF16).astype(F32)
    rest = value - top
    middle = rest.astype(BF16).astype(F32)
    return [top, middle, rest - middle]


def prep_kernel(
    hidden, exit_depth, teacher, normalizer, depth_gain, depth_bias,
    out, gain_out, bias_out, int_buf, float_buf, sems,
):
    rows, width = hidden.shape
    copies = [
        pltpu.make_async_copy(hidden, out.at[:, pl.ds(0, hidden.shape[1])], sems.at[0]),
        pltpu.make_async_copy(exit_depth, int_buf.at[0], sems.at[1]),
        pltpu.make_async_copy(teacher, int_buf.at[1], sems.at[2]),
        pltpu.make_async_copy(normalizer, float_buf, sems.at[3]),
        pltpu.make_async_copy(depth_gain, gain_out, sems.at[4]),
        pltpu.make_async_copy(depth_bias, bias_out, sems.at[5]),
    ]
    for copy in copies:
        copy.start()
    for copy in copies[1:4]:
        copy.wait()
    down = lax.broadcasted_iota(jnp.int32, (rows, rows), 0)
    across = lax.broadcasted_iota(jnp.int32, (rows, rows), 1)

    def column(line):
        square = jnp.broadcast_to(line, (rows, rows))
        return jnp.sum(jnp.where(down == across, square, 0.0), axis=1, keepdims=True)

    token = int_buf[1]
    columns = pieces(column(float_buf[...]))
    for digit in (token & 127, (token >> 7) & 127, token >> 14):
        columns.append(column(digit.astype(F32)))
    columns.append(column(int_buf[0].astype(F32)))
    copies[0].wait()
    wide = out[:, :width].astype(F32)
    mean = jnp.sum(wide * wide, axis=1, keepdims=True) * (1.0 / width)
    columns = pieces(lax.rsqrt(mean + 1e-06)) + columns
    lane = lax.broadcasted_iota(jnp.int32, (rows, LANES), 1)
    meta = jnp.zeros((rows, LANES), F32)
    for i, value in enumerate(columns):
        meta = jnp.where(lane == i, value, meta)
    out[:, width:] = meta.astype(BF16)
    for copy in copies[4:]:
        copy.wait()


def prep(hidden, exit_depth, teacher, normalizer, depth_gain, depth_bias):
    rows, width = hidden.shape
    return pl.pallas_call(
        prep_kernel,
        out_shape=(
            pltpu.VMEM((rows, width + LANES), BF16),
            pltpu.VMEM(depth_gain.shape, F32),
            pltpu.VMEM(depth_bias.shape, F32),
        ),
        in_specs=[HBM] * 6,
        out_specs=(VMEM, VMEM, VMEM),
        scratch_shapes=[
            pltpu.VMEM((2, 1, rows), jnp.int32),
            pltpu.VMEM((1, rows), F32),
            pltpu.SemaphoreType.DMA((6,)),
        ],
        compiler_params=pltpu.CompilerParams(vmem_limit_bytes=8 << 20),
    )(
        in_hbm(hidden),
        in_hbm(exit_depth.reshape(1, rows)),
        in_hbm(teacher.reshape(1, rows)),
        in_hbm(normalizer.reshape(1, rows)),
        in_hbm(depth_gain),
        in_hbm(depth_bias),
    )


def hop_pairs(order, step, cross):
    chips = len(order)
    first = 1 - step % 2
    pairs = []
    for i in range(chips):
        here, after = 2 * order[i], 2 * order[(i + 1) % chips]
        if cross:
            pairs += [(here + first, after + 1 - first), (after + 1 - first, here + first)]
        else:
            pairs += [(here + 1 - first, after + 1 - first), (after + first, here + first)]
    return pairs


def gather_blocks(block, loop, tied_head, mapper):
    chips = loop // 2
    order = ring_of(chips)
    half = chips // 2
    tie = lambda *xs: lax.optimization_barrier(xs)
    send = lambda x, pairs: lax.ppermute(x, "loop", pairs)
    swap = lambda x: send(x, [(i, i ^ 1) for i in range(loop)])
    blocks = [None] * loop
    blocks[0], blocks[chips] = block, swap(block)
    crossed = plain = block
    ready = [0, chips]
    mapped = None
    for step in range(1, half + 1):
        crossed = send(crossed, hop_pairs(order, step, True))
        if step < half:
            plain = send(plain, hop_pairs(order, step, step > 1))
        if step == 1:
            head = load(tied_head)
            crossed, head = tie(crossed, head)
        if mapper is not None and step == 3:
            mapped = mapper(None, {i: blocks[i] for i in ready[:6]})
            plain, mapped = tie(plain, mapped)
        if mapper is not None and step == half:
            mapped = mapper(mapped, {i: blocks[i] for i in ready[6:12]})
            crossed, mapped = tie(crossed, mapped)
        far = step if step % 2 else chips - step
        near = chips - far
        mine, theirs = (chips, 0) if step % 2 else (0, chips)
        blocks[mine + far] = crossed
        if step < half:
            blocks[theirs + far] = plain
            blocks[theirs + near] = swap(crossed)
            blocks[mine + near] = swap(plain)
            ready += [mine + far, theirs + far, theirs + near, mine + near]
        else:
            blocks[theirs + far] = swap(crossed)
            ready += [mine + far, theirs + far]
            if mapper is not None:
                mapped = mapper(mapped, {i: blocks[i] for i in ready[12:15]})
    return blocks, head, mapped, ready[15:] if mapper is not None else ready


def map_rows(blocks, places, gain, bias, mapped):
    size, width = blocks[0].shape[0], mapped.shape[1]
    levels = gain.shape[0]
    cut = width // CUTS if width % (CUTS * LANES) == 0 else LANES
    for first in range(0, len(blocks), TOGETHER):
        some = blocks[first : first + TOGETHER]
        meta = jnp.concatenate([b[:, width:] for b in some], axis=0).astype(F32)
        scale = (meta[:, 0:1] + meta[:, 1:2]) + meta[:, 2:3]
        depth = meta[:, 9:10]
        for start in range(0, width, cut):
            at = slice(start, start + cut)
            g, c = gain[0:1, at], bias[0:1, at]
            for level in range(1, levels):
                here = depth == float(level)
                g = jnp.where(here, gain[level : level + 1, at], g)
                c = jnp.where(here, bias[level : level + 1, at], c)
            wide = jnp.concatenate([b[:, at] for b in some], axis=0).astype(F32)
            value = ((wide * scale) * g + c).astype(BF16)
            for i, place in enumerate(places[first : first + TOGETHER]):
                mapped[place * size : (place + 1) * size, at] = value[i * size : (i + 1) * size]


def map_kernel(places, *refs):
    blocks = refs[: len(places)]
    gain, bias = refs[len(places) : len(places) + 2]
    map_rows(blocks, places, gain, bias, refs[-1])


def map_early(rows, gain, bias, mapped, blocks):
    places, blocks = list(blocks), list(blocks.values())
    width = gain.shape[1]
    operands = blocks + [gain, bias] + ([] if mapped is None else [mapped])
    count = len(blocks) * blocks[0].shape[0]
    return pl.pallas_call(
        functools.partial(map_kernel, places),
        out_shape=pltpu.VMEM((rows, width), BF16),
        in_specs=[VMEM] * len(operands),
        out_specs=VMEM,
        input_output_aliases={} if mapped is None else {len(operands) - 1: 0},
        compiler_params=pltpu.CompilerParams(vmem_limit_bytes=8 << 20),
        cost_estimate=pl.CostEstimate(
            flops=20 * count * width, bytes_accessed=4 * count * width, transcendentals=0
        ),
    )(*operands)


def load_kernel(head_hbm, head, sems):
    count = sems.shape[0]
    size = head.shape[0] // count
    copies = []
    for k in range(count):
        at = pl.ds(k * size, size)
        copies.append(pltpu.make_async_copy(head_hbm.at[at], head.at[at], sems.at[k]))
    for copy in copies:
        copy.start()
    for copy in copies:
        copy.wait()


def load(tied_head):
    voc, width = tied_head.shape
    return pl.pallas_call(
        load_kernel,
        out_shape=pltpu.VMEM(tied_head.shape, BF16),
        in_specs=[HBM],
        out_specs=VMEM,
        scratch_shapes=[pltpu.SemaphoreType.DMA((4,))],
        compiler_params=pltpu.CompilerParams(vmem_limit_bytes=16 << 20),
        cost_estimate=pl.CostEstimate(
            flops=0, bytes_accessed=4 * voc * width, transcendentals=0
        ),
    )(in_hbm(tied_head))


def half_sums(blocks, head, slopes, scaled, which, work, out):
    levels = out.shape[0] // 2
    rows = sum(b.shape[0] for b in blocks)
    half = head.shape[1] // 2
    add3 = lambda x: (x[:levels] + x[levels : 2 * levels]) + x[2 * levels : 3 * levels]
    done = 0
    while done < half:
        size = min(256, half - done)
        here = slice(done, done + size)
        at = pl.ds(pl.multiple_of(which * half + done, LANES), size)
        back = jnp.dot(slopes[...], head[:, at], preferred_element_type=F32)
        wide = jnp.concatenate([b[:, at] for b in blocks], axis=0).astype(F32)
        work[:, here] = (back[:rows] * wide).astype(BF16)
        out[levels:, here] = add3(back[rows:])
        done += size
    out[:levels, :half] = add3(jnp.dot(scaled, work[:, :half], preferred_element_type=F32))


def front_kernel(levels, count, late, *refs):
    blocks = refs[:count]
    head, gain, bias = refs[count : count + 3]
    give, slopes, scaled_out, mass_out, mapped = refs[-5:]
    voc, width = head.shape
    rows = mapped.shape[0]
    me = lax.axis_index("loop")
    core = me % 2
    meta = jnp.concatenate([b[:, width:] for b in blocks], axis=0).astype(F32)
    col = lambda i: meta[:, i : i + 1]
    scale = (col(0) + col(1)) + col(2)
    norm = (col(3) + col(4)) + col(5)
    target = (col(6) + 128.0 * col(7) + 16384.0 * col(8)).astype(jnp.int32)
    depth = col(9)

    map_rows([blocks[i] for i in late], late, gain, bias, mapped)
    logits = lax.dot_general(mapped[...], head[...], NT, preferred_element_type=F32)
    prob = jnp.exp(logits - norm)
    columns = me * voc + lax.broadcasted_iota(jnp.int32, (rows, voc), 1)
    slopes[:rows, :] = jnp.where(columns == target, prob - 1.0, prob).astype(BF16)

    mass = prob[:, :LANES]
    for j in range(1, voc // LANES):
        mass = mass + prob[:, j * LANES : (j + 1) * LANES]
    mass_out[...] = mass

    lane = lax.broadcasted_iota(jnp.int32, (rows, LANES), 1).astype(F32)
    pick = jnp.where(lane == depth, 1.0, 0.0).T[:levels]
    scaled = pick * jnp.broadcast_to(scale, (rows, LANES)).T[:levels]
    none = jnp.zeros((16 - 3 * levels, rows), F32)
    scaled = jnp.concatenate(pieces(scaled) + [none], axis=0).astype(BF16)
    scaled_out[...] = scaled
    sums = jnp.dot(pick.astype(BF16), slopes[:rows, :], preferred_element_type=F32)
    none = jnp.zeros((16 - 3 * levels, voc), F32)
    slopes[rows:, :] = jnp.concatenate(pieces(sums) + [none], axis=0).astype(BF16)
    half_sums(blocks, head, slopes, scaled, 1 - core, mapped, give)
    give[:, width // 2 :] = jnp.zeros((2 * levels, rows), F32)


def back_kernel(loop, count, *refs):
    blocks = refs[:count]
    head, slopes, scaled, mass, keep, work = refs[count:]
    rows, half = work.shape
    rows_dev = rows // loop
    chips = loop // 2
    me = lax.axis_index("loop")
    core = me % 2
    half_sums(blocks, head, slopes, scaled[...], core, work, keep)

    index = lax.broadcasted_iota(jnp.int32, (rows, LANES), 0)
    flip = index // (rows // 2)
    relative = (index - flip * (rows // 2)) // rows_dev
    place = place_of(me // 2, chips) + jnp.where(core == 0, relative, chips - relative)
    place = jnp.where(place >= chips, place - chips, place)
    owner = 2 * chip_at(place, chips) + jnp.where(flip == 0, core, 1 - core)
    goes_to = owner * rows_dev + index % rows_dev
    lane = lax.broadcasted_iota(jnp.int32, (rows, LANES), 1)
    move = [jnp.where(goes_to == lane + k, 1.0, 0.0) for k in range(0, rows, LANES)]
    move = jnp.concatenate(move, axis=1).astype(BF16)
    line = jnp.sum(mass[...].T, axis=0, keepdims=True)
    lines = jnp.concatenate(pieces(line) + [jnp.zeros((13, rows), F32)], axis=0)
    moved = jnp.dot(lines.astype(BF16), move, preferred_element_type=F32)
    moved = (moved[0:1] + moved[1:2]) + moved[2:3]
    keep[:, half:] = jnp.broadcast_to(moved, (keep.shape[0], rows))


def main(blocks, head, gain, bias, mapped, late, loop):
    levels = gain.shape[0]
    voc, width = head.shape
    rows = sum(b.shape[0] for b in blocks)
    half = pltpu.VMEM((2 * levels, width // 2 + rows), F32)
    operands = list(blocks) + [head, gain, bias] + ([] if mapped is None else [mapped])
    cost = lambda passes: pl.CostEstimate(
        flops=passes * rows * voc * width, bytes_accessed=voc * width, transcendentals=0
    )
    give, slopes, scaled, mass, _ = pl.pallas_call(
        functools.partial(front_kernel, levels, len(blocks), late),
        out_shape=(
            half,
            pltpu.VMEM((rows + 16, voc), BF16),
            pltpu.VMEM((16, rows), BF16),
            pltpu.VMEM((rows, LANES), F32),
            pltpu.VMEM((rows, width), BF16),
        ),
        in_specs=[VMEM] * len(operands),
        out_specs=(VMEM,) * 5,
        input_output_aliases={} if mapped is None else {len(operands) - 1: 4},
        compiler_params=pltpu.CompilerParams(vmem_limit_bytes=16 << 20),
        cost_estimate=cost(3),
    )(*operands)
    operands = list(blocks) + [head, slopes, scaled, mass]
    keep = pl.pallas_call(
        functools.partial(back_kernel, loop, len(blocks)),
        out_shape=half,
        in_specs=[VMEM] * len(operands),
        out_specs=VMEM,
        scratch_shapes=[pltpu.VMEM((rows, width // 2), BF16)],
        compiler_params=pltpu.CompilerParams(vmem_limit_bytes=16 << 20),
        cost_estimate=cost(1),
    )(*operands)
    return keep, give


def sum_over_loop(keep, give, loop):
    send = lambda x, mask: lax.ppermute(x, "loop", [(i, i ^ mask) for i in range(loop)])
    total = keep + send(give, 1)
    bits = [1 << k for k in range(1, loop.bit_length() - 1)]
    for k in range(0, len(bits) - 1, 2):
        dims = bits[:-1][k : k + 2]
        total = lax.reduce_precision(total, 8, 7)
        sent = total.astype(BF16)
        take = lambda mask: send(sent, mask).astype(F32)
        total = total + take(dims[0])
        if len(dims) == 2:
            total = total + (take(dims[1]) + take(dims[0] ^ dims[1]))
    total = lax.reduce_precision(total, 8, 7)
    total = total + send(total.astype(BF16), bits[-1]).astype(F32)
    return total, send(total, 1)


def last_kernel(levels, rows, kept, given, mass_out, gain_out, bias_out, buf, line, sems):
    width = gain_out.shape[1]
    me = lax.axis_index("loop")
    cut = width // 2
    low = jnp.where(me % 2 == 0, kept[...], given[...])
    high = jnp.where(me % 2 == 0, given[...], kept[...])
    buf[:, :cut], buf[:, cut:width] = low[:, :cut], high[:, :cut]
    every = kept[0:1, cut:] + given[0:1, cut:]
    spread = lax.broadcasted_iota(jnp.int32, (every.shape[1], LANES), 0)
    target = lax.broadcasted_iota(jnp.int32, (every.shape[1], LANES), 1)
    move = jnp.where(spread - me * rows == target, 1.0, 0.0).astype(BF16)
    lines = jnp.concatenate(pieces(every) + [jnp.zeros((13, every.shape[1]), F32)], axis=0)
    own = jnp.dot(lines.astype(BF16), move, preferred_element_type=F32)
    line[...] = ((own[0:1] + own[1:2]) + own[2:3])[:, :rows]
    copies = [
        pltpu.make_async_copy(buf.at[pl.ds(0, levels)], gain_out, sems.at[0]),
        pltpu.make_async_copy(buf.at[pl.ds(levels, levels)], bias_out, sems.at[1]),
        pltpu.make_async_copy(line, mass_out, sems.at[2]),
    ]
    for copy in copies:
        copy.start()
    for copy in copies:
        copy.wait()


def last(kept, given, levels, width, rows):
    grad = pltpu.HBM((levels, width), F32)
    mass, gain, bias = pl.pallas_call(
        functools.partial(last_kernel, levels, rows),
        out_shape=(pltpu.HBM((1, rows), F32), grad, grad),
        in_specs=[VMEM, VMEM],
        out_specs=(HBM, HBM, HBM),
        scratch_shapes=[
            pltpu.VMEM((2 * levels, width), F32),
            pltpu.VMEM((1, rows), F32),
            pltpu.SemaphoreType.DMA((3,)),
        ],
        compiler_params=pltpu.CompilerParams(vmem_limit_bytes=8 << 20),
    )(kept, given)
    return mass.reshape(rows), gain, bias


def shards(loop, hidden, exit_depth, teacher, normalizer, tied_head, depth_gain, depth_bias):
    rows_dev, width = hidden.shape
    levels = depth_gain.shape[0]
    block, gain, bias = prep(hidden, exit_depth, teacher, normalizer, depth_gain, depth_bias)
    rows = rows_dev * loop
    early = rows_dev % 16 == 0 and loop == 16
    mapper = functools.partial(map_early, rows, gain, bias) if early else None
    blocks, head, mapped, late = gather_blocks(block, loop, tied_head, mapper)
    if rows_dev % 16:
        whole = jnp.concatenate(blocks, axis=0)
        blocks = [whole[i : i + 16] for i in range(0, rows, 16)]
        late = range(len(blocks))
    keep, give = main(blocks, head, gain, bias, mapped, late, loop)
    return last(*sum_over_loop(keep, give, loop), levels, width, rows_dev)


def solution(mesh):
    loop = mesh.shape["loop"]

    def body(*args):
        return shards(loop, *args)

    return jax.shard_map(
        body,
        mesh=mesh,
        in_specs=(
            P(("groups", "loop"), None),
            P(("groups", "loop")),
            P(("groups", "loop")),
            P(("groups", "loop")),
            P("loop", None),
            P(),
            P(),
        ),
        out_specs=(P(("groups", "loop")), P("groups", None), P("groups", None)),
        check_vma=False,
    )
```

```python
import functools

import jax
import jax.numpy as jnp
from jax import lax
from jax.experimental import pallas as pl
from jax.experimental.pallas import tpu as pltpu
from jax.sharding import PartitionSpec as P

BF16 = jnp.bfloat16
F32 = jnp.float32
LANES = 128
CUTS = 42
TOGETHER = 2
NT = (((1,), (1,)), ((), ()))
VMEM = pl.BlockSpec(memory_space=pltpu.VMEM)
HBM = pl.BlockSpec(memory_space=pl.ANY)


def in_hbm(x):
    return pltpu.with_memory_space_constraint(x, pltpu.HBM)


def ring_of(chips):
    return list(range(0, chips, 2)) + list(range(chips - 1, 0, -2))


def chip_at(place, chips):
    return jnp.where(place < chips // 2, 2 * place, 2 * (chips - 1 - place) + 1)


def place_of(chip, chips):
    return jnp.where(chip % 2 == 0, chip // 2, chips - 1 - chip // 2)


def pieces(value):
    top = value.astype(BF16).astype(F32)
    rest = value - top
    middle = rest.astype(BF16).astype(F32)
    return [top, middle, rest - middle]


def prep_kernel(
    hidden, exit_depth, teacher, normalizer, depth_gain, depth_bias,
    out, gain_out, bias_out, int_buf, float_buf, sems,
):
    rows, width = hidden.shape
    copies = [
        pltpu.make_async_copy(hidden, out.at[:, pl.ds(0, hidden.shape[1])], sems.at[0]),
        pltpu.make_async_copy(exit_depth, int_buf.at[0], sems.at[1]),
        pltpu.make_async_copy(teacher, int_buf.at[1], sems.at[2]),
        pltpu.make_async_copy(normalizer, float_buf, sems.at[3]),
        pltpu.make_async_copy(depth_gain, gain_out, sems.at[4]),
        pltpu.make_async_copy(depth_bias, bias_out, sems.at[5]),
    ]
    for copy in copies:
        copy.start()
    for copy in copies[1:4]:
        copy.wait()
    down = lax.broadcasted_iota(jnp.int32, (rows, rows), 0)
    across = lax.broadcasted_iota(jnp.int32, (rows, rows), 1)

    def column(line):
        square = jnp.broadcast_to(line, (rows, rows))
        return jnp.sum(jnp.where(down == across, square, 0.0), axis=1, keepdims=True)

    token = int_buf[1]
    columns = pieces(column(float_buf[...]))
    for digit in (token & 127, (token >> 7) & 127, token >> 14):
        columns.append(column(digit.astype(F32)))
    columns.append(column(int_buf[0].astype(F32)))
    copies[0].wait()
    wide = out[:, :width].astype(F32)
    mean = jnp.sum(wide * wide, axis=1, keepdims=True) * (1.0 / width)
    columns = pieces(lax.rsqrt(mean + 1e-06)) + columns
    lane = lax.broadcasted_iota(jnp.int32, (rows, LANES), 1)
    meta = jnp.zeros((rows, LANES), F32)
    for i, value in enumerate(columns):
        meta = jnp.where(lane == i, value, meta)
    out[:, width:] = meta.astype(BF16)
    for copy in copies[4:]:
        copy.wait()


def prep(hidden, exit_depth, teacher, normalizer, depth_gain, depth_bias):
    rows, width = hidden.shape
    return pl.pallas_call(
        prep_kernel,
        out_shape=(
            pltpu.VMEM((rows, width + LANES), BF16),
            pltpu.VMEM(depth_gain.shape, F32),
            pltpu.VMEM(depth_bias.shape, F32),
        ),
        in_specs=[HBM] * 6,
        out_specs=(VMEM, VMEM, VMEM),
        scratch_shapes=[
            pltpu.VMEM((2, 1, rows), jnp.int32),
            pltpu.VMEM((1, rows), F32),
            pltpu.SemaphoreType.DMA((6,)),
        ],
        compiler_params=pltpu.CompilerParams(vmem_limit_bytes=8 << 20),
    )(
        in_hbm(hidden),
        in_hbm(exit_depth.reshape(1, rows)),
        in_hbm(teacher.reshape(1, rows)),
        in_hbm(normalizer.reshape(1, rows)),
        in_hbm(depth_gain),
        in_hbm(depth_bias),
    )


def hop_pairs(order, step):
    chips = len(order)
    first = 1 - step % 2
    pairs = []
    for i in range(chips):
        here, after = 2 * order[i], 2 * order[(i + 1) % chips]
        pairs += [(here + first, after + 1 - first), (after + 1 - first, here + first)]
    return pairs


def gather_blocks(block, loop, tied_head, mapper):
    chips = loop // 2
    order = ring_of(chips)
    half = chips // 2
    tie = lambda *xs: lax.optimization_barrier(xs)
    send = lambda x, pairs: lax.ppermute(x, "loop", pairs)
    swap = lambda x: send(x, [(i, i ^ 1) for i in range(loop)])
    blocks = [None] * loop
    first = swap(block)
    blocks[0], blocks[chips] = block, first
    crossed, plain = block, first
    ready = [0, chips]
    mapped = None
    for step in range(1, half + 1):
        crossed = send(crossed, hop_pairs(order, step))
        if step < half:
            plain = send(plain, hop_pairs(order, step))
        if step <= 2:
            head = load(tied_head, step - 1, min(2, half), head if step > 1 else None)
            crossed, head = tie(crossed, head)
        if mapper is not None and step == 3:
            mapped = mapper(None, {i: blocks[i] for i in ready[:6]})
            plain, mapped = tie(plain, mapped)
        if mapper is not None and step == half:
            mapped = mapper(mapped, {i: blocks[i] for i in ready[6:12]})
            crossed, mapped = tie(crossed, mapped)
        far = step if step % 2 else chips - step
        near = chips - far
        mine, theirs = (chips, 0) if step % 2 else (0, chips)
        blocks[mine + far] = crossed
        if step < half:
            blocks[theirs + far] = plain
            blocks[theirs + near] = swap(crossed)
            blocks[mine + near] = swap(plain)
            ready += [mine + far, theirs + far, theirs + near, mine + near]
        else:
            blocks[theirs + far] = swap(crossed)
            ready += [mine + far, theirs + far]
            if mapper is not None:
                mapped = mapper(mapped, {i: blocks[i] for i in ready[12:15]})
    return blocks, head, mapped, ready[15:] if mapper is not None else ready


def map_rows(blocks, places, gain, bias, mapped):
    size, width = blocks[0].shape[0], mapped.shape[1]
    levels = gain.shape[0]
    cut = width // CUTS if width % (CUTS * LANES) == 0 else LANES
    for first in range(0, len(blocks), TOGETHER):
        some = blocks[first : first + TOGETHER]
        meta = jnp.concatenate([b[:, width:] for b in some], axis=0).astype(F32)
        scale = (meta[:, 0:1] + meta[:, 1:2]) + meta[:, 2:3]
        depth = meta[:, 9:10]
        for start in range(0, width, cut):
            at = slice(start, start + cut)
            g, c = gain[0:1, at], bias[0:1, at]
            for level in range(1, levels):
                here = depth == float(level)
                g = jnp.where(here, gain[level : level + 1, at], g)
                c = jnp.where(here, bias[level : level + 1, at], c)
            wide = jnp.concatenate([b[:, at] for b in some], axis=0).astype(F32)
            value = ((wide * scale) * g + c).astype(BF16)
            for i, place in enumerate(places[first : first + TOGETHER]):
                mapped[place * size : (place + 1) * size, at] = value[i * size : (i + 1) * size]


def map_kernel(places, *refs):
    blocks = refs[: len(places)]
    gain, bias = refs[len(places) : len(places) + 2]
    map_rows(blocks, places, gain, bias, refs[-1])


def map_early(rows, gain, bias, mapped, blocks):
    places, blocks = list(blocks), list(blocks.values())
    width = gain.shape[1]
    operands = blocks + [gain, bias] + ([] if mapped is None else [mapped])
    count = len(blocks) * blocks[0].shape[0]
    return pl.pallas_call(
        functools.partial(map_kernel, places),
        out_shape=pltpu.VMEM((rows, width), BF16),
        in_specs=[VMEM] * len(operands),
        out_specs=VMEM,
        input_output_aliases={} if mapped is None else {len(operands) - 1: 0},
        compiler_params=pltpu.CompilerParams(vmem_limit_bytes=8 << 20),
        cost_estimate=pl.CostEstimate(
            flops=20 * count * width, bytes_accessed=4 * count * width, transcendentals=0
        ),
    )(*operands)


def load_kernel(part, parts, head_hbm, *refs):
    head, sems = refs[-2:]
    count = sems.shape[0]
    size = head.shape[0] // (parts * count)
    copies = []
    for k in range(count):
        at = pl.ds((part * count + k) * size, size)
        copies.append(pltpu.make_async_copy(head_hbm.at[at], head.at[at], sems.at[k]))
    for copy in copies:
        copy.start()
    for copy in copies:
        copy.wait()


def load(tied_head, part, parts, loaded):
    operands = [in_hbm(tied_head)] + ([] if loaded is None else [loaded])
    voc, width = tied_head.shape
    return pl.pallas_call(
        functools.partial(load_kernel, part, parts),
        out_shape=pltpu.VMEM(tied_head.shape, BF16),
        in_specs=[HBM] + [VMEM] * (len(operands) - 1),
        out_specs=VMEM,
        input_output_aliases={} if loaded is None else {1: 0},
        scratch_shapes=[pltpu.SemaphoreType.DMA((4,))],
        compiler_params=pltpu.CompilerParams(vmem_limit_bytes=16 << 20),
        cost_estimate=pl.CostEstimate(
            flops=0, bytes_accessed=4 * voc * width // parts, transcendentals=0
        ),
    )(*operands)


def half_sums(blocks, head, slopes, scaled, which, work, out):
    levels = out.shape[0] // 2
    rows = sum(b.shape[0] for b in blocks)
    half = head.shape[1] // 2
    add3 = lambda x: (x[:levels] + x[levels : 2 * levels]) + x[2 * levels : 3 * levels]
    done = 0
    while done < half:
        size = min(256, half - done)
        here = slice(done, done + size)
        at = pl.ds(pl.multiple_of(which * half + done, LANES), size)
        back = jnp.dot(slopes[...], head[:, at], preferred_element_type=F32)
        wide = jnp.concatenate([b[:, at] for b in blocks], axis=0).astype(F32)
        work[:, here] = (back[:rows] * wide).astype(BF16)
        out[levels:, here] = add3(back[rows:])
        done += size
    out[:levels, :half] = add3(jnp.dot(scaled, work[:, :half], preferred_element_type=F32))


def front_kernel(levels, count, late, *refs):
    blocks = refs[:count]
    head, gain, bias = refs[count : count + 3]
    give, slopes, scaled_out, mass_out, mapped = refs[-5:]
    voc, width = head.shape
    rows = mapped.shape[0]
    me = lax.axis_index("loop")
    core = me % 2
    meta = jnp.concatenate([b[:, width:] for b in blocks], axis=0).astype(F32)
    col = lambda i: meta[:, i : i + 1]
    scale = (col(0) + col(1)) + col(2)
    norm = (col(3) + col(4)) + col(5)
    target = (col(6) + 128.0 * col(7) + 16384.0 * col(8)).astype(jnp.int32)
    depth = col(9)

    map_rows([blocks[i] for i in late], late, gain, bias, mapped)
    logits = lax.dot_general(mapped[...], head[...], NT, preferred_element_type=F32)
    prob = jnp.exp(logits - norm)
    columns = me * voc + lax.broadcasted_iota(jnp.int32, (rows, voc), 1)
    slopes[:rows, :] = jnp.where(columns == target, prob - 1.0, prob).astype(BF16)

    mass = prob[:, :LANES]
    for j in range(1, voc // LANES):
        mass = mass + prob[:, j * LANES : (j + 1) * LANES]
    mass_out[...] = mass

    lane = lax.broadcasted_iota(jnp.int32, (rows, LANES), 1).astype(F32)
    pick = jnp.where(lane == depth, 1.0, 0.0).T[:levels]
    scaled = pick * jnp.broadcast_to(scale, (rows, LANES)).T[:levels]
    none = jnp.zeros((16 - 3 * levels, rows), F32)
    scaled = jnp.concatenate(pieces(scaled) + [none], axis=0).astype(BF16)
    scaled_out[...] = scaled
    sums = jnp.dot(pick.astype(BF16), slopes[:rows, :], preferred_element_type=F32)
    none = jnp.zeros((16 - 3 * levels, voc), F32)
    slopes[rows:, :] = jnp.concatenate(pieces(sums) + [none], axis=0).astype(BF16)
    half_sums(blocks, head, slopes, scaled, 1 - core, mapped, give)
    give[:, width // 2 :] = jnp.zeros((2 * levels, rows), F32)


def back_kernel(loop, count, *refs):
    blocks = refs[:count]
    head, slopes, scaled, mass, keep, work = refs[count:]
    rows, half = work.shape
    rows_dev = rows // loop
    chips = loop // 2
    me = lax.axis_index("loop")
    core = me % 2
    half_sums(blocks, head, slopes, scaled[...], core, work, keep)

    index = lax.broadcasted_iota(jnp.int32, (rows, LANES), 0)
    flip = index // (rows // 2)
    relative = (index - flip * (rows // 2)) // rows_dev
    place = place_of(me // 2, chips) + jnp.where(core == 0, relative, chips - relative)
    place = jnp.where(place >= chips, place - chips, place)
    owner = 2 * chip_at(place, chips) + jnp.where(flip == 0, core, 1 - core)
    goes_to = owner * rows_dev + index % rows_dev
    lane = lax.broadcasted_iota(jnp.int32, (rows, LANES), 1)
    move = [jnp.where(goes_to == lane + k, 1.0, 0.0) for k in range(0, rows, LANES)]
    move = jnp.concatenate(move, axis=1).astype(BF16)
    line = jnp.sum(mass[...].T, axis=0, keepdims=True)
    lines = jnp.concatenate(pieces(line) + [jnp.zeros((13, rows), F32)], axis=0)
    moved = jnp.dot(lines.astype(BF16), move, preferred_element_type=F32)
    moved = (moved[0:1] + moved[1:2]) + moved[2:3]
    keep[:, half:] = jnp.broadcast_to(moved, (keep.shape[0], rows))


def main(blocks, head, gain, bias, mapped, late, loop):
    levels = gain.shape[0]
    voc, width = head.shape
    rows = sum(b.shape[0] for b in blocks)
    half = pltpu.VMEM((2 * levels, width // 2 + rows), F32)
    operands = list(blocks) + [head, gain, bias] + ([] if mapped is None else [mapped])
    cost = lambda passes: pl.CostEstimate(
        flops=passes * rows * voc * width, bytes_accessed=voc * width, transcendentals=0
    )
    give, slopes, scaled, mass, _ = pl.pallas_call(
        functools.partial(front_kernel, levels, len(blocks), late),
        out_shape=(
            half,
            pltpu.VMEM((rows + 16, voc), BF16),
            pltpu.VMEM((16, rows), BF16),
            pltpu.VMEM((rows, LANES), F32),
            pltpu.VMEM((rows, width), BF16),
        ),
        in_specs=[VMEM] * len(operands),
        out_specs=(VMEM,) * 5,
        input_output_aliases={} if mapped is None else {len(operands) - 1: 4},
        compiler_params=pltpu.CompilerParams(vmem_limit_bytes=16 << 20),
        cost_estimate=cost(3),
    )(*operands)
    operands = list(blocks) + [head, slopes, scaled, mass]
    keep = pl.pallas_call(
        functools.partial(back_kernel, loop, len(blocks)),
        out_shape=half,
        in_specs=[VMEM] * len(operands),
        out_specs=VMEM,
        scratch_shapes=[pltpu.VMEM((rows, width // 2), BF16)],
        compiler_params=pltpu.CompilerParams(vmem_limit_bytes=16 << 20),
        cost_estimate=cost(1),
    )(*operands)
    return keep, give


def sum_over_loop(keep, give, loop):
    send = lambda x, mask: lax.ppermute(x, "loop", [(i, i ^ mask) for i in range(loop)])
    total = keep + send(give, 1)
    bits = [1 << k for k in range(1, loop.bit_length() - 1)]
    for k in range(0, len(bits) - 1, 2):
        dims = bits[:-1][k : k + 2]
        total = lax.reduce_precision(total, 8, 7)
        sent = total.astype(BF16)
        take = lambda mask: send(sent, mask).astype(F32)
        total = total + take(dims[0])
        if len(dims) == 2:
            total = total + (take(dims[1]) + take(dims[0] ^ dims[1]))
    total = lax.reduce_precision(total, 8, 7)
    total = total + send(total.astype(BF16), bits[-1]).astype(F32)
    return total, send(total, 1)


def last_kernel(levels, rows, kept, given, mass_out, gain_out, bias_out, buf, line, sems):
    width = gain_out.shape[1]
    me = lax.axis_index("loop")
    cut = width // 2
    low = jnp.where(me % 2 == 0, kept[...], given[...])
    high = jnp.where(me % 2 == 0, given[...], kept[...])
    buf[:, :cut], buf[:, cut:width] = low[:, :cut], high[:, :cut]
    every = kept[0:1, cut:] + given[0:1, cut:]
    spread = lax.broadcasted_iota(jnp.int32, (every.shape[1], LANES), 0)
    target = lax.broadcasted_iota(jnp.int32, (every.shape[1], LANES), 1)
    move = jnp.where(spread - me * rows == target, 1.0, 0.0).astype(BF16)
    lines = jnp.concatenate(pieces(every) + [jnp.zeros((13, every.shape[1]), F32)], axis=0)
    own = jnp.dot(lines.astype(BF16), move, preferred_element_type=F32)
    line[...] = ((own[0:1] + own[1:2]) + own[2:3])[:, :rows]
    copies = [
        pltpu.make_async_copy(buf.at[pl.ds(0, levels)], gain_out, sems.at[0]),
        pltpu.make_async_copy(buf.at[pl.ds(levels, levels)], bias_out, sems.at[1]),
        pltpu.make_async_copy(line, mass_out, sems.at[2]),
    ]
    for copy in copies:
        copy.start()
    for copy in copies:
        copy.wait()


def last(kept, given, levels, width, rows):
    grad = pltpu.HBM((levels, width), F32)
    mass, gain, bias = pl.pallas_call(
        functools.partial(last_kernel, levels, rows),
        out_shape=(pltpu.HBM((1, rows), F32), grad, grad),
        in_specs=[VMEM, VMEM],
        out_specs=(HBM, HBM, HBM),
        scratch_shapes=[
            pltpu.VMEM((2 * levels, width), F32),
            pltpu.VMEM((1, rows), F32),
            pltpu.SemaphoreType.DMA((3,)),
        ],
        compiler_params=pltpu.CompilerParams(vmem_limit_bytes=8 << 20),
    )(kept, given)
    return mass.reshape(rows), gain, bias


def shards(loop, hidden, exit_depth, teacher, normalizer, tied_head, depth_gain, depth_bias):
    rows_dev, width = hidden.shape
    levels = depth_gain.shape[0]
    block, gain, bias = prep(hidden, exit_depth, teacher, normalizer, depth_gain, depth_bias)
    rows = rows_dev * loop
    early = rows_dev % 16 == 0 and loop == 16
    mapper = functools.partial(map_early, rows, gain, bias) if early else None
    blocks, head, mapped, late = gather_blocks(block, loop, tied_head, mapper)
    if rows_dev % 16:
        whole = jnp.concatenate(blocks, axis=0)
        blocks = [whole[i : i + 16] for i in range(0, rows, 16)]
        late = range(len(blocks))
    keep, give = main(blocks, head, gain, bias, mapped, late, loop)
    return last(*sum_over_loop(keep, give, loop), levels, width, rows_dev)


def solution(mesh):
    loop = mesh.shape["loop"]

    def body(*args):
        return shards(loop, *args)

    return jax.shard_map(
        body,
        mesh=mesh,
        in_specs=(
            P(("groups", "loop"), None),
            P(("groups", "loop")),
            P(("groups", "loop")),
            P(("groups", "loop")),
            P("loop", None),
            P(),
            P(),
        ),
        out_specs=(P(("groups", "loop")), P("groups", None), P("groups", None)),
        check_vma=False,
    )
```

```python
import functools

import jax
import jax.numpy as jnp
from jax import lax
from jax.experimental import pallas as pl
from jax.experimental.pallas import tpu as pltpu
from jax.sharding import PartitionSpec as P

BF16 = jnp.bfloat16
F32 = jnp.float32
LANES = 128
CUTS = 42
TOGETHER = 2
LOADS = ((0, 3), (3, 4))
NT = (((1,), (1,)), ((), ()))
VMEM = pl.BlockSpec(memory_space=pltpu.VMEM)
HBM = pl.BlockSpec(memory_space=pl.ANY)


def in_hbm(x):
    return pltpu.with_memory_space_constraint(x, pltpu.HBM)


def ring_of(chips):
    return list(range(0, chips, 2)) + list(range(chips - 1, 0, -2))


def chip_at(place, chips):
    return jnp.where(place < chips // 2, 2 * place, 2 * (chips - 1 - place) + 1)


def place_of(chip, chips):
    return jnp.where(chip % 2 == 0, chip // 2, chips - 1 - chip // 2)


def pieces(value):
    top = value.astype(BF16).astype(F32)
    rest = value - top
    middle = rest.astype(BF16).astype(F32)
    return [top, middle, rest - middle]


def prep_kernel(
    hidden, exit_depth, teacher, normalizer, depth_gain, depth_bias,
    out, gain_out, bias_out, int_buf, float_buf, sems,
):
    rows, width = hidden.shape
    copies = [
        pltpu.make_async_copy(hidden, out.at[:, pl.ds(0, hidden.shape[1])], sems.at[0]),
        pltpu.make_async_copy(exit_depth, int_buf.at[0], sems.at[1]),
        pltpu.make_async_copy(teacher, int_buf.at[1], sems.at[2]),
        pltpu.make_async_copy(normalizer, float_buf, sems.at[3]),
        pltpu.make_async_copy(depth_gain, gain_out, sems.at[4]),
        pltpu.make_async_copy(depth_bias, bias_out, sems.at[5]),
    ]
    for copy in copies:
        copy.start()
    for copy in copies[1:4]:
        copy.wait()
    down = lax.broadcasted_iota(jnp.int32, (rows, rows), 0)
    across = lax.broadcasted_iota(jnp.int32, (rows, rows), 1)

    def column(line):
        square = jnp.broadcast_to(line, (rows, rows))
        return jnp.sum(jnp.where(down == across, square, 0.0), axis=1, keepdims=True)

    token = int_buf[1]
    columns = pieces(column(float_buf[...]))
    for digit in (token & 127, (token >> 7) & 127, token >> 14):
        columns.append(column(digit.astype(F32)))
    columns.append(column(int_buf[0].astype(F32)))
    copies[0].wait()
    wide = out[:, :width].astype(F32)
    mean = jnp.sum(wide * wide, axis=1, keepdims=True) * (1.0 / width)
    columns = pieces(lax.rsqrt(mean + 1e-06)) + columns
    lane = lax.broadcasted_iota(jnp.int32, (rows, LANES), 1)
    meta = jnp.zeros((rows, LANES), F32)
    for i, value in enumerate(columns):
        meta = jnp.where(lane == i, value, meta)
    out[:, width:] = meta.astype(BF16)
    for copy in copies[4:]:
        copy.wait()


def prep(hidden, exit_depth, teacher, normalizer, depth_gain, depth_bias):
    rows, width = hidden.shape
    return pl.pallas_call(
        prep_kernel,
        out_shape=(
            pltpu.VMEM((rows, width + LANES), BF16),
            pltpu.VMEM(depth_gain.shape, F32),
            pltpu.VMEM(depth_bias.shape, F32),
        ),
        in_specs=[HBM] * 6,
        out_specs=(VMEM, VMEM, VMEM),
        scratch_shapes=[
            pltpu.VMEM((2, 1, rows), jnp.int32),
            pltpu.VMEM((1, rows), F32),
            pltpu.SemaphoreType.DMA((6,)),
        ],
        compiler_params=pltpu.CompilerParams(vmem_limit_bytes=8 << 20),
    )(
        in_hbm(hidden),
        in_hbm(exit_depth.reshape(1, rows)),
        in_hbm(teacher.reshape(1, rows)),
        in_hbm(normalizer.reshape(1, rows)),
        in_hbm(depth_gain),
        in_hbm(depth_bias),
    )


def hop_pairs(order, step):
    chips = len(order)
    first = 1 - step % 2
    pairs = []
    for i in range(chips):
        here, after = 2 * order[i], 2 * order[(i + 1) % chips]
        pairs += [(here + first, after + 1 - first), (after + 1 - first, here + first)]
    return pairs


def gather_blocks(block, loop, tied_head, mapper):
    chips = loop // 2
    order = ring_of(chips)
    half = chips // 2
    tie = lambda *xs: lax.optimization_barrier(xs)
    send = lambda x, pairs: lax.ppermute(x, "loop", pairs)
    swap = lambda x: send(x, [(i, i ^ 1) for i in range(loop)])
    blocks = [None] * loop
    first = swap(block)
    blocks[0], blocks[chips] = block, first
    crossed, plain = block, first
    ready = [0, chips]
    mapped = None
    for step in range(1, half + 1):
        crossed = send(crossed, hop_pairs(order, step))
        if step < half:
            plain = send(plain, hop_pairs(order, step))
        if step <= 2:
            head = load(tied_head, *(LOADS[step - 1]), head if step > 1 else None)
            crossed, head = tie(crossed, head)
        if mapper is not None and step == 3:
            mapped = mapper(None, {i: blocks[i] for i in ready[:6]})
            plain, mapped = tie(plain, mapped)
        if mapper is not None and step == half:
            mapped = mapper(mapped, {i: blocks[i] for i in ready[6:12]})
            crossed, mapped = tie(crossed, mapped)
        far = step if step % 2 else chips - step
        near = chips - far
        mine, theirs = (chips, 0) if step % 2 else (0, chips)
        blocks[mine + far] = crossed
        if step < half:
            blocks[theirs + far] = plain
            blocks[theirs + near] = swap(crossed)
            blocks[mine + near] = swap(plain)
            ready += [mine + far, theirs + far, theirs + near, mine + near]
        else:
            blocks[theirs + far] = swap(crossed)
            ready += [mine + far, theirs + far]
            if mapper is not None:
                mapped = mapper(mapped, {i: blocks[i] for i in ready[12:15]})
    return blocks, head, mapped, ready[15:] if mapper is not None else ready


def map_rows(blocks, places, gain, bias, mapped):
    size, width = blocks[0].shape[0], mapped.shape[1]
    levels = gain.shape[0]
    cut = width // CUTS if width % (CUTS * LANES) == 0 else LANES
    for first in range(0, len(blocks), TOGETHER):
        some = blocks[first : first + TOGETHER]
        meta = jnp.concatenate([b[:, width:] for b in some], axis=0).astype(F32)
        scale = (meta[:, 0:1] + meta[:, 1:2]) + meta[:, 2:3]
        depth = meta[:, 9:10]
        for start in range(0, width, cut):
            at = slice(start, start + cut)
            g, c = gain[0:1, at], bias[0:1, at]
            for level in range(1, levels):
                here = depth == float(level)
                g = jnp.where(here, gain[level : level + 1, at], g)
                c = jnp.where(here, bias[level : level + 1, at], c)
            wide = jnp.concatenate([b[:, at] for b in some], axis=0).astype(F32)
            value = ((wide * scale) * g + c).astype(BF16)
            for i, place in enumerate(places[first : first + TOGETHER]):
                mapped[place * size : (place + 1) * size, at] = value[i * size : (i + 1) * size]


def map_kernel(places, *refs):
    blocks = refs[: len(places)]
    gain, bias = refs[len(places) : len(places) + 2]
    map_rows(blocks, places, gain, bias, refs[-1])


def map_early(rows, gain, bias, mapped, blocks):
    places, blocks = list(blocks), list(blocks.values())
    width = gain.shape[1]
    operands = blocks + [gain, bias] + ([] if mapped is None else [mapped])
    count = len(blocks) * blocks[0].shape[0]
    return pl.pallas_call(
        functools.partial(map_kernel, places),
        out_shape=pltpu.VMEM((rows, width), BF16),
        in_specs=[VMEM] * len(operands),
        out_specs=VMEM,
        input_output_aliases={} if mapped is None else {len(operands) - 1: 0},
        compiler_params=pltpu.CompilerParams(vmem_limit_bytes=8 << 20),
        cost_estimate=pl.CostEstimate(
            flops=20 * count * width, bytes_accessed=4 * count * width, transcendentals=0
        ),
    )(*operands)


def load_kernel(first, last, head_hbm, *refs):
    head, sems = refs[-2:]
    quarter = head.shape[0] // 4
    size = quarter if last - first > 1 else quarter // 4
    copies = []
    for k, start in enumerate(range(first * quarter, last * quarter, size)):
        at = pl.ds(start, size)
        copies.append(pltpu.make_async_copy(head_hbm.at[at], head.at[at], sems.at[k]))
    for copy in copies:
        copy.start()
    for copy in copies:
        copy.wait()


def load(tied_head, first, last, loaded):
    operands = [in_hbm(tied_head)] + ([] if loaded is None else [loaded])
    voc, width = tied_head.shape
    return pl.pallas_call(
        functools.partial(load_kernel, first, last),
        out_shape=pltpu.VMEM(tied_head.shape, BF16),
        in_specs=[HBM] + [VMEM] * (len(operands) - 1),
        out_specs=VMEM,
        input_output_aliases={} if loaded is None else {1: 0},
        scratch_shapes=[pltpu.SemaphoreType.DMA((4,))],
        compiler_params=pltpu.CompilerParams(vmem_limit_bytes=16 << 20),
        cost_estimate=pl.CostEstimate(
            flops=0, bytes_accessed=voc * width * (last - first), transcendentals=0
        ),
    )(*operands)


def half_sums(blocks, head, slopes, scaled, which, work, out):
    levels = out.shape[0] // 2
    rows = sum(b.shape[0] for b in blocks)
    half = head.shape[1] // 2
    add3 = lambda x: (x[:levels] + x[levels : 2 * levels]) + x[2 * levels : 3 * levels]
    done = 0
    while done < half:
        size = min(256, half - done)
        here = slice(done, done + size)
        at = pl.ds(pl.multiple_of(which * half + done, LANES), size)
        back = jnp.dot(slopes[...], head[:, at], preferred_element_type=F32)
        wide = jnp.concatenate([b[:, at] for b in blocks], axis=0).astype(F32)
        work[:, here] = (back[:rows] * wide).astype(BF16)
        out[levels:, here] = add3(back[rows:])
        done += size
    out[:levels, :half] = add3(jnp.dot(scaled, work[:, :half], preferred_element_type=F32))


def front_kernel(levels, count, late, *refs):
    blocks = refs[:count]
    head, gain, bias = refs[count : count + 3]
    give, slopes, scaled_out, mass_out, mapped = refs[-5:]
    voc, width = head.shape
    rows = mapped.shape[0]
    me = lax.axis_index("loop")
    core = me % 2
    meta = jnp.concatenate([b[:, width:] for b in blocks], axis=0).astype(F32)
    col = lambda i: meta[:, i : i + 1]
    scale = (col(0) + col(1)) + col(2)
    norm = (col(3) + col(4)) + col(5)
    target = (col(6) + 128.0 * col(7) + 16384.0 * col(8)).astype(jnp.int32)
    depth = col(9)

    map_rows([blocks[i] for i in late], late, gain, bias, mapped)
    logits = lax.dot_general(mapped[...], head[...], NT, preferred_element_type=F32)
    prob = jnp.exp(logits - norm)
    columns = me * voc + lax.broadcasted_iota(jnp.int32, (rows, voc), 1)
    slopes[:rows, :] = jnp.where(columns == target, prob - 1.0, prob).astype(BF16)

    mass = prob[:, :LANES]
    for j in range(1, voc // LANES):
        mass = mass + prob[:, j * LANES : (j + 1) * LANES]
    mass_out[...] = mass

    lane = lax.broadcasted_iota(jnp.int32, (rows, LANES), 1).astype(F32)
    pick = jnp.where(lane == depth, 1.0, 0.0).T[:levels]
    scaled = pick * jnp.broadcast_to(scale, (rows, LANES)).T[:levels]
    none = jnp.zeros((16 - 3 * levels, rows), F32)
    scaled = jnp.concatenate(pieces(scaled) + [none], axis=0).astype(BF16)
    scaled_out[...] = scaled
    sums = jnp.dot(pick.astype(BF16), slopes[:rows, :], preferred_element_type=F32)
    none = jnp.zeros((16 - 3 * levels, voc), F32)
    slopes[rows:, :] = jnp.concatenate(pieces(sums) + [none], axis=0).astype(BF16)
    half_sums(blocks, head, slopes, scaled, 1 - core, mapped, give)
    give[:, width // 2 :] = jnp.zeros((2 * levels, rows), F32)


def back_kernel(loop, count, *refs):
    blocks = refs[:count]
    head, slopes, scaled, mass, keep, work = refs[count:]
    rows, half = work.shape
    rows_dev = rows // loop
    chips = loop // 2
    me = lax.axis_index("loop")
    core = me % 2
    half_sums(blocks, head, slopes, scaled[...], core, work, keep)

    index = lax.broadcasted_iota(jnp.int32, (rows, LANES), 0)
    flip = index // (rows // 2)
    relative = (index - flip * (rows // 2)) // rows_dev
    place = place_of(me // 2, chips) + jnp.where(core == 0, relative, chips - relative)
    place = jnp.where(place >= chips, place - chips, place)
    owner = 2 * chip_at(place, chips) + jnp.where(flip == 0, core, 1 - core)
    goes_to = owner * rows_dev + index % rows_dev
    lane = lax.broadcasted_iota(jnp.int32, (rows, LANES), 1)
    move = [jnp.where(goes_to == lane + k, 1.0, 0.0) for k in range(0, rows, LANES)]
    move = jnp.concatenate(move, axis=1).astype(BF16)
    line = jnp.sum(mass[...].T, axis=0, keepdims=True)
    lines = jnp.concatenate(pieces(line) + [jnp.zeros((13, rows), F32)], axis=0)
    moved = jnp.dot(lines.astype(BF16), move, preferred_element_type=F32)
    moved = (moved[0:1] + moved[1:2]) + moved[2:3]
    keep[:, half:] = jnp.broadcast_to(moved, (keep.shape[0], rows))


def main(blocks, head, gain, bias, mapped, late, loop):
    levels = gain.shape[0]
    voc, width = head.shape
    rows = sum(b.shape[0] for b in blocks)
    half = pltpu.VMEM((2 * levels, width // 2 + rows), F32)
    operands = list(blocks) + [head, gain, bias] + ([] if mapped is None else [mapped])
    cost = lambda passes: pl.CostEstimate(
        flops=passes * rows * voc * width, bytes_accessed=voc * width, transcendentals=0
    )
    give, slopes, scaled, mass, _ = pl.pallas_call(
        functools.partial(front_kernel, levels, len(blocks), late),
        out_shape=(
            half,
            pltpu.VMEM((rows + 16, voc), BF16),
            pltpu.VMEM((16, rows), BF16),
            pltpu.VMEM((rows, LANES), F32),
            pltpu.VMEM((rows, width), BF16),
        ),
        in_specs=[VMEM] * len(operands),
        out_specs=(VMEM,) * 5,
        input_output_aliases={} if mapped is None else {len(operands) - 1: 4},
        compiler_params=pltpu.CompilerParams(vmem_limit_bytes=16 << 20),
        cost_estimate=cost(3),
    )(*operands)
    operands = list(blocks) + [head, slopes, scaled, mass]
    keep = pl.pallas_call(
        functools.partial(back_kernel, loop, len(blocks)),
        out_shape=half,
        in_specs=[VMEM] * len(operands),
        out_specs=VMEM,
        scratch_shapes=[pltpu.VMEM((rows, width // 2), BF16)],
        compiler_params=pltpu.CompilerParams(vmem_limit_bytes=16 << 20),
        cost_estimate=cost(1),
    )(*operands)
    return keep, give


def sum_over_loop(keep, give, loop):
    send = lambda x, mask: lax.ppermute(x, "loop", [(i, i ^ mask) for i in range(loop)])
    total = keep + send(give, 1)
    bits = [1 << k for k in range(1, loop.bit_length() - 1)]
    for k in range(0, len(bits) - 1, 2):
        dims = bits[:-1][k : k + 2]
        total = lax.reduce_precision(total, 8, 7)
        sent = total.astype(BF16)
        take = lambda mask: send(sent, mask).astype(F32)
        total = total + take(dims[0])
        if len(dims) == 2:
            total = total + (take(dims[1]) + take(dims[0] ^ dims[1]))
    total = lax.reduce_precision(total, 8, 7)
    total = total + send(total.astype(BF16), bits[-1]).astype(F32)
    return total, send(total, 1)


def last_kernel(levels, rows, kept, given, mass_out, gain_out, bias_out, buf, line, sems):
    width = gain_out.shape[1]
    me = lax.axis_index("loop")
    cut = width // 2
    low = jnp.where(me % 2 == 0, kept[...], given[...])
    high = jnp.where(me % 2 == 0, given[...], kept[...])
    buf[:, :cut], buf[:, cut:width] = low[:, :cut], high[:, :cut]
    every = kept[0:1, cut:] + given[0:1, cut:]
    spread = lax.broadcasted_iota(jnp.int32, (every.shape[1], LANES), 0)
    target = lax.broadcasted_iota(jnp.int32, (every.shape[1], LANES), 1)
    move = jnp.where(spread - me * rows == target, 1.0, 0.0).astype(BF16)
    lines = jnp.concatenate(pieces(every) + [jnp.zeros((13, every.shape[1]), F32)], axis=0)
    own = jnp.dot(lines.astype(BF16), move, preferred_element_type=F32)
    line[...] = ((own[0:1] + own[1:2]) + own[2:3])[:, :rows]
    copies = [
        pltpu.make_async_copy(buf.at[pl.ds(0, levels)], gain_out, sems.at[0]),
        pltpu.make_async_copy(buf.at[pl.ds(levels, levels)], bias_out, sems.at[1]),
        pltpu.make_async_copy(line, mass_out, sems.at[2]),
    ]
    for copy in copies:
        copy.start()
    for copy in copies:
        copy.wait()


def last(kept, given, levels, width, rows):
    grad = pltpu.HBM((levels, width), F32)
    mass, gain, bias = pl.pallas_call(
        functools.partial(last_kernel, levels, rows),
        out_shape=(pltpu.HBM((1, rows), F32), grad, grad),
        in_specs=[VMEM, VMEM],
        out_specs=(HBM, HBM, HBM),
        scratch_shapes=[
            pltpu.VMEM((2 * levels, width), F32),
            pltpu.VMEM((1, rows), F32),
            pltpu.SemaphoreType.DMA((3,)),
        ],
        compiler_params=pltpu.CompilerParams(vmem_limit_bytes=8 << 20),
    )(kept, given)
    return mass.reshape(rows), gain, bias


def shards(loop, hidden, exit_depth, teacher, normalizer, tied_head, depth_gain, depth_bias):
    rows_dev, width = hidden.shape
    levels = depth_gain.shape[0]
    block, gain, bias = prep(hidden, exit_depth, teacher, normalizer, depth_gain, depth_bias)
    rows = rows_dev * loop
    early = rows_dev % 16 == 0 and loop == 16
    mapper = functools.partial(map_early, rows, gain, bias) if early else None
    blocks, head, mapped, late = gather_blocks(block, loop, tied_head, mapper)
    if rows_dev % 16:
        whole = jnp.concatenate(blocks, axis=0)
        blocks = [whole[i : i + 16] for i in range(0, rows, 16)]
        late = range(len(blocks))
    keep, give = main(blocks, head, gain, bias, mapped, late, loop)
    return last(*sum_over_loop(keep, give, loop), levels, width, rows_dev)


def solution(mesh):
    loop = mesh.shape["loop"]

    def body(*args):
        return shards(loop, *args)

    return jax.shard_map(
        body,
        mesh=mesh,
        in_specs=(
            P(("groups", "loop"), None),
            P(("groups", "loop")),
            P(("groups", "loop")),
            P(("groups", "loop")),
            P("loop", None),
            P(),
            P(),
        ),
        out_specs=(P(("groups", "loop")), P("groups", None), P("groups", None)),
        check_vma=False,
    )
```

```python
import functools

import jax
import jax.numpy as jnp
from jax import lax
from jax.experimental import pallas as pl
from jax.experimental.pallas import tpu as pltpu
from jax.sharding import PartitionSpec as P

BF16 = jnp.bfloat16
F32 = jnp.float32
LANES = 128
CUTS = 42
TOGETHER = 2
NT = (((1,), (1,)), ((), ()))
VMEM = pl.BlockSpec(memory_space=pltpu.VMEM)
HBM = pl.BlockSpec(memory_space=pl.ANY)


def in_hbm(x):
    return pltpu.with_memory_space_constraint(x, pltpu.HBM)


def ring_of(chips):
    return list(range(0, chips, 2)) + list(range(chips - 1, 0, -2))


def chip_at(place, chips):
    return jnp.where(place < chips // 2, 2 * place, 2 * (chips - 1 - place) + 1)


def place_of(chip, chips):
    return jnp.where(chip % 2 == 0, chip // 2, chips - 1 - chip // 2)


def pieces(value):
    top = value.astype(BF16).astype(F32)
    rest = value - top
    middle = rest.astype(BF16).astype(F32)
    return [top, middle, rest - middle]


def prep_kernel(
    hidden, exit_depth, teacher, normalizer, depth_gain, depth_bias,
    out, gain_out, bias_out, int_buf, float_buf, sems,
):
    rows, width = hidden.shape
    copies = [
        pltpu.make_async_copy(hidden, out.at[:, pl.ds(0, hidden.shape[1])], sems.at[0]),
        pltpu.make_async_copy(exit_depth, int_buf.at[0], sems.at[1]),
        pltpu.make_async_copy(teacher, int_buf.at[1], sems.at[2]),
        pltpu.make_async_copy(normalizer, float_buf, sems.at[3]),
        pltpu.make_async_copy(depth_gain, gain_out, sems.at[4]),
        pltpu.make_async_copy(depth_bias, bias_out, sems.at[5]),
    ]
    for copy in copies:
        copy.start()
    for copy in copies[1:4]:
        copy.wait()
    down = lax.broadcasted_iota(jnp.int32, (rows, rows), 0)
    across = lax.broadcasted_iota(jnp.int32, (rows, rows), 1)

    def column(line):
        square = jnp.broadcast_to(line, (rows, rows))
        return jnp.sum(jnp.where(down == across, square, 0.0), axis=1, keepdims=True)

    token = int_buf[1]
    columns = pieces(column(float_buf[...]))
    for digit in (token & 127, (token >> 7) & 127, token >> 14):
        columns.append(column(digit.astype(F32)))
    columns.append(column(int_buf[0].astype(F32)))
    copies[0].wait()
    wide = out[:, :width].astype(F32)
    mean = jnp.sum(wide * wide, axis=1, keepdims=True) * (1.0 / width)
    columns = pieces(lax.rsqrt(mean + 1e-06)) + columns
    lane = lax.broadcasted_iota(jnp.int32, (rows, LANES), 1)
    meta = jnp.zeros((rows, LANES), F32)
    for i, value in enumerate(columns):
        meta = jnp.where(lane == i, value, meta)
    out[:, width:] = meta.astype(BF16)
    for copy in copies[4:]:
        copy.wait()


def prep(hidden, exit_depth, teacher, normalizer, depth_gain, depth_bias):
    rows, width = hidden.shape
    return pl.pallas_call(
        prep_kernel,
        out_shape=(
            pltpu.VMEM((rows, width + LANES), BF16),
            pltpu.VMEM(depth_gain.shape, F32),
            pltpu.VMEM(depth_bias.shape, F32),
        ),
        in_specs=[HBM] * 6,
        out_specs=(VMEM, VMEM, VMEM),
        scratch_shapes=[
            pltpu.VMEM((2, 1, rows), jnp.int32),
            pltpu.VMEM((1, rows), F32),
            pltpu.SemaphoreType.DMA((6,)),
        ],
        compiler_params=pltpu.CompilerParams(vmem_limit_bytes=8 << 20),
    )(
        in_hbm(hidden),
        in_hbm(exit_depth.reshape(1, rows)),
        in_hbm(teacher.reshape(1, rows)),
        in_hbm(normalizer.reshape(1, rows)),
        in_hbm(depth_gain),
        in_hbm(depth_bias),
    )


def hop_pairs(order, step):
    chips = len(order)
    first = 1 - step % 2
    pairs = []
    for i in range(chips):
        here, after = 2 * order[i], 2 * order[(i + 1) % chips]
        pairs += [(here + first, after + 1 - first), (after + 1 - first, here + first)]
    return pairs


def gather_blocks(block, loop, tied_head, mapper):
    chips = loop // 2
    order = ring_of(chips)
    half = chips // 2
    tie = lambda *xs: lax.optimization_barrier(xs)
    send = lambda x, pairs: lax.ppermute(x, "loop", pairs)
    swap = lambda x: send(x, [(i, i ^ 1) for i in range(loop)])
    blocks = [None] * loop
    first = swap(block)
    blocks[0], blocks[chips] = block, first
    crossed, plain = block, first
    ready = [0, chips]
    mapped = None
    for step in range(1, half + 1):
        crossed = send(crossed, hop_pairs(order, step))
        if step < half:
            plain = send(plain, hop_pairs(order, step))
        if step == 1:
            head = load(tied_head, 0, 2, None)
            crossed, head = tie(crossed, head)
        if mapper is not None and step == 3:
            mapped = mapper(None, {i: blocks[i] for i in ready[:6]})
            plain, mapped = tie(plain, mapped)
        if step == half:
            head = load(tied_head, 1, 2, head)
            crossed, head = tie(crossed, head)
        far = step if step % 2 else chips - step
        near = chips - far
        mine, theirs = (chips, 0) if step % 2 else (0, chips)
        blocks[mine + far] = crossed
        if step < half:
            blocks[theirs + far] = plain
            blocks[theirs + near] = swap(crossed)
            blocks[mine + near] = swap(plain)
            ready += [mine + far, theirs + far, theirs + near, mine + near]
        else:
            blocks[theirs + far] = swap(crossed)
            ready += [mine + far, theirs + far]
            if mapper is not None:
                mapped = mapper(mapped, {i: blocks[i] for i in ready[6:15]})
    return blocks, head, mapped, ready[15:] if mapper is not None else ready


def map_rows(blocks, places, gain, bias, mapped):
    size, width = blocks[0].shape[0], mapped.shape[1]
    levels = gain.shape[0]
    cut = width // CUTS if width % (CUTS * LANES) == 0 else LANES
    for first in range(0, len(blocks), TOGETHER):
        some = blocks[first : first + TOGETHER]
        meta = jnp.concatenate([b[:, width:] for b in some], axis=0).astype(F32)
        scale = (meta[:, 0:1] + meta[:, 1:2]) + meta[:, 2:3]
        depth = meta[:, 9:10]
        for start in range(0, width, cut):
            at = slice(start, start + cut)
            g, c = gain[0:1, at], bias[0:1, at]
            for level in range(1, levels):
                here = depth == float(level)
                g = jnp.where(here, gain[level : level + 1, at], g)
                c = jnp.where(here, bias[level : level + 1, at], c)
            wide = jnp.concatenate([b[:, at] for b in some], axis=0).astype(F32)
            value = ((wide * scale) * g + c).astype(BF16)
            for i, place in enumerate(places[first : first + TOGETHER]):
                mapped[place * size : (place + 1) * size, at] = value[i * size : (i + 1) * size]


def map_kernel(places, *refs):
    blocks = refs[: len(places)]
    gain, bias = refs[len(places) : len(places) + 2]
    map_rows(blocks, places, gain, bias, refs[-1])


def map_early(rows, gain, bias, mapped, blocks):
    places, blocks = list(blocks), list(blocks.values())
    width = gain.shape[1]
    operands = blocks + [gain, bias] + ([] if mapped is None else [mapped])
    count = len(blocks) * blocks[0].shape[0]
    return pl.pallas_call(
        functools.partial(map_kernel, places),
        out_shape=pltpu.VMEM((rows, width), BF16),
        in_specs=[VMEM] * len(operands),
        out_specs=VMEM,
        input_output_aliases={} if mapped is None else {len(operands) - 1: 0},
        compiler_params=pltpu.CompilerParams(vmem_limit_bytes=8 << 20),
        cost_estimate=pl.CostEstimate(
            flops=20 * count * width, bytes_accessed=4 * count * width, transcendentals=0
        ),
    )(*operands)


def load_kernel(part, parts, head_hbm, *refs):
    head, sems = refs[-2:]
    count = sems.shape[0]
    size = head.shape[0] // (parts * count)
    copies = []
    for k in range(count):
        at = pl.ds((part * count + k) * size, size)
        copies.append(pltpu.make_async_copy(head_hbm.at[at], head.at[at], sems.at[k]))
    for copy in copies:
        copy.start()
    for copy in copies:
        copy.wait()


def load(tied_head, part, parts, loaded):
    operands = [in_hbm(tied_head)] + ([] if loaded is None else [loaded])
    voc, width = tied_head.shape
    return pl.pallas_call(
        functools.partial(load_kernel, part, parts),
        out_shape=pltpu.VMEM(tied_head.shape, BF16),
        in_specs=[HBM] + [VMEM] * (len(operands) - 1),
        out_specs=VMEM,
        input_output_aliases={} if loaded is None else {1: 0},
        scratch_shapes=[pltpu.SemaphoreType.DMA((4,))],
        compiler_params=pltpu.CompilerParams(vmem_limit_bytes=16 << 20),
        cost_estimate=pl.CostEstimate(
            flops=0, bytes_accessed=4 * voc * width // parts, transcendentals=0
        ),
    )(*operands)


def half_sums(blocks, head, slopes, scaled, which, work, out):
    levels = out.shape[0] // 2
    rows = sum(b.shape[0] for b in blocks)
    half = head.shape[1] // 2
    add3 = lambda x: (x[:levels] + x[levels : 2 * levels]) + x[2 * levels : 3 * levels]
    done = 0
    while done < half:
        size = min(256, half - done)
        here = slice(done, done + size)
        at = pl.ds(pl.multiple_of(which * half + done, LANES), size)
        back = jnp.dot(slopes[...], head[:, at], preferred_element_type=F32)
        wide = jnp.concatenate([b[:, at] for b in blocks], axis=0).astype(F32)
        work[:, here] = (back[:rows] * wide).astype(BF16)
        out[levels:, here] = add3(back[rows:])
        done += size
    out[:levels, :half] = add3(jnp.dot(scaled, work[:, :half], preferred_element_type=F32))


def front_kernel(levels, count, late, *refs):
    blocks = refs[:count]
    head, gain, bias = refs[count : count + 3]
    give, slopes, scaled_out, mass_out, mapped = refs[-5:]
    voc, width = head.shape
    rows = mapped.shape[0]
    me = lax.axis_index("loop")
    core = me % 2
    meta = jnp.concatenate([b[:, width:] for b in blocks], axis=0).astype(F32)
    col = lambda i: meta[:, i : i + 1]
    scale = (col(0) + col(1)) + col(2)
    norm = (col(3) + col(4)) + col(5)
    target = (col(6) + 128.0 * col(7) + 16384.0 * col(8)).astype(jnp.int32)
    depth = col(9)

    map_rows([blocks[i] for i in late], late, gain, bias, mapped)
    logits = lax.dot_general(mapped[...], head[...], NT, preferred_element_type=F32)
    prob = jnp.exp(logits - norm)
    columns = me * voc + lax.broadcasted_iota(jnp.int32, (rows, voc), 1)
    slopes[:rows, :] = jnp.where(columns == target, prob - 1.0, prob).astype(BF16)

    mass = prob[:, :LANES]
    for j in range(1, voc // LANES):
        mass = mass + prob[:, j * LANES : (j + 1) * LANES]
    mass_out[...] = mass

    lane = lax.broadcasted_iota(jnp.int32, (rows, LANES), 1).astype(F32)
    pick = jnp.where(lane == depth, 1.0, 0.0).T[:levels]
    scaled = pick * jnp.broadcast_to(scale, (rows, LANES)).T[:levels]
    none = jnp.zeros((16 - 3 * levels, rows), F32)
    scaled = jnp.concatenate(pieces(scaled) + [none], axis=0).astype(BF16)
    scaled_out[...] = scaled
    sums = jnp.dot(pick.astype(BF16), slopes[:rows, :], preferred_element_type=F32)
    none = jnp.zeros((16 - 3 * levels, voc), F32)
    slopes[rows:, :] = jnp.concatenate(pieces(sums) + [none], axis=0).astype(BF16)
    half_sums(blocks, head, slopes, scaled, 1 - core, mapped, give)
    give[:, width // 2 :] = jnp.zeros((2 * levels, rows), F32)


def back_kernel(loop, count, *refs):
    blocks = refs[:count]
    head, slopes, scaled, mass, keep, work = refs[count:]
    rows, half = work.shape
    rows_dev = rows // loop
    chips = loop // 2
    me = lax.axis_index("loop")
    core = me % 2
    half_sums(blocks, head, slopes, scaled[...], core, work, keep)

    index = lax.broadcasted_iota(jnp.int32, (rows, LANES), 0)
    flip = index // (rows // 2)
    relative = (index - flip * (rows // 2)) // rows_dev
    place = place_of(me // 2, chips) + jnp.where(core == 0, relative, chips - relative)
    place = jnp.where(place >= chips, place - chips, place)
    owner = 2 * chip_at(place, chips) + jnp.where(flip == 0, core, 1 - core)
    goes_to = owner * rows_dev + index % rows_dev
    lane = lax.broadcasted_iota(jnp.int32, (rows, LANES), 1)
    move = [jnp.where(goes_to == lane + k, 1.0, 0.0) for k in range(0, rows, LANES)]
    move = jnp.concatenate(move, axis=1).astype(BF16)
    line = jnp.sum(mass[...].T, axis=0, keepdims=True)
    lines = jnp.concatenate(pieces(line) + [jnp.zeros((13, rows), F32)], axis=0)
    moved = jnp.dot(lines.astype(BF16), move, preferred_element_type=F32)
    moved = (moved[0:1] + moved[1:2]) + moved[2:3]
    keep[:, half:] = jnp.broadcast_to(moved, (keep.shape[0], rows))


def main(blocks, head, gain, bias, mapped, late, loop):
    levels = gain.shape[0]
    voc, width = head.shape
    rows = sum(b.shape[0] for b in blocks)
    half = pltpu.VMEM((2 * levels, width // 2 + rows), F32)
    operands = list(blocks) + [head, gain, bias] + ([] if mapped is None else [mapped])
    cost = lambda passes: pl.CostEstimate(
        flops=passes * rows * voc * width, bytes_accessed=voc * width, transcendentals=0
    )
    give, slopes, scaled, mass, _ = pl.pallas_call(
        functools.partial(front_kernel, levels, len(blocks), late),
        out_shape=(
            half,
            pltpu.VMEM((rows + 16, voc), BF16),
            pltpu.VMEM((16, rows), BF16),
            pltpu.VMEM((rows, LANES), F32),
            pltpu.VMEM((rows, width), BF16),
        ),
        in_specs=[VMEM] * len(operands),
        out_specs=(VMEM,) * 5,
        input_output_aliases={} if mapped is None else {len(operands) - 1: 4},
        compiler_params=pltpu.CompilerParams(vmem_limit_bytes=16 << 20),
        cost_estimate=cost(3),
    )(*operands)
    operands = list(blocks) + [head, slopes, scaled, mass]
    keep = pl.pallas_call(
        functools.partial(back_kernel, loop, len(blocks)),
        out_shape=half,
        in_specs=[VMEM] * len(operands),
        out_specs=VMEM,
        scratch_shapes=[pltpu.VMEM((rows, width // 2), BF16)],
        compiler_params=pltpu.CompilerParams(vmem_limit_bytes=16 << 20),
        cost_estimate=cost(1),
    )(*operands)
    return keep, give


def sum_over_loop(keep, give, loop):
    send = lambda x, mask: lax.ppermute(x, "loop", [(i, i ^ mask) for i in range(loop)])
    total = keep + send(give, 1)
    bits = [1 << k for k in range(1, loop.bit_length() - 1)]
    for k in range(0, len(bits) - 1, 2):
        dims = bits[:-1][k : k + 2]
        total = lax.reduce_precision(total, 8, 7)
        sent = total.astype(BF16)
        take = lambda mask: send(sent, mask).astype(F32)
        total = total + take(dims[0])
        if len(dims) == 2:
            total = total + (take(dims[1]) + take(dims[0] ^ dims[1]))
    total = lax.reduce_precision(total, 8, 7)
    total = total + send(total.astype(BF16), bits[-1]).astype(F32)
    return total, send(total, 1)


def last_kernel(levels, rows, kept, given, mass_out, gain_out, bias_out, buf, line, sems):
    width = gain_out.shape[1]
    me = lax.axis_index("loop")
    cut = width // 2
    low = jnp.where(me % 2 == 0, kept[...], given[...])
    high = jnp.where(me % 2 == 0, given[...], kept[...])
    buf[:, :cut], buf[:, cut:width] = low[:, :cut], high[:, :cut]
    every = kept[0:1, cut:] + given[0:1, cut:]
    spread = lax.broadcasted_iota(jnp.int32, (every.shape[1], LANES), 0)
    target = lax.broadcasted_iota(jnp.int32, (every.shape[1], LANES), 1)
    move = jnp.where(spread - me * rows == target, 1.0, 0.0).astype(BF16)
    lines = jnp.concatenate(pieces(every) + [jnp.zeros((13, every.shape[1]), F32)], axis=0)
    own = jnp.dot(lines.astype(BF16), move, preferred_element_type=F32)
    line[...] = ((own[0:1] + own[1:2]) + own[2:3])[:, :rows]
    copies = [
        pltpu.make_async_copy(buf.at[pl.ds(0, levels)], gain_out, sems.at[0]),
        pltpu.make_async_copy(buf.at[pl.ds(levels, levels)], bias_out, sems.at[1]),
        pltpu.make_async_copy(line, mass_out, sems.at[2]),
    ]
    for copy in copies:
        copy.start()
    for copy in copies:
        copy.wait()


def last(kept, given, levels, width, rows):
    grad = pltpu.HBM((levels, width), F32)
    mass, gain, bias = pl.pallas_call(
        functools.partial(last_kernel, levels, rows),
        out_shape=(pltpu.HBM((1, rows), F32), grad, grad),
        in_specs=[VMEM, VMEM],
        out_specs=(HBM, HBM, HBM),
        scratch_shapes=[
            pltpu.VMEM((2 * levels, width), F32),
            pltpu.VMEM((1, rows), F32),
            pltpu.SemaphoreType.DMA((3,)),
        ],
        compiler_params=pltpu.CompilerParams(vmem_limit_bytes=8 << 20),
    )(kept, given)
    return mass.reshape(rows), gain, bias


def shards(loop, hidden, exit_depth, teacher, normalizer, tied_head, depth_gain, depth_bias):
    rows_dev, width = hidden.shape
    levels = depth_gain.shape[0]
    block, gain, bias = prep(hidden, exit_depth, teacher, normalizer, depth_gain, depth_bias)
    rows = rows_dev * loop
    early = rows_dev % 16 == 0 and loop == 16
    mapper = functools.partial(map_early, rows, gain, bias) if early else None
    blocks, head, mapped, late = gather_blocks(block, loop, tied_head, mapper)
    if rows_dev % 16:
        whole = jnp.concatenate(blocks, axis=0)
        blocks = [whole[i : i + 16] for i in range(0, rows, 16)]
        late = range(len(blocks))
    keep, give = main(blocks, head, gain, bias, mapped, late, loop)
    return last(*sum_over_loop(keep, give, loop), levels, width, rows_dev)


def solution(mesh):
    loop = mesh.shape["loop"]

    def body(*args):
        return shards(loop, *args)

    return jax.shard_map(
        body,
        mesh=mesh,
        in_specs=(
            P(("groups", "loop"), None),
            P(("groups", "loop")),
            P(("groups", "loop")),
            P(("groups", "loop")),
            P("loop", None),
            P(),
            P(),
        ),
        out_specs=(P(("groups", "loop")), P("groups", None), P("groups", None)),
        check_vma=False,
    )
```

```python
import functools

import jax
import jax.numpy as jnp
from jax import lax
from jax.experimental import pallas as pl
from jax.experimental.pallas import tpu as pltpu
from jax.sharding import PartitionSpec as P

BF16 = jnp.bfloat16
F32 = jnp.float32
LANES = 128
CUTS = 42
TOGETHER = 2
FLOPS_HINT = 4_000_000_000
NT = (((1,), (1,)), ((), ()))
VMEM = pl.BlockSpec(memory_space=pltpu.VMEM)
HBM = pl.BlockSpec(memory_space=pl.ANY)


def in_hbm(x):
    return pltpu.with_memory_space_constraint(x, pltpu.HBM)


def ring_of(chips):
    return list(range(0, chips, 2)) + list(range(chips - 1, 0, -2))


def chip_at(place, chips):
    return jnp.where(place < chips // 2, 2 * place, 2 * (chips - 1 - place) + 1)


def place_of(chip, chips):
    return jnp.where(chip % 2 == 0, chip // 2, chips - 1 - chip // 2)


def pieces(value):
    top = value.astype(BF16).astype(F32)
    rest = value - top
    middle = rest.astype(BF16).astype(F32)
    return [top, middle, rest - middle]


def prep_kernel(
    hidden, exit_depth, teacher, normalizer, depth_gain, depth_bias,
    out, gain_out, bias_out, int_buf, float_buf, sems,
):
    rows, width = hidden.shape
    copies = [
        pltpu.make_async_copy(hidden, out.at[:, pl.ds(0, hidden.shape[1])], sems.at[0]),
        pltpu.make_async_copy(exit_depth, int_buf.at[0], sems.at[1]),
        pltpu.make_async_copy(teacher, int_buf.at[1], sems.at[2]),
        pltpu.make_async_copy(normalizer, float_buf, sems.at[3]),
        pltpu.make_async_copy(depth_gain, gain_out, sems.at[4]),
        pltpu.make_async_copy(depth_bias, bias_out, sems.at[5]),
    ]
    for copy in copies:
        copy.start()
    for copy in copies[1:4]:
        copy.wait()
    down = lax.broadcasted_iota(jnp.int32, (rows, rows), 0)
    across = lax.broadcasted_iota(jnp.int32, (rows, rows), 1)

    def column(line):
        square = jnp.broadcast_to(line, (rows, rows))
        return jnp.sum(jnp.where(down == across, square, 0.0), axis=1, keepdims=True)

    token = int_buf[1]
    columns = pieces(column(float_buf[...]))
    for digit in (token & 127, (token >> 7) & 127, token >> 14):
        columns.append(column(digit.astype(F32)))
    columns.append(column(int_buf[0].astype(F32)))
    copies[0].wait()
    wide = out[:, :width].astype(F32)
    mean = jnp.sum(wide * wide, axis=1, keepdims=True) * (1.0 / width)
    columns = pieces(lax.rsqrt(mean + 1e-06)) + columns
    lane = lax.broadcasted_iota(jnp.int32, (rows, LANES), 1)
    meta = jnp.zeros((rows, LANES), F32)
    for i, value in enumerate(columns):
        meta = jnp.where(lane == i, value, meta)
    out[:, width:] = meta.astype(BF16)
    for copy in copies[4:]:
        copy.wait()


def prep(hidden, exit_depth, teacher, normalizer, depth_gain, depth_bias):
    rows, width = hidden.shape
    return pl.pallas_call(
        prep_kernel,
        out_shape=(
            pltpu.VMEM((rows, width + LANES), BF16),
            pltpu.VMEM(depth_gain.shape, F32),
            pltpu.VMEM(depth_bias.shape, F32),
        ),
        in_specs=[HBM] * 6,
        out_specs=(VMEM, VMEM, VMEM),
        scratch_shapes=[
            pltpu.VMEM((2, 1, rows), jnp.int32),
            pltpu.VMEM((1, rows), F32),
            pltpu.SemaphoreType.DMA((6,)),
        ],
        compiler_params=pltpu.CompilerParams(vmem_limit_bytes=8 << 20),
    )(
        in_hbm(hidden),
        in_hbm(exit_depth.reshape(1, rows)),
        in_hbm(teacher.reshape(1, rows)),
        in_hbm(normalizer.reshape(1, rows)),
        in_hbm(depth_gain),
        in_hbm(depth_bias),
    )


def hop_pairs(order, step):
    chips = len(order)
    first = 1 - step % 2
    pairs = []
    for i in range(chips):
        here, after = 2 * order[i], 2 * order[(i + 1) % chips]
        pairs += [(here + first, after + 1 - first), (after + 1 - first, here + first)]
    return pairs


def gather_blocks(block, loop, mapper):
    chips = loop // 2
    order = ring_of(chips)
    half = chips // 2
    tie = lambda *xs: lax.optimization_barrier(xs)
    send = lambda x, pairs: lax.ppermute(x, "loop", pairs)
    swap = lambda x: send(x, [(i, i ^ 1) for i in range(loop)])
    blocks = [None] * loop
    first = swap(block)
    blocks[0], blocks[chips] = block, first
    crossed, plain = block, first
    ready = [0, chips]
    mapped = None
    for step in range(1, half + 1):
        crossed = send(crossed, hop_pairs(order, step))
        if step < half:
            plain = send(plain, hop_pairs(order, step))
        if mapper is not None and step == 3:
            mapped = mapper(None, {i: blocks[i] for i in ready[:6]})
            plain, mapped = tie(plain, mapped)
        if mapper is not None and step == half:
            mapped = mapper(mapped, {i: blocks[i] for i in ready[6:12]})
            crossed, mapped = tie(crossed, mapped)
        far = step if step % 2 else chips - step
        near = chips - far
        mine, theirs = (chips, 0) if step % 2 else (0, chips)
        blocks[mine + far] = crossed
        if step < half:
            blocks[theirs + far] = plain
            blocks[theirs + near] = swap(crossed)
            blocks[mine + near] = swap(plain)
            ready += [mine + far, theirs + far, theirs + near, mine + near]
        else:
            blocks[theirs + far] = swap(crossed)
            ready += [mine + far, theirs + far]
            if mapper is not None:
                mapped = mapper(mapped, {i: blocks[i] for i in ready[12:15]})
    return blocks, mapped, ready[15:] if mapper is not None else ready


def map_rows(blocks, places, gain, bias, mapped):
    size, width = blocks[0].shape[0], mapped.shape[1]
    levels = gain.shape[0]
    cut = width // CUTS if width % (CUTS * LANES) == 0 else LANES
    for first in range(0, len(blocks), TOGETHER):
        some = blocks[first : first + TOGETHER]
        meta = jnp.concatenate([b[:, width:] for b in some], axis=0).astype(F32)
        scale = (meta[:, 0:1] + meta[:, 1:2]) + meta[:, 2:3]
        depth = meta[:, 9:10]
        for start in range(0, width, cut):
            at = slice(start, start + cut)
            g, c = gain[0:1, at], bias[0:1, at]
            for level in range(1, levels):
                here = depth == float(level)
                g = jnp.where(here, gain[level : level + 1, at], g)
                c = jnp.where(here, bias[level : level + 1, at], c)
            wide = jnp.concatenate([b[:, at] for b in some], axis=0).astype(F32)
            value = ((wide * scale) * g + c).astype(BF16)
            for i, place in enumerate(places[first : first + TOGETHER]):
                mapped[place * size : (place + 1) * size, at] = value[i * size : (i + 1) * size]


def map_kernel(places, *refs):
    blocks = refs[: len(places)]
    gain, bias = refs[len(places) : len(places) + 2]
    map_rows(blocks, places, gain, bias, refs[-1])


def map_early(rows, gain, bias, mapped, blocks):
    places, blocks = list(blocks), list(blocks.values())
    width = gain.shape[1]
    operands = blocks + [gain, bias] + ([] if mapped is None else [mapped])
    count = len(blocks) * blocks[0].shape[0]
    return pl.pallas_call(
        functools.partial(map_kernel, places),
        out_shape=pltpu.VMEM((rows, width), BF16),
        in_specs=[VMEM] * len(operands),
        out_specs=VMEM,
        input_output_aliases={} if mapped is None else {len(operands) - 1: 0},
        compiler_params=pltpu.CompilerParams(vmem_limit_bytes=8 << 20),
        cost_estimate=pl.CostEstimate(
            flops=FLOPS_HINT if mapped is None else 0, bytes_accessed=4 * count * width, transcendentals=0
        ),
    )(*operands)


def half_sums(blocks, head, slopes, scaled, which, work, out):
    levels = out.shape[0] // 2
    rows = sum(b.shape[0] for b in blocks)
    half = head.shape[1] // 2
    add3 = lambda x: (x[:levels] + x[levels : 2 * levels]) + x[2 * levels : 3 * levels]
    done = 0
    while done < half:
        size = min(256, half - done)
        here = slice(done, done + size)
        at = pl.ds(pl.multiple_of(which * half + done, LANES), size)
        back = jnp.dot(slopes[...], head[:, at], preferred_element_type=F32)
        wide = jnp.concatenate([b[:, at] for b in blocks], axis=0).astype(F32)
        work[:, here] = (back[:rows] * wide).astype(BF16)
        out[levels:, here] = add3(back[rows:])
        done += size
    out[:levels, :half] = add3(jnp.dot(scaled, work[:, :half], preferred_element_type=F32))


def front_kernel(levels, count, late, *refs):
    blocks = refs[:count]
    head, gain, bias = refs[count : count + 3]
    give, slopes, scaled_out, mass_out, mapped = refs[-5:]
    voc, width = head.shape
    rows = mapped.shape[0]
    me = lax.axis_index("loop")
    core = me % 2
    meta = jnp.concatenate([b[:, width:] for b in blocks], axis=0).astype(F32)
    col = lambda i: meta[:, i : i + 1]
    scale = (col(0) + col(1)) + col(2)
    norm = (col(3) + col(4)) + col(5)
    target = (col(6) + 128.0 * col(7) + 16384.0 * col(8)).astype(jnp.int32)
    depth = col(9)

    map_rows([blocks[i] for i in late], late, gain, bias, mapped)
    logits = lax.dot_general(mapped[...], head[...], NT, preferred_element_type=F32)
    prob = jnp.exp(logits - norm)
    columns = me * voc + lax.broadcasted_iota(jnp.int32, (rows, voc), 1)
    slopes[:rows, :] = jnp.where(columns == target, prob - 1.0, prob).astype(BF16)

    mass = prob[:, :LANES]
    for j in range(1, voc // LANES):
        mass = mass + prob[:, j * LANES : (j + 1) * LANES]
    mass_out[...] = mass

    lane = lax.broadcasted_iota(jnp.int32, (rows, LANES), 1).astype(F32)
    pick = jnp.where(lane == depth, 1.0, 0.0).T[:levels]
    scaled = pick * jnp.broadcast_to(scale, (rows, LANES)).T[:levels]
    none = jnp.zeros((16 - 3 * levels, rows), F32)
    scaled = jnp.concatenate(pieces(scaled) + [none], axis=0).astype(BF16)
    scaled_out[...] = scaled
    sums = jnp.dot(pick.astype(BF16), slopes[:rows, :], preferred_element_type=F32)
    none = jnp.zeros((16 - 3 * levels, voc), F32)
    slopes[rows:, :] = jnp.concatenate(pieces(sums) + [none], axis=0).astype(BF16)
    half_sums(blocks, head, slopes, scaled, 1 - core, mapped, give)
    give[:, width // 2 :] = jnp.zeros((2 * levels, rows), F32)


def back_kernel(loop, count, *refs):
    blocks = refs[:count]
    head, slopes, scaled, mass, keep, work = refs[count:]
    rows, half = work.shape
    rows_dev = rows // loop
    chips = loop // 2
    me = lax.axis_index("loop")
    core = me % 2
    half_sums(blocks, head, slopes, scaled[...], core, work, keep)

    index = lax.broadcasted_iota(jnp.int32, (rows, LANES), 0)
    flip = index // (rows // 2)
    relative = (index - flip * (rows // 2)) // rows_dev
    place = place_of(me // 2, chips) + jnp.where(core == 0, relative, chips - relative)
    place = jnp.where(place >= chips, place - chips, place)
    owner = 2 * chip_at(place, chips) + jnp.where(flip == 0, core, 1 - core)
    goes_to = owner * rows_dev + index % rows_dev
    lane = lax.broadcasted_iota(jnp.int32, (rows, LANES), 1)
    move = [jnp.where(goes_to == lane + k, 1.0, 0.0) for k in range(0, rows, LANES)]
    move = jnp.concatenate(move, axis=1).astype(BF16)
    line = jnp.sum(mass[...].T, axis=0, keepdims=True)
    lines = jnp.concatenate(pieces(line) + [jnp.zeros((13, rows), F32)], axis=0)
    moved = jnp.dot(lines.astype(BF16), move, preferred_element_type=F32)
    moved = (moved[0:1] + moved[1:2]) + moved[2:3]
    keep[:, half:] = jnp.broadcast_to(moved, (keep.shape[0], rows))


def main(blocks, head, gain, bias, mapped, late, loop):
    levels = gain.shape[0]
    voc, width = head.shape
    rows = sum(b.shape[0] for b in blocks)
    half = pltpu.VMEM((2 * levels, width // 2 + rows), F32)
    operands = list(blocks) + [head, gain, bias] + ([] if mapped is None else [mapped])
    cost = lambda passes: pl.CostEstimate(
        flops=passes * rows * voc * width, bytes_accessed=voc * width, transcendentals=0
    )
    give, slopes, scaled, mass, _ = pl.pallas_call(
        functools.partial(front_kernel, levels, len(blocks), late),
        out_shape=(
            half,
            pltpu.VMEM((rows + 16, voc), BF16),
            pltpu.VMEM((16, rows), BF16),
            pltpu.VMEM((rows, LANES), F32),
            pltpu.VMEM((rows, width), BF16),
        ),
        in_specs=[VMEM] * len(operands),
        out_specs=(VMEM,) * 5,
        input_output_aliases={} if mapped is None else {len(operands) - 1: 4},
        compiler_params=pltpu.CompilerParams(vmem_limit_bytes=16 << 20),
        cost_estimate=cost(3),
    )(*operands)
    operands = list(blocks) + [head, slopes, scaled, mass]
    keep = pl.pallas_call(
        functools.partial(back_kernel, loop, len(blocks)),
        out_shape=half,
        in_specs=[VMEM] * len(operands),
        out_specs=VMEM,
        scratch_shapes=[pltpu.VMEM((rows, width // 2), BF16)],
        compiler_params=pltpu.CompilerParams(vmem_limit_bytes=16 << 20),
        cost_estimate=cost(1),
    )(*operands)
    return keep, give


def sum_over_loop(keep, give, loop):
    send = lambda x, mask: lax.ppermute(x, "loop", [(i, i ^ mask) for i in range(loop)])
    total = keep + send(give, 1)
    bits = [1 << k for k in range(1, loop.bit_length() - 1)]
    for k in range(0, len(bits) - 1, 2):
        dims = bits[:-1][k : k + 2]
        total = lax.reduce_precision(total, 8, 7)
        sent = total.astype(BF16)
        take = lambda mask: send(sent, mask).astype(F32)
        total = total + take(dims[0])
        if len(dims) == 2:
            total = total + (take(dims[1]) + take(dims[0] ^ dims[1]))
    total = lax.reduce_precision(total, 8, 7)
    total = total + send(total.astype(BF16), bits[-1]).astype(F32)
    return total, send(total, 1)


def last_kernel(levels, rows, kept, given, mass_out, gain_out, bias_out, buf, line, sems):
    width = gain_out.shape[1]
    me = lax.axis_index("loop")
    cut = width // 2
    low = jnp.where(me % 2 == 0, kept[...], given[...])
    high = jnp.where(me % 2 == 0, given[...], kept[...])
    buf[:, :cut], buf[:, cut:width] = low[:, :cut], high[:, :cut]
    every = kept[0:1, cut:] + given[0:1, cut:]
    spread = lax.broadcasted_iota(jnp.int32, (every.shape[1], LANES), 0)
    target = lax.broadcasted_iota(jnp.int32, (every.shape[1], LANES), 1)
    move = jnp.where(spread - me * rows == target, 1.0, 0.0).astype(BF16)
    lines = jnp.concatenate(pieces(every) + [jnp.zeros((13, every.shape[1]), F32)], axis=0)
    own = jnp.dot(lines.astype(BF16), move, preferred_element_type=F32)
    line[...] = ((own[0:1] + own[1:2]) + own[2:3])[:, :rows]
    copies = [
        pltpu.make_async_copy(buf.at[pl.ds(0, levels)], gain_out, sems.at[0]),
        pltpu.make_async_copy(buf.at[pl.ds(levels, levels)], bias_out, sems.at[1]),
        pltpu.make_async_copy(line, mass_out, sems.at[2]),
    ]
    for copy in copies:
        copy.start()
    for copy in copies:
        copy.wait()


def last(kept, given, levels, width, rows):
    grad = pltpu.HBM((levels, width), F32)
    mass, gain, bias = pl.pallas_call(
        functools.partial(last_kernel, levels, rows),
        out_shape=(pltpu.HBM((1, rows), F32), grad, grad),
        in_specs=[VMEM, VMEM],
        out_specs=(HBM, HBM, HBM),
        scratch_shapes=[
            pltpu.VMEM((2 * levels, width), F32),
            pltpu.VMEM((1, rows), F32),
            pltpu.SemaphoreType.DMA((3,)),
        ],
        compiler_params=pltpu.CompilerParams(vmem_limit_bytes=8 << 20),
    )(kept, given)
    return mass.reshape(rows), gain, bias


def shards(loop, hidden, exit_depth, teacher, normalizer, tied_head, depth_gain, depth_bias):
    rows_dev, width = hidden.shape
    levels = depth_gain.shape[0]
    block, gain, bias = prep(hidden, exit_depth, teacher, normalizer, depth_gain, depth_bias)
    rows = rows_dev * loop
    early = rows_dev % 16 == 0 and loop == 16
    mapper = functools.partial(map_early, rows, gain, bias) if early else None
    blocks, mapped, late = gather_blocks(block, loop, mapper)
    if rows_dev % 16:
        whole = jnp.concatenate(blocks, axis=0)
        blocks = [whole[i : i + 16] for i in range(0, rows, 16)]
        late = range(len(blocks))
    keep, give = main(blocks, tied_head, gain, bias, mapped, late, loop)
    return last(*sum_over_loop(keep, give, loop), levels, width, rows_dev)


def solution(mesh):
    loop = mesh.shape["loop"]

    def body(*args):
        return shards(loop, *args)

    return jax.shard_map(
        body,
        mesh=mesh,
        in_specs=(
            P(("groups", "loop"), None),
            P(("groups", "loop")),
            P(("groups", "loop")),
            P(("groups", "loop")),
            P("loop", None),
            P(),
            P(),
        ),
        out_specs=(P(("groups", "loop")), P("groups", None), P("groups", None)),
        check_vma=False,
    )
```

```python
import functools

import jax
import jax.numpy as jnp
from jax import lax
from jax.experimental import pallas as pl
from jax.experimental.pallas import tpu as pltpu
from jax.sharding import PartitionSpec as P

BF16 = jnp.bfloat16
F32 = jnp.float32
LANES = 128
CUTS = 42
TOGETHER = 2
FLOPS_HINT = 4_000_000_000
NT = (((1,), (1,)), ((), ()))
VMEM = pl.BlockSpec(memory_space=pltpu.VMEM)
HBM = pl.BlockSpec(memory_space=pl.ANY)


def in_hbm(x):
    return pltpu.with_memory_space_constraint(x, pltpu.HBM)


def ring_of(chips):
    return list(range(0, chips, 2)) + list(range(chips - 1, 0, -2))


def chip_at(place, chips):
    return jnp.where(place < chips // 2, 2 * place, 2 * (chips - 1 - place) + 1)


def place_of(chip, chips):
    return jnp.where(chip % 2 == 0, chip // 2, chips - 1 - chip // 2)


def pieces(value):
    top = value.astype(BF16).astype(F32)
    rest = value - top
    middle = rest.astype(BF16).astype(F32)
    return [top, middle, rest - middle]


def prep_kernel(
    hidden, exit_depth, teacher, normalizer, depth_gain, depth_bias,
    out, gain_out, bias_out, int_buf, float_buf, sems,
):
    rows, width = hidden.shape
    copies = [
        pltpu.make_async_copy(hidden, out.at[:, pl.ds(0, hidden.shape[1])], sems.at[0]),
        pltpu.make_async_copy(exit_depth, int_buf.at[0], sems.at[1]),
        pltpu.make_async_copy(teacher, int_buf.at[1], sems.at[2]),
        pltpu.make_async_copy(normalizer, float_buf, sems.at[3]),
        pltpu.make_async_copy(depth_gain, gain_out, sems.at[4]),
        pltpu.make_async_copy(depth_bias, bias_out, sems.at[5]),
    ]
    for copy in copies:
        copy.start()
    for copy in copies[1:4]:
        copy.wait()
    down = lax.broadcasted_iota(jnp.int32, (rows, rows), 0)
    across = lax.broadcasted_iota(jnp.int32, (rows, rows), 1)

    def column(line):
        square = jnp.broadcast_to(line, (rows, rows))
        return jnp.sum(jnp.where(down == across, square, 0.0), axis=1, keepdims=True)

    token = int_buf[1]
    columns = pieces(column(float_buf[...]))
    for digit in (token & 127, (token >> 7) & 127, token >> 14):
        columns.append(column(digit.astype(F32)))
    columns.append(column(int_buf[0].astype(F32)))
    copies[0].wait()
    wide = out[:, :width].astype(F32)
    mean = jnp.sum(wide * wide, axis=1, keepdims=True) * (1.0 / width)
    columns = pieces(lax.rsqrt(mean + 1e-06)) + columns
    lane = lax.broadcasted_iota(jnp.int32, (rows, LANES), 1)
    meta = jnp.zeros((rows, LANES), F32)
    for i, value in enumerate(columns):
        meta = jnp.where(lane == i, value, meta)
    out[:, width:] = meta.astype(BF16)
    for copy in copies[4:]:
        copy.wait()


def prep(hidden, exit_depth, teacher, normalizer, depth_gain, depth_bias):
    rows, width = hidden.shape
    return pl.pallas_call(
        prep_kernel,
        out_shape=(
            pltpu.VMEM((rows, width + LANES), BF16),
            pltpu.VMEM(depth_gain.shape, F32),
            pltpu.VMEM(depth_bias.shape, F32),
        ),
        in_specs=[HBM] * 6,
        out_specs=(VMEM, VMEM, VMEM),
        scratch_shapes=[
            pltpu.VMEM((2, 1, rows), jnp.int32),
            pltpu.VMEM((1, rows), F32),
            pltpu.SemaphoreType.DMA((6,)),
        ],
        compiler_params=pltpu.CompilerParams(vmem_limit_bytes=8 << 20),
    )(
        in_hbm(hidden),
        in_hbm(exit_depth.reshape(1, rows)),
        in_hbm(teacher.reshape(1, rows)),
        in_hbm(normalizer.reshape(1, rows)),
        in_hbm(depth_gain),
        in_hbm(depth_bias),
    )


def hop_pairs(order, step, cross):
    chips = len(order)
    first = 1 - step % 2
    pairs = []
    for i in range(chips):
        here, after = 2 * order[i], 2 * order[(i + 1) % chips]
        if cross:
            pairs += [(here + first, after + 1 - first), (after + 1 - first, here + first)]
        else:
            pairs += [(here + 1 - first, after + 1 - first), (after + first, here + first)]
    return pairs


def gather_blocks(block, loop, mapper):
    chips = loop // 2
    order = ring_of(chips)
    half = chips // 2
    tie = lambda *xs: lax.optimization_barrier(xs)
    send = lambda x, pairs: lax.ppermute(x, "loop", pairs)
    swap = lambda x: send(x, [(i, i ^ 1) for i in range(loop)])
    blocks = [None] * loop
    blocks[0], blocks[chips] = block, swap(block)
    crossed = plain = block
    ready = [0, chips]
    mapped = None
    for step in range(1, half + 1):
        crossed = send(crossed, hop_pairs(order, step, True))
        if step < half:
            plain = send(plain, hop_pairs(order, step, step > 1))
        if step == 1:
            crossed, plain = tie(crossed, plain)
        if mapper is not None and step == 3:
            mapped = mapper(None, {i: blocks[i] for i in ready[:6]})
            plain, mapped = tie(plain, mapped)
        if mapper is not None and step == half:
            mapped = mapper(mapped, {i: blocks[i] for i in ready[6:12]})
            crossed, mapped = tie(crossed, mapped)
        far = step if step % 2 else chips - step
        near = chips - far
        mine, theirs = (chips, 0) if step % 2 else (0, chips)
        blocks[mine + far] = crossed
        if step < half:
            blocks[theirs + far] = plain
            blocks[theirs + near] = swap(crossed)
            blocks[mine + near] = swap(plain)
            ready += [mine + far, theirs + far, theirs + near, mine + near]
        else:
            blocks[theirs + far] = swap(crossed)
            ready += [mine + far, theirs + far]
            if mapper is not None:
                mapped = mapper(mapped, {i: blocks[i] for i in ready[12:15]})
    return blocks, mapped, ready[15:] if mapper is not None else ready


def map_rows(blocks, places, gain, bias, mapped):
    size, width = blocks[0].shape[0], mapped.shape[1]
    levels = gain.shape[0]
    cut = width // CUTS if width % (CUTS * LANES) == 0 else LANES
    for first in range(0, len(blocks), TOGETHER):
        some = blocks[first : first + TOGETHER]
        meta = jnp.concatenate([b[:, width:] for b in some], axis=0).astype(F32)
        scale = (meta[:, 0:1] + meta[:, 1:2]) + meta[:, 2:3]
        depth = meta[:, 9:10]
        for start in range(0, width, cut):
            at = slice(start, start + cut)
            g, c = gain[0:1, at], bias[0:1, at]
            for level in range(1, levels):
                here = depth == float(level)
                g = jnp.where(here, gain[level : level + 1, at], g)
                c = jnp.where(here, bias[level : level + 1, at], c)
            wide = jnp.concatenate([b[:, at] for b in some], axis=0).astype(F32)
            value = ((wide * scale) * g + c).astype(BF16)
            for i, place in enumerate(places[first : first + TOGETHER]):
                mapped[place * size : (place + 1) * size, at] = value[i * size : (i + 1) * size]


def map_kernel(places, *refs):
    blocks = refs[: len(places)]
    gain, bias = refs[len(places) : len(places) + 2]
    map_rows(blocks, places, gain, bias, refs[-1])


def map_early(rows, gain, bias, mapped, blocks):
    places, blocks = list(blocks), list(blocks.values())
    width = gain.shape[1]
    operands = blocks + [gain, bias] + ([] if mapped is None else [mapped])
    count = len(blocks) * blocks[0].shape[0]
    return pl.pallas_call(
        functools.partial(map_kernel, places),
        out_shape=pltpu.VMEM((rows, width), BF16),
        in_specs=[VMEM] * len(operands),
        out_specs=VMEM,
        input_output_aliases={} if mapped is None else {len(operands) - 1: 0},
        compiler_params=pltpu.CompilerParams(vmem_limit_bytes=8 << 20),
        cost_estimate=pl.CostEstimate(
            flops=FLOPS_HINT if mapped is None else 0, bytes_accessed=4 * count * width, transcendentals=0
        ),
    )(*operands)


def half_sums(blocks, head, slopes, scaled, which, work, out):
    levels = out.shape[0] // 2
    rows = sum(b.shape[0] for b in blocks)
    half = head.shape[1] // 2
    add3 = lambda x: (x[:levels] + x[levels : 2 * levels]) + x[2 * levels : 3 * levels]
    done = 0
    while done < half:
        size = min(256, half - done)
        here = slice(done, done + size)
        at = pl.ds(pl.multiple_of(which * half + done, LANES), size)
        back = jnp.dot(slopes[...], head[:, at], preferred_element_type=F32)
        wide = jnp.concatenate([b[:, at] for b in blocks], axis=0).astype(F32)
        work[:, here] = (back[:rows] * wide).astype(BF16)
        out[levels:, here] = add3(back[rows:])
        done += size
    out[:levels, :half] = add3(jnp.dot(scaled, work[:, :half], preferred_element_type=F32))


def front_kernel(levels, count, late, *refs):
    blocks = refs[:count]
    head, gain, bias = refs[count : count + 3]
    give, slopes, scaled_out, mass_out, mapped = refs[-5:]
    voc, width = head.shape
    rows = mapped.shape[0]
    me = lax.axis_index("loop")
    core = me % 2
    meta = jnp.concatenate([b[:, width:] for b in blocks], axis=0).astype(F32)
    col = lambda i: meta[:, i : i + 1]
    scale = (col(0) + col(1)) + col(2)
    norm = (col(3) + col(4)) + col(5)
    target = (col(6) + 128.0 * col(7) + 16384.0 * col(8)).astype(jnp.int32)
    depth = col(9)

    map_rows([blocks[i] for i in late], late, gain, bias, mapped)
    logits = lax.dot_general(mapped[...], head[...], NT, preferred_element_type=F32)
    prob = jnp.exp(logits - norm)
    columns = me * voc + lax.broadcasted_iota(jnp.int32, (rows, voc), 1)
    slopes[:rows, :] = jnp.where(columns == target, prob - 1.0, prob).astype(BF16)

    mass = prob[:, :LANES]
    for j in range(1, voc // LANES):
        mass = mass + prob[:, j * LANES : (j + 1) * LANES]
    mass_out[...] = mass

    lane = lax.broadcasted_iota(jnp.int32, (rows, LANES), 1).astype(F32)
    pick = jnp.where(lane == depth, 1.0, 0.0).T[:levels]
    scaled = pick * jnp.broadcast_to(scale, (rows, LANES)).T[:levels]
    none = jnp.zeros((16 - 3 * levels, rows), F32)
    scaled = jnp.concatenate(pieces(scaled) + [none], axis=0).astype(BF16)
    scaled_out[...] = scaled
    sums = jnp.dot(pick.astype(BF16), slopes[:rows, :], preferred_element_type=F32)
    none = jnp.zeros((16 - 3 * levels, voc), F32)
    slopes[rows:, :] = jnp.concatenate(pieces(sums) + [none], axis=0).astype(BF16)
    half_sums(blocks, head, slopes, scaled, 1 - core, mapped, give)
    give[:, width // 2 :] = jnp.zeros((2 * levels, rows), F32)


def back_kernel(loop, count, *refs):
    blocks = refs[:count]
    head, slopes, scaled, mass, keep, work = refs[count:]
    rows, half = work.shape
    rows_dev = rows // loop
    chips = loop // 2
    me = lax.axis_index("loop")
    core = me % 2
    half_sums(blocks, head, slopes, scaled[...], core, work, keep)

    index = lax.broadcasted_iota(jnp.int32, (rows, LANES), 0)
    flip = index // (rows // 2)
    relative = (index - flip * (rows // 2)) // rows_dev
    place = place_of(me // 2, chips) + jnp.where(core == 0, relative, chips - relative)
    place = jnp.where(place >= chips, place - chips, place)
    owner = 2 * chip_at(place, chips) + jnp.where(flip == 0, core, 1 - core)
    goes_to = owner * rows_dev + index % rows_dev
    lane = lax.broadcasted_iota(jnp.int32, (rows, LANES), 1)
    move = [jnp.where(goes_to == lane + k, 1.0, 0.0) for k in range(0, rows, LANES)]
    move = jnp.concatenate(move, axis=1).astype(BF16)
    line = jnp.sum(mass[...].T, axis=0, keepdims=True)
    lines = jnp.concatenate(pieces(line) + [jnp.zeros((13, rows), F32)], axis=0)
    moved = jnp.dot(lines.astype(BF16), move, preferred_element_type=F32)
    moved = (moved[0:1] + moved[1:2]) + moved[2:3]
    keep[:, half:] = jnp.broadcast_to(moved, (keep.shape[0], rows))


def main(blocks, head, gain, bias, mapped, late, loop):
    levels = gain.shape[0]
    voc, width = head.shape
    rows = sum(b.shape[0] for b in blocks)
    half = pltpu.VMEM((2 * levels, width // 2 + rows), F32)
    operands = list(blocks) + [head, gain, bias] + ([] if mapped is None else [mapped])
    cost = lambda passes: pl.CostEstimate(
        flops=passes * rows * voc * width, bytes_accessed=voc * width, transcendentals=0
    )
    give, slopes, scaled, mass, _ = pl.pallas_call(
        functools.partial(front_kernel, levels, len(blocks), late),
        out_shape=(
            half,
            pltpu.VMEM((rows + 16, voc), BF16),
            pltpu.VMEM((16, rows), BF16),
            pltpu.VMEM((rows, LANES), F32),
            pltpu.VMEM((rows, width), BF16),
        ),
        in_specs=[VMEM] * len(operands),
        out_specs=(VMEM,) * 5,
        input_output_aliases={} if mapped is None else {len(operands) - 1: 4},
        compiler_params=pltpu.CompilerParams(vmem_limit_bytes=16 << 20),
        cost_estimate=cost(3),
    )(*operands)
    operands = list(blocks) + [head, slopes, scaled, mass]
    keep = pl.pallas_call(
        functools.partial(back_kernel, loop, len(blocks)),
        out_shape=half,
        in_specs=[VMEM] * len(operands),
        out_specs=VMEM,
        scratch_shapes=[pltpu.VMEM((rows, width // 2), BF16)],
        compiler_params=pltpu.CompilerParams(vmem_limit_bytes=16 << 20),
        cost_estimate=cost(1),
    )(*operands)
    return keep, give


def sum_over_loop(keep, give, loop):
    send = lambda x, mask: lax.ppermute(x, "loop", [(i, i ^ mask) for i in range(loop)])
    total = keep + send(give, 1)
    bits = [1 << k for k in range(1, loop.bit_length() - 1)]
    for k in range(0, len(bits) - 1, 2):
        dims = bits[:-1][k : k + 2]
        total = lax.reduce_precision(total, 8, 7)
        sent = total.astype(BF16)
        take = lambda mask: send(sent, mask).astype(F32)
        total = total + take(dims[0])
        if len(dims) == 2:
            total = total + (take(dims[1]) + take(dims[0] ^ dims[1]))
    total = lax.reduce_precision(total, 8, 7)
    total = total + send(total.astype(BF16), bits[-1]).astype(F32)
    return total, send(total, 1)


def last_kernel(levels, rows, kept, given, mass_out, gain_out, bias_out, buf, line, sems):
    width = gain_out.shape[1]
    me = lax.axis_index("loop")
    cut = width // 2
    low = jnp.where(me % 2 == 0, kept[...], given[...])
    high = jnp.where(me % 2 == 0, given[...], kept[...])
    buf[:, :cut], buf[:, cut:width] = low[:, :cut], high[:, :cut]
    every = kept[0:1, cut:] + given[0:1, cut:]
    spread = lax.broadcasted_iota(jnp.int32, (every.shape[1], LANES), 0)
    target = lax.broadcasted_iota(jnp.int32, (every.shape[1], LANES), 1)
    move = jnp.where(spread - me * rows == target, 1.0, 0.0).astype(BF16)
    lines = jnp.concatenate(pieces(every) + [jnp.zeros((13, every.shape[1]), F32)], axis=0)
    own = jnp.dot(lines.astype(BF16), move, preferred_element_type=F32)
    line[...] = ((own[0:1] + own[1:2]) + own[2:3])[:, :rows]
    copies = [
        pltpu.make_async_copy(buf.at[pl.ds(0, levels)], gain_out, sems.at[0]),
        pltpu.make_async_copy(buf.at[pl.ds(levels, levels)], bias_out, sems.at[1]),
        pltpu.make_async_copy(line, mass_out, sems.at[2]),
    ]
    for copy in copies:
        copy.start()
    for copy in copies:
        copy.wait()


def last(kept, given, levels, width, rows):
    grad = pltpu.HBM((levels, width), F32)
    mass, gain, bias = pl.pallas_call(
        functools.partial(last_kernel, levels, rows),
        out_shape=(pltpu.HBM((1, rows), F32), grad, grad),
        in_specs=[VMEM, VMEM],
        out_specs=(HBM, HBM, HBM),
        scratch_shapes=[
            pltpu.VMEM((2 * levels, width), F32),
            pltpu.VMEM((1, rows), F32),
            pltpu.SemaphoreType.DMA((3,)),
        ],
        compiler_params=pltpu.CompilerParams(vmem_limit_bytes=8 << 20),
    )(kept, given)
    return mass.reshape(rows), gain, bias


def shards(loop, hidden, exit_depth, teacher, normalizer, tied_head, depth_gain, depth_bias):
    rows_dev, width = hidden.shape
    levels = depth_gain.shape[0]
    block, gain, bias = prep(hidden, exit_depth, teacher, normalizer, depth_gain, depth_bias)
    rows = rows_dev * loop
    early = rows_dev % 16 == 0 and loop == 16
    mapper = functools.partial(map_early, rows, gain, bias) if early else None
    blocks, mapped, late = gather_blocks(block, loop, mapper)
    if rows_dev % 16:
        whole = jnp.concatenate(blocks, axis=0)
        blocks = [whole[i : i + 16] for i in range(0, rows, 16)]
        late = range(len(blocks))
    keep, give = main(blocks, tied_head, gain, bias, mapped, late, loop)
    return last(*sum_over_loop(keep, give, loop), levels, width, rows_dev)


def solution(mesh):
    loop = mesh.shape["loop"]

    def body(*args):
        return shards(loop, *args)

    return jax.shard_map(
        body,
        mesh=mesh,
        in_specs=(
            P(("groups", "loop"), None),
            P(("groups", "loop")),
            P(("groups", "loop")),
            P(("groups", "loop")),
            P("loop", None),
            P(),
            P(),
        ),
        out_specs=(P(("groups", "loop")), P("groups", None), P("groups", None)),
        check_vma=False,
    )
```
